32 devices in a mesh: batch: 4 (over x, core), seq: 8 (over z, y).
Axes of the slice: x: 2, y: 2, z: 4, core: 2. Of those that a mesh axis runs over, the one named last changes fastest.
Arguments:
- tokens: bfloat16 [4, 8192, 768], P('batch', 'seq'), may hold values from -6 to 6
- glob_tokens: bfloat16 [4, 128, 768], P('batch'), may hold values from -6 to 6
- w_qkv: bfloat16 [768, 2304], replicated, may hold values from -0.21875 to 0.21875
- w_out: bfloat16 [768, 768], replicated, may hold values from -1.25 to 1.25
- w_up: bfloat16 [768, 3072], replicated, may hold values from -0.21875 to 0.21875
- w_down: bfloat16 [3072, 768], replicated, may hold values from -0.109375 to 0.109375
- vec_params: float32 [5, 768], replicated, may hold values from -1 to 2.5, as said below
- hidden_bias: float32 [3072], replicated, may hold values from -1.5 to 1.5
- row_qkv: float32 [768], P(('batch', 'seq')), may hold values from 2276.352 to 9105.408
- col_qkv: float32 [2304], replicated, may hold values from 2276.352 to 9105.408
- row_out: float32 [768], P(('batch', 'seq')), may hold values from 63.232 to 252.928
- col_out: float32 [768], replicated, may hold values from 63.232 to 252.928
- row_up: float32 [768], P(('batch', 'seq')), may hold values from 1896.96 to 7587.84
- col_up: float32 [3072], replicated, may hold values from 1896.96 to 7587.84
- row_down: float32 [3072], P(('batch', 'seq')), may hold values from 5058.56 to 20234.24
- col_down: float32 [768], replicated, may hold values from 5058.56 to 20234.24
- vec_state: float32 [5, 768], replicated, may hold values from 9484.8 to 37939.2
- bias_state: float32 [3072], replicated, may hold values from 1580.8 to 6323.2
- segments: int32 [4, 8192], P('batch'), may hold values from 0 to 3, as said below
- valid_mask: int32 [4, 8192], P('batch'), may hold values from 0 to 1
- out_cotangent: bfloat16 [4, 8192, 768], P('batch', 'seq'), may hold values from -6 to 6
- glob_cotangent: bfloat16 [4, 128, 768], P('batch'), may hold values from -6 to 6
Outputs:
- block_out: bfloat16 [4, 8192, 768], P('batch', 'seq')
- glob_out: bfloat16 [4, 128, 768], P('batch')
- tokens_grad: float32 [4, 8192, 768], P('batch', 'seq')
- glob_grad: float32 [4, 128, 768], P('batch')
- grad_qkv: float32 [768, 2304], P(('batch', 'seq'))
- row_qkv_new: float32 [768], P(('batch', 'seq'))
- col_qkv_new: float32 [2304], replicated
- new_qkv: float32 [768, 2304], P(('batch', 'seq'))
- grad_out: float32 [768, 768], P(('batch', 'seq'))
- row_out_new: float32 [768], P(('batch', 'seq'))
- col_out_new: float32 [768], replicated
- new_out: float32 [768, 768], P(('batch', 'seq'))
- grad_up: float32 [768, 3072], P(('batch', 'seq'))
- row_up_new: float32 [768], P(('batch', 'seq'))
- col_up_new: float32 [3072], replicated
- new_up: float32 [768, 3072], P(('batch', 'seq'))
- grad_down: float32 [3072, 768], P(('batch', 'seq'))
- row_down_new: float32 [3072], P(('batch', 'seq'))
- col_down_new: float32 [768], replicated
- new_down: float32 [3072, 768], P(('batch', 'seq'))
- vec_grad: float32 [5, 768], replicated
- vec_state_new: float32 [5, 768], replicated
- vec_new: float32 [5, 768], replicated
- bias_grad: float32 [3072], replicated
- bias_state_new: float32 [3072], replicated
- bias_new: float32 [3072], replicated
The draws below stay inside these ranges and needn't reach their ends.
Inputs may be any that keep to these rules, and one draw needn't show every extreme that they name: `segments`: non-decreasing along each group. `vec_params`: rows 0 and 2 are positive.
All inputs are finite; a program needn't handle non-finite values.
Results may differ from the reference program's by a relative error of at most 0.013.
Values may be sent and summed in bfloat16 or wider, within the bound.
No kernel may reach another device: no remote copies, remote signals or barrier semaphores. Data moves between devices by JAX's collectives and lax.ppermute only.
A program may use at most 320 MiB of HBM per device.

```python
import math
import jax
import jax.numpy as jnp
from jax import lax

D = 768
HEADS = 12
FF = 3072
GLOBALS = 128
BLOCK = 512
STEP = 10
HEAD = 64
TOK_DEV = 1024
LENGTH = 8192
GROUPS = 4


def draw_segments(key, part):
    key = jax.random.fold_in(key, 11)
    key_parts = jax.random.split(key, 3)
    doc_start = jax.random.randint(key_parts[0], (GROUPS, 1), 1, TOK_DEV // 2 + 1)
    tail_rows = jax.random.randint(key_parts[1], (GROUPS, 1), 1, TOK_DEV // 2 + 1)
    tail_split = jnp.minimum(jax.random.randint(key_parts[2], (GROUPS, 1), 0, TOK_DEV // 2 + 1), tail_rows - 1)
    places = jnp.arange(LENGTH, dtype=jnp.int32)[None, :]
    doc_stop = LENGTH - tail_rows
    numbers = (places >= doc_start).astype(jnp.int32) + (places >= doc_stop).astype(jnp.int32)
    return numbers + (places >= doc_stop + tail_split).astype(jnp.int32)


def draw_valid_mask(key, part):
    key = jax.random.fold_in(key, 13)
    pad_rows = jax.random.randint(key, (GROUPS, LENGTH // BLOCK, 1), 1, BLOCK * 3 // 8 + 1)
    within = jnp.arange(BLOCK, dtype=jnp.int32)[None, None, :]
    return (within < BLOCK - pad_rows).astype(jnp.int32).reshape(GROUPS, LENGTH)


def draw_vec_params(key, part):
    key = jax.random.fold_in(key, 17)
    key_parts = jax.random.split(key, 2)
    ramp = jnp.arange(D, dtype=jnp.float32) / (D - 1)
    rising = (0.5 + ramp) * jnp.exp(0.12 * jnp.clip(jax.random.normal(key_parts[0], (2, D), jnp.float32), -3.0, 3.0))
    shifts = 0.3 * jnp.clip(jax.random.normal(key_parts[1], (3, D), jnp.float32), -3.0, 3.0)
    return jnp.stack([rising[0], shifts[0], rising[1], shifts[1], shifts[2]])


def level_of(key, extent, cuts, low, largest):
    factor_of, own = 1.0, jax.random.fold_in(key, 6)
    for axis_at, blocks in cuts:
        draws = jnp.exp(jax.random.uniform(jax.random.fold_in(own, axis_at), (blocks,), jnp.float32, low / len(cuts), largest / len(cuts)))
        factor_of = factor_of * jnp.repeat(draws, extent[axis_at] // blocks).reshape([-1 if axis == axis_at else 1 for axis in range(len(extent))])
    return factor_of


def normal_values(rng, dims, scale, most, cuts=(), kind=jnp.bfloat16):
    drawn = scale * jax.random.normal(rng, dims, jnp.float32)
    if cuts:
        drawn = drawn * level_of(rng, dims, cuts, -0.22, 0.18)
    return jnp.clip(drawn, -most, most).astype(kind)


def setup_inputs(seed: int = 0) -> dict:
    streams_of = jax.random.split(jax.random.key(seed), 23)
    return {
        "tokens": normal_values(streams_of[0], (GROUPS, LENGTH, D), 1.0, 6.0, ((0, 4), (1, 8))),
        "glob_tokens": normal_values(streams_of[1], (GROUPS, GLOBALS, D), 1.0, 6.0, ((0, 4),)),
        "w_qkv": normal_values(streams_of[2], (D, 3 * D), D ** -0.5, 0.21875),
        "w_out": normal_values(streams_of[3], (D, D), (D // 32) ** -0.5, 1.25),
        "w_up": normal_values(streams_of[4], (D, FF), D ** -0.5, 0.21875),
        "w_down": normal_values(streams_of[5], (FF, D), FF ** -0.5, 0.109375),
        "vec_params": draw_vec_params(jax.random.fold_in(streams_of[22], 71), 0),
        "hidden_bias": normal_values(streams_of[7], (FF,), 0.3, 1.5, (), jnp.float32),
        "row_qkv": jnp.clip(jnp.exp(math.log(9105.408) - 1.3862944 * jax.random.uniform(streams_of[8], (D,), jnp.float32) ** level_of(streams_of[8], (D,), ((0, 32),), -0.2, 0.2)), 2276.352, 9105.408),
        "col_qkv": jnp.clip(jnp.exp(jax.random.uniform(streams_of[9], (3 * D,), jnp.float32, math.log(2276.352), math.log(9105.408))), 2276.352, 9105.408),
        "row_out": jnp.clip(jnp.exp(math.log(252.928) - 1.3862944 * jax.random.uniform(streams_of[10], (D,), jnp.float32) ** level_of(streams_of[10], (D,), ((0, 32),), -0.2, 0.2)), 63.232, 252.928),
        "col_out": jnp.clip(jnp.exp(jax.random.uniform(streams_of[11], (D,), jnp.float32, math.log(63.232), math.log(252.928))), 63.232, 252.928),
        "row_up": jnp.clip(jnp.exp(math.log(7587.84) - 1.3862944 * jax.random.uniform(streams_of[12], (D,), jnp.float32) ** level_of(streams_of[12], (D,), ((0, 32),), -0.2, 0.2)), 1896.96, 7587.84),
        "col_up": jnp.clip(jnp.exp(jax.random.uniform(streams_of[13], (FF,), jnp.float32, math.log(1896.96), math.log(7587.84))), 1896.96, 7587.84),
        "row_down": jnp.clip(jnp.exp(math.log(20234.24) - 1.3862944 * jax.random.uniform(streams_of[14], (FF,), jnp.float32) ** level_of(streams_of[14], (FF,), ((0, 32),), -0.2, 0.2)), 5058.56, 20234.24),
        "col_down": jnp.clip(jnp.exp(jax.random.uniform(streams_of[15], (D,), jnp.float32, math.log(5058.56), math.log(20234.24))), 5058.56, 20234.24),
        "vec_state": jnp.clip(jnp.exp(jax.random.uniform(streams_of[16], (5, D), jnp.float32, math.log(9484.8), math.log(37939.2))), 9484.8, 37939.2),
        "bias_state": jnp.clip(jnp.exp(jax.random.uniform(streams_of[17], (FF,), jnp.float32, math.log(1580.8), math.log(6323.2))), 1580.8, 6323.2),
        "segments": draw_segments(jax.random.fold_in(streams_of[22], 71), 0),
        "valid_mask": draw_valid_mask(jax.random.fold_in(streams_of[22], 71), 0),
        "out_cotangent": normal_values(streams_of[20], (GROUPS, LENGTH, D), 1.0, 6.0, ((0, 4), (1, 8))),
        "glob_cotangent": normal_values(streams_of[21], (GROUPS, GLOBALS, D), 1.0, 6.0, ((0, 4),)),
    }


@jax.custom_vjp
def low(v):
    return lax.optimization_barrier(v.astype(jnp.bfloat16)).astype(jnp.float32)

@jax.custom_vjp
def low_back(v):
    return v

def low_keep(v):
    return (low(v), None)

def low_pass(kept, grad):
    return (grad,)

def back_keep(v):
    return (v, None)

def back_low(kept, grad):
    return (low(grad),)
low.defvjp(low_keep, low_pass)
low_back.defvjp(back_keep, back_low)
NEG_FILL = -1000000000.0
NORM_EPS = 1e-06
TINY_SQUARE = 1e-30
RATE_MATRIX = 0.03
RATE_VECTOR = 0.2

def layer_norm(values, norm_gain, norm_shift):
    average = lax.optimization_barrier(jnp.mean(values, axis=-1, keepdims=True))
    centred = values - average
    variance = lax.optimization_barrier(jnp.mean(centred * centred, axis=-1, keepdims=True))
    return centred * lax.rsqrt(variance + NORM_EPS) * norm_gain + norm_shift

def product(left_rows, right_rows):
    return jnp.dot(left_rows, right_rows, precision=lax.Precision.HIGHEST)

def spread_blocks(values):
    grouped = values.reshape((-1, BLOCK) + values.shape[1:])
    return jnp.repeat(grouped, 2, axis=0)[1:-1]

def attend_rows(queries, key_rows, value_rows, allowed):
    score_scale = HEAD ** (-0.5)
    scores = jnp.einsum('qhe,khe->hqk', queries, key_rows, precision=lax.Precision.HIGHEST) * score_scale
    scores = low_back(jnp.where(allowed[None], scores, NEG_FILL))
    log_total = jax.nn.logsumexp(scores, axis=-1, keepdims=True)
    weights = low(jnp.exp(scores - log_total))
    return jnp.einsum('hqk,khe->qhe', weights, value_rows, precision=lax.Precision.HIGHEST)

def to_heads(values):
    return values.reshape(values.shape[0], HEADS, HEAD)

def group_forward(params, token_rows, glob_rows, seg_row, valid_row):
    w_qkv, w_out, w_up, w_down, vec_params, hidden_bias = params
    model_width = w_out.shape[0]
    half_rows = BLOCK // 2
    token_count = token_rows.shape[0]
    glob_count = glob_rows.shape[0]
    rows_all = jnp.concatenate([token_rows, glob_rows], axis=0)
    normed = low(layer_norm(rows_all, vec_params[0], vec_params[1]))
    qkv_all = low(low_back(product(normed, w_qkv)))
    queries = to_heads(qkv_all[:, :model_width])
    key_all = to_heads(qkv_all[:, model_width:2 * model_width])
    value_all = to_heads(qkv_all[:, 2 * model_width:])
    glob_keys = key_all[token_count:]
    glob_values = value_all[token_count:]
    padding = ((half_rows, half_rows), (0, 0), (0, 0))
    block_keys = spread_blocks(jnp.pad(key_all[:token_count], padding))
    block_values = spread_blocks(jnp.pad(value_all[:token_count], padding))
    block_seg = spread_blocks(jnp.pad(seg_row, half_rows, constant_values=-1))
    block_valid = spread_blocks(jnp.pad(valid_row, half_rows))
    halves = token_count // half_rows
    query_halves = queries[:token_count].reshape(halves, half_rows, HEADS, HEAD)
    query_seg = seg_row.reshape(halves, half_rows)
    glob_ones = jnp.ones((half_rows, glob_count), dtype=bool)

    def one_half(pieces):
        query_part, key_part, value_part, seg_query, seg_key, valid_key = pieces
        allowed = (seg_query[:, None] == seg_key[None, :]) & (valid_key[None, :] > 0)
        allowed = jnp.concatenate([allowed, glob_ones], axis=1)
        return attend_rows(query_part, jnp.concatenate([key_part, glob_keys], axis=0), jnp.concatenate([value_part, glob_values], axis=0), allowed)
    local_out = lax.map(jax.checkpoint(one_half), (query_halves, block_keys, block_values, query_seg, block_seg, block_valid))
    local_out = local_out.reshape(token_count, model_width)
    key_ok = jnp.concatenate([valid_row > 0, jnp.ones((glob_count,), dtype=bool)])
    glob_allowed = jnp.broadcast_to(key_ok[None, :], (glob_count, token_count + glob_count))
    glob_heads = attend_rows(queries[token_count:], key_all, value_all, glob_allowed)
    attended = low(low_back(jnp.concatenate([local_out, glob_heads.reshape(glob_count, model_width)], axis=0)))
    mixed = rows_all + low_back(product(attended, w_out))
    normed_two = low(layer_norm(mixed, vec_params[2], vec_params[3]))
    hidden = low_back(product(normed_two, w_up) + hidden_bias)
    active = low(jax.nn.gelu(hidden, approximate=False))
    result = mixed + low_back(product(active, w_down) + vec_params[4])
    return (result[:token_count], result[token_count:])

def factored_update(weight, grad, row_old, col_old):
    decay_rate = 1.0 - STEP ** (-0.8)
    square = grad * grad + TINY_SQUARE
    row_new = decay_rate * row_old + (1.0 - decay_rate) * lax.optimization_barrier(jnp.mean(square, axis=1))
    col_new = decay_rate * col_old + (1.0 - decay_rate) * lax.optimization_barrier(jnp.mean(square, axis=0))
    estimate = row_new[:, None] * col_new[None, :] / jnp.mean(row_new)
    return (grad, row_new, col_new, weight - RATE_MATRIX * grad * lax.rsqrt(estimate))

def vector_update(params, grad, state):
    decay_rate = 1.0 - STEP ** (-0.8)
    state_new = decay_rate * state + (1.0 - decay_rate) * (grad * grad + TINY_SQUARE)
    return (grad, state_new, params - RATE_VECTOR * grad * lax.rsqrt(state_new))

def reference(tokens, glob_tokens, w_qkv, w_out, w_up, w_down, vec_params, hidden_bias, row_qkv, col_qkv, row_out, col_out, row_up, col_up, row_down, col_down, vec_state, bias_state, segments, valid_mask, out_cotangent, glob_cotangent):
    params = (w_qkv.astype(jnp.float32), w_out.astype(jnp.float32), w_up.astype(jnp.float32), w_down.astype(jnp.float32), vec_params, hidden_bias)

    def forward(weights_all, token_rows, glob_rows):

        def one_group(pieces):
            return group_forward(weights_all, pieces[0], pieces[1], pieces[2], pieces[3])
        return lax.map(jax.checkpoint(one_group), (token_rows, glob_rows, segments, valid_mask))
    outputs, pullback = jax.vjp(forward, params, tokens.astype(jnp.float32), glob_tokens.astype(jnp.float32))
    param_grads, tokens_grad, glob_grad = pullback((out_cotangent.astype(jnp.float32), glob_cotangent.astype(jnp.float32)))
    qkv_parts = factored_update(params[0], param_grads[0], row_qkv, col_qkv)
    out_parts = factored_update(params[1], param_grads[1], row_out, col_out)
    up_parts = factored_update(params[2], param_grads[2], row_up, col_up)
    down_parts = factored_update(params[3], param_grads[3], row_down, col_down)
    vec_parts = vector_update(vec_params, param_grads[4], vec_state)
    bias_parts = vector_update(hidden_bias, param_grads[5], bias_state)
    return (outputs[0].astype(jnp.bfloat16), outputs[1].astype(jnp.bfloat16), tokens_grad, glob_grad, qkv_parts[0], qkv_parts[1], qkv_parts[2], qkv_parts[3], out_parts[0], out_parts[1], out_parts[2], out_parts[3], up_parts[0], up_parts[1], up_parts[2], up_parts[3], down_parts[0], down_parts[1], down_parts[2], down_parts[3], vec_parts[0], vec_parts[1], vec_parts[2], bias_parts[0], bias_parts[1], bias_parts[2])
```

```python
from functools import partial

import jax
import jax.numpy as jnp
from jax import lax
from jax.sharding import PartitionSpec as P

HEADS = 12
BLOCK = 512
STEP = 10


NEG_FILL = -1000000000.0
NORM_EPS = 1e-06
TINY_SQUARE = 1e-30
RATE_MATRIX = 0.03
RATE_VECTOR = 0.2


def with_halo(x, sides, width):
    for axis, dim in sides:
        size, length = (lax.axis_size(axis), x.shape[dim])
        up = [(i, (i + 1) % size) for i in range(size - 1)]
        down = [(j, i) for i, j in up]
        last = lax.slice_in_dim(x, length - width, length, axis=dim)
        initial = lax.slice_in_dim(x, 0, width, axis=dim)
        before = lax.ppermute(last, axis, up)
        after = lax.ppermute(initial, axis, down)
        x = jnp.concatenate([before, x, after], axis=dim)
    return x


def bits_of(axis):
    size = lax.axis_size(axis)
    assert size & (size - 1) == 0
    return [(axis, 1 << k) for k in range(size.bit_length() - 1)]


def side_of(axis, bit):
    return (lax.axis_index(axis) // bit) % 2


def swapped(values, axis, bit):
    return lax.ppermute(values, axis, [(i, i ^ bit) for i in range(lax.axis_size(axis))])


def summed(parts, bits):
    leaves, tree = jax.tree.flatten(parts)
    flat = jnp.concatenate([leaf.reshape(-1) for leaf in leaves])
    count = flat.shape[0]
    flat = jnp.pad(flat, (0, -count % 1024)).reshape(-1, 128)
    for axis, bit in bits:
        flat = flat + swapped(flat, axis, bit)
    flat = flat.reshape(-1)
    out, place = [], 0
    for leaf in leaves:
        out.append(flat[place : place + leaf.size].reshape(leaf.shape))
        place += leaf.size
    return jax.tree.unflatten(tree, out)


def scattered(grad, order):
    labels = bits_of("batch")[::-1] + bits_of("seq")[::-1]
    held = grad.reshape((2,) * len(labels) + (-1, grad.shape[-1]))
    for axis, bit in order:
        dim = labels.index((axis, bit))
        labels.pop(dim)
        mine = side_of(axis, bit)
        sent = lax.dynamic_index_in_dim(held, 1 - mine, dim, False).astype(jnp.bfloat16)
        kept = lax.dynamic_index_in_dim(held, mine, dim, False).astype(jnp.float32)
        held = kept + swapped(sent, axis, bit).astype(jnp.float32)
    return held


def joined(state, axis, combine):
    for _, bit in bits_of(axis):
        other = jax.tree.map(lambda a: swapped(a, axis, bit), state)
        upper = side_of(axis, bit) == 1
        first = jax.tree.map(lambda a, b: jnp.where(upper, b, a), state, other)
        second = jax.tree.map(lambda a, b: jnp.where(upper, a, b), state, other)
        state = combine(first, second)
    return state


def from_behind(block, axis, distance):
    devices = range(lax.axis_size(axis))
    route = [(i - distance, i) for i in devices if i - distance in devices]
    return lax.ppermute(block, axis, route)


def layer_norm(values, norm_gain, norm_shift):
    average = jnp.mean(values, axis=-1, keepdims=True)
    centred = values - average
    variance = jnp.mean(centred * centred, axis=-1, keepdims=True)
    return centred * lax.rsqrt(variance + NORM_EPS) * norm_gain + norm_shift


def norm_terms(values, upstream):
    average = jnp.mean(values, axis=-1, keepdims=True)
    centred = values - average
    variance = jnp.mean(centred * centred, axis=-1, keepdims=True)
    normalized = centred * lax.rsqrt(variance + NORM_EPS)
    return (jnp.sum(upstream * normalized, axis=0), jnp.sum(upstream, axis=0))


def norm_backward(values, norm_gain, norm_shift, upstream):
    pullback = jax.vjp(lambda inner_rows: layer_norm(inner_rows, norm_gain, norm_shift), values)[1]
    return pullback(upstream)[0]


def dense(left_rows, right_rows):
    return jnp.dot(left_rows, right_rows, preferred_element_type=jnp.float32)


def dense_back(grad_rows, matrix):
    return lax.dot_general(
        grad_rows, matrix, (((1,), (1,)), ((), ())), preferred_element_type=jnp.float32
    )


def outer_sum(input_rows, grad_rows):
    return lax.dot_general(
        input_rows, grad_rows, (((0,), (0,)), ((), ())), preferred_element_type=jnp.float32
    )


def spread_blocks(values):
    grouped = values.reshape((-1, BLOCK) + values.shape[1:])
    return jnp.repeat(grouped, 2, axis=0)[1:-1]


def fold_blocks(values):
    zero_block = jnp.zeros((1,) + values.shape[1:], values.dtype)
    padded = jnp.concatenate([zero_block, values, zero_block], axis=0)
    paired = padded.reshape((-1, 2) + values.shape[1:])
    return jnp.sum(paired, axis=1).reshape((-1,) + values.shape[2:])


def combine_totals(earlier, later):
    top_score = jnp.maximum(earlier[0], later[0])
    return (
        top_score,
        earlier[1] * jnp.exp(earlier[0] - top_score) + later[1] * jnp.exp(later[0] - top_score),
    )


def body(
    tokens,
    glob_tokens,
    w_qkv,
    w_out,
    w_up,
    w_down,
    vec_params,
    hidden_bias,
    row_qkv,
    col_qkv,
    row_out,
    col_out,
    row_up,
    col_up,
    row_down,
    col_down,
    vec_state,
    bias_state,
    segments,
    valid_mask,
    out_cotangent,
    glob_cotangent,
):
    model_width = w_out.shape[0]
    head_size = model_width // HEADS
    score_scale = head_size ** (-0.5)
    half_rows = BLOCK // 2
    own_rows = tokens.shape[1]
    glob_count = glob_tokens.shape[1]
    halves = own_rows // half_rows
    seq_index = lax.axis_index("seq")
    row_start = seq_index * own_rows
    bf16 = jnp.bfloat16
    f32 = jnp.float32
    first_flag = seq_index == 0

    def counted(values):
        glob_rows = values[own_rows:] * first_flag.astype(values.dtype)
        return jnp.concatenate([values[:own_rows], glob_rows], axis=0)

    def to_heads(values):
        return values.reshape(values.shape[0], HEADS, head_size)

    rows_all = jnp.concatenate([tokens[0].astype(f32), glob_tokens[0].astype(f32)], axis=0)
    normed_low = layer_norm(rows_all, vec_params[0], vec_params[1]).astype(bf16)
    qkv_low = dense(normed_low, w_qkv).astype(bf16)
    pair_low = qkv_low[:own_rows, model_width:]
    query_own = to_heads(qkv_low[:own_rows, :model_width])
    key_own = to_heads(pair_low[:, :model_width])
    value_own = to_heads(pair_low[:, model_width:])
    glob_query = to_heads(qkv_low[own_rows:, :model_width])
    glob_key = to_heads(qkv_low[own_rows:, model_width : 2 * model_width])
    glob_value = to_heads(qkv_low[own_rows:, 2 * model_width :])
    extended = with_halo(pair_low, (("seq", 0),), half_rows)
    pair_blocks = spread_blocks(extended)
    key_blocks = pair_blocks[..., :model_width].reshape(halves, BLOCK, HEADS, head_size)
    value_blocks = pair_blocks[..., model_width:].reshape(halves, BLOCK, HEADS, head_size)
    seg_all = segments[0]
    mask_all = valid_mask[0]
    seg_ext = lax.dynamic_slice_in_dim(
        jnp.pad(seg_all, half_rows, constant_values=-1), row_start, own_rows + BLOCK
    )
    mask_ext = lax.dynamic_slice_in_dim(jnp.pad(mask_all, half_rows), row_start, own_rows + BLOCK)
    seg_own = lax.dynamic_slice_in_dim(seg_all, row_start, own_rows)
    mask_own = lax.dynamic_slice_in_dim(mask_all, row_start, own_rows) > 0
    seg_blocks = spread_blocks(seg_ext)
    mask_blocks = spread_blocks(mask_ext)
    allowed = (seg_own.reshape(halves, half_rows)[:, :, None] == seg_blocks[:, None, :]) & (
        mask_blocks[:, None, :] > 0
    )
    query_halves = query_own.reshape(halves, half_rows, HEADS, head_size)

    def local_scores():
        near_scores = (
            jnp.einsum("nqhe,nkhe->nhqk", query_halves, key_blocks, preferred_element_type=f32)
            * score_scale
        )
        near_scores = jnp.where(allowed[:, None], near_scores, NEG_FILL)
        far_scores = (
            jnp.einsum("nqhe,ghe->nhqg", query_halves, glob_key, preferred_element_type=f32)
            * score_scale
        )
        return jnp.concatenate([near_scores, far_scores], axis=-1)

    def glob_scores():
        to_tokens = (
            jnp.einsum("ghe,khe->hgk", glob_query, key_own, preferred_element_type=f32)
            * score_scale
        )
        to_tokens = jnp.where(mask_own[None, None, :], to_tokens, NEG_FILL)
        to_globs = (
            jnp.einsum("ghe,jhe->hgj", glob_query, glob_key, preferred_element_type=f32)
            * score_scale
        )
        return (to_tokens, to_globs)

    scores = local_scores()
    local_total = jax.nn.logsumexp(scores, axis=-1, keepdims=True)
    weights_low = jnp.exp(scores - local_total).astype(bf16)
    local_att = jnp.einsum(
        "nhqk,nkhe->nqhe", weights_low[..., :BLOCK], value_blocks, preferred_element_type=f32
    )
    local_att = local_att + jnp.einsum(
        "nhqg,ghe->nqhe", weights_low[..., BLOCK:], glob_value, preferred_element_type=f32
    )
    local_att = local_att.reshape(own_rows, model_width)
    to_tokens, to_globs = glob_scores()
    part_max = jnp.max(to_tokens, axis=-1)
    part_sum = jnp.sum(jnp.exp(to_tokens - part_max[..., None]), axis=-1)
    merged_max, merged_sum = joined((part_max, part_sum), "seq", combine_totals)
    top_score = jnp.maximum(merged_max, jnp.max(to_globs, axis=-1))
    glob_sum = merged_sum * jnp.exp(merged_max - top_score) + jnp.sum(
        jnp.exp(to_globs - top_score[..., None]), axis=-1
    )
    glob_total = (top_score + jnp.log(glob_sum))[..., None]
    token_weights_low = jnp.exp(to_tokens - glob_total).astype(bf16)
    self_weights_low = jnp.exp(to_globs - glob_total).astype(bf16)
    glob_part = jnp.einsum("hgk,khe->ghe", token_weights_low, value_own, preferred_element_type=f32)
    glob_att = summed(glob_part, bits_of("seq"))
    glob_att = glob_att + jnp.einsum(
        "hgj,jhe->ghe", self_weights_low, glob_value, preferred_element_type=f32
    )
    attended_low = jnp.concatenate(
        [local_att, glob_att.reshape(glob_count, model_width)], axis=0
    ).astype(bf16)
    mixed = rows_all + dense(attended_low, w_out)
    normed_two_low = layer_norm(mixed, vec_params[2], vec_params[3]).astype(bf16)
    hidden = dense(normed_two_low, w_up) + hidden_bias
    active_low = jax.nn.gelu(hidden, approximate=False).astype(bf16)
    result = mixed + (dense(active_low, w_down) + vec_params[4])
    upstream = jnp.concatenate(
        [out_cotangent[0].astype(f32), glob_cotangent[0].astype(f32)], axis=0
    )
    branch_low = upstream.astype(bf16)
    grad_down = outer_sum(counted(active_low), counted(branch_low))
    bias_two_grad = jnp.sum(counted(branch_low).astype(f32), axis=0)
    d_active = dense_back(branch_low, w_down)
    gelu_pull = jax.vjp(partial(jax.nn.gelu, approximate=False), hidden)[1]
    hidden_grad_low = gelu_pull(d_active)[0].astype(bf16)
    grad_up = outer_sum(counted(normed_two_low), counted(hidden_grad_low))
    bias_grad_part = jnp.sum(counted(hidden_grad_low).astype(f32), axis=0)
    d_normed_two = dense_back(hidden_grad_low, w_up)
    mixed_grad = upstream + norm_backward(mixed, vec_params[2], vec_params[3], d_normed_two)
    gain_two, shift_two = norm_terms(counted(mixed), counted(d_normed_two))
    attn_grad_low = mixed_grad.astype(bf16)
    grad_out = outer_sum(counted(attended_low), counted(attn_grad_low))
    heads_grad_low = dense_back(attn_grad_low, w_out).astype(bf16)
    local_grad = heads_grad_low[:own_rows].reshape(halves, half_rows, HEADS, head_size)
    glob_heads_grad = heads_grad_low[own_rows:].reshape(glob_count, HEADS, head_size)
    scores_again = local_scores()
    weights_again = jnp.exp(scores_again - local_total)
    weights_again_low = weights_again.astype(bf16)
    weight_grad = jnp.concatenate(
        [
            jnp.einsum("nqhe,nkhe->nhqk", local_grad, value_blocks, preferred_element_type=f32),
            jnp.einsum("nqhe,ghe->nhqg", local_grad, glob_value, preferred_element_type=f32),
        ],
        axis=-1,
    )
    row_inner = jnp.sum(weights_again * weight_grad, axis=-1, keepdims=True)
    score_grad_low = (weights_again * (weight_grad - row_inner)).astype(bf16)
    query_grad = jnp.einsum(
        "nhqk,nkhe->nqhe", score_grad_low[..., :BLOCK], key_blocks, preferred_element_type=f32
    )
    query_grad = (
        query_grad
        + jnp.einsum(
            "nhqg,ghe->nqhe", score_grad_low[..., BLOCK:], glob_key, preferred_element_type=f32
        )
    ) * score_scale
    key_block_grad = (
        jnp.einsum(
            "nhqk,nqhe->nkhe", score_grad_low[..., :BLOCK], query_halves, preferred_element_type=f32
        )
        * score_scale
    )
    value_block_grad = jnp.einsum(
        "nhqk,nqhe->nkhe", weights_again_low[..., :BLOCK], local_grad, preferred_element_type=f32
    )
    pair_grad_ext = fold_blocks(
        jnp.concatenate(
            [
                key_block_grad.reshape(halves, BLOCK, model_width),
                value_block_grad.reshape(halves, BLOCK, model_width),
            ],
            axis=-1,
        )
    )
    glob_key_part = (
        jnp.einsum(
            "nhqg,nqhe->ghe", score_grad_low[..., BLOCK:], query_halves, preferred_element_type=f32
        )
        * score_scale
    )
    glob_value_part = jnp.einsum(
        "nhqg,nqhe->ghe", weights_again_low[..., BLOCK:], local_grad, preferred_element_type=f32
    )
    glob_pair_part = jnp.concatenate(
        [
            glob_key_part.reshape(glob_count, model_width),
            glob_value_part.reshape(glob_count, model_width),
        ],
        axis=-1,
    )
    from_right = from_behind(pair_grad_ext[:half_rows].astype(jnp.bfloat16), "seq", -1).astype(
        jnp.float32
    )
    from_left = from_behind(
        pair_grad_ext[own_rows + half_rows :].astype(jnp.bfloat16), "seq", 1
    ).astype(jnp.float32)
    pair_grad = pair_grad_ext[half_rows : own_rows + half_rows]
    pair_grad = pair_grad.at[:half_rows].add(from_left).at[own_rows - half_rows :].add(from_right)
    tokens_again, globs_again = glob_scores()
    token_weights = jnp.exp(tokens_again - glob_total)
    self_weights = jnp.exp(globs_again - glob_total)
    token_weight_grad = jnp.einsum(
        "ghe,khe->hgk", glob_heads_grad, value_own, preferred_element_type=f32
    )
    self_weight_grad = jnp.einsum(
        "ghe,jhe->hgj", glob_heads_grad, glob_value, preferred_element_type=f32
    )
    part_inner = jnp.sum(token_weights * token_weight_grad, axis=-1)
    glob_inner = summed(part_inner, bits_of("seq")) + jnp.sum(self_weights * self_weight_grad, axis=-1)
    token_score_low = (token_weights * (token_weight_grad - glob_inner[..., None])).astype(bf16)
    self_score_low = (self_weights * (self_weight_grad - glob_inner[..., None])).astype(bf16)
    glob_query_part = (
        jnp.einsum("hgk,khe->ghe", token_score_low, key_own, preferred_element_type=f32)
        * score_scale
    )
    key_from_glob = (
        jnp.einsum("hgk,ghe->khe", token_score_low, glob_query, preferred_element_type=f32)
        * score_scale
    )
    value_from_glob = jnp.einsum(
        "hgk,ghe->khe", token_weights.astype(bf16), glob_heads_grad, preferred_element_type=f32
    )
    pair_grad = pair_grad + jnp.concatenate(
        [
            key_from_glob.reshape(own_rows, model_width),
            value_from_glob.reshape(own_rows, model_width),
        ],
        axis=-1,
    )
    query_sum, pair_sum = summed(
        (glob_query_part.reshape(glob_count, model_width), glob_pair_part), bits_of("seq")
    )
    glob_query_grad = query_sum + (
        jnp.einsum("hgj,jhe->ghe", self_score_low, glob_key, preferred_element_type=f32)
        * score_scale
    ).reshape(glob_count, model_width)
    glob_key_grad = pair_sum[:, :model_width] + (
        jnp.einsum("hgj,ghe->jhe", self_score_low, glob_query, preferred_element_type=f32)
        * score_scale
    ).reshape(glob_count, model_width)
    glob_value_grad = pair_sum[:, model_width:] + jnp.einsum(
        "hgj,ghe->jhe", self_weights_low, glob_heads_grad, preferred_element_type=f32
    ).reshape(glob_count, model_width)
    qkv_grad_low = jnp.concatenate(
        [
            jnp.concatenate([query_grad.reshape(own_rows, model_width), pair_grad], axis=-1),
            jnp.concatenate([glob_query_grad, glob_key_grad, glob_value_grad], axis=-1),
        ],
        axis=0,
    ).astype(bf16)
    grad_qkv = outer_sum(counted(normed_low), counted(qkv_grad_low))
    d_normed = dense_back(qkv_grad_low, w_qkv)
    row_grad = mixed_grad + norm_backward(rows_all, vec_params[0], vec_params[1], d_normed)
    gain_one, shift_one = norm_terms(counted(rows_all), counted(d_normed))
    vec_grad_part = jnp.stack([gain_one, shift_one, gain_two, shift_two, bias_two_grad])
    batch_bits, seq_bits = bits_of("batch"), bits_of("seq")
    order_one = batch_bits + seq_bits
    order_two = batch_bits[:1] + seq_bits[:1] + batch_bits[1:] + seq_bits[1:]
    shards = (
        scattered(grad_qkv, order_two),
        scattered(grad_out, order_two),
        scattered(grad_up, order_two),
        scattered(grad_down, order_one),
    )
    decay_rate = 1.0 - STEP ** (-0.8)
    owner_index = lax.axis_index(("batch", "seq"))
    matrices = (w_qkv, w_out, w_up, w_down)
    row_olds = (row_qkv, row_out, row_up, row_down)
    col_olds = (col_qkv, col_out, col_up, col_down)
    squares = [shard_grad * shard_grad + TINY_SQUARE for shard_grad in shards]
    row_news = [
        decay_rate * old_rows + (1.0 - decay_rate) * jnp.mean(square, axis=1)
        for old_rows, square in zip(row_olds, squares)
    ]
    col_parts = [jnp.sum(square, axis=0) for square in squares]
    row_totals = jnp.stack([jnp.sum(row_new) for row_new in row_news])
    stats = summed(
        (
            col_parts[0],
            col_parts[1],
            col_parts[2],
            col_parts[3],
            row_totals,
            vec_grad_part,
            bias_grad_part,
        ),
        batch_bits + seq_bits,
    )
    updates = []
    for matrix_index in range(4):
        full_rows = matrices[matrix_index].shape[0]
        shard_rows = shards[matrix_index].shape[0]
        col_new = decay_rate * col_olds[matrix_index] + (1.0 - decay_rate) * (
            stats[matrix_index] / full_rows
        )
        row_mean = stats[4][matrix_index] / full_rows
        master = lax.dynamic_slice_in_dim(
            matrices[matrix_index], owner_index * shard_rows, shard_rows, 0
        ).astype(f32)
        estimate = row_news[matrix_index][:, None] * col_new[None, :] / row_mean
        new_weight = master - RATE_MATRIX * shards[matrix_index] * lax.rsqrt(estimate)
        updates += [shards[matrix_index], row_news[matrix_index], col_new, new_weight]
    vec_grad = stats[5]
    bias_grad = stats[6]
    vec_state_new = decay_rate * vec_state + (1.0 - decay_rate) * (
        vec_grad * vec_grad + TINY_SQUARE
    )
    vec_new = vec_params - RATE_VECTOR * vec_grad * lax.rsqrt(vec_state_new)
    bias_state_new = decay_rate * bias_state + (1.0 - decay_rate) * (
        bias_grad * bias_grad + TINY_SQUARE
    )
    bias_new = hidden_bias - RATE_VECTOR * bias_grad * lax.rsqrt(bias_state_new)
    return (
        result[:own_rows].astype(bf16)[None],
        result[own_rows:].astype(bf16)[None],
        row_grad[:own_rows][None],
        row_grad[own_rows:][None],
        updates[0],
        updates[1],
        updates[2],
        updates[3],
        updates[4],
        updates[5],
        updates[6],
        updates[7],
        updates[8],
        updates[9],
        updates[10],
        updates[11],
        updates[12],
        updates[13],
        updates[14],
        updates[15],
        vec_grad,
        vec_state_new,
        vec_new,
        bias_grad,
        bias_state_new,
        bias_new,
    )


def solution(mesh):
    in_specs = (
        P("batch", "seq", None),
        P("batch", None, None),
        P(),
        P(),
        P(),
        P(),
        P(),
        P(),
        P(("batch", "seq")),
        P(),
        P(("batch", "seq")),
        P(),
        P(("batch", "seq")),
        P(),
        P(("batch", "seq")),
        P(),
        P(),
        P(),
        P("batch", None),
        P("batch", None),
        P("batch", "seq", None),
        P("batch", None, None),
    )
    out_specs = (
        P("batch", "seq", None),
        P("batch", None, None),
        P("batch", "seq", None),
        P("batch", None, None),
        P(("batch", "seq"), None),
        P(("batch", "seq")),
        P(),
        P(("batch", "seq"), None),
        P(("batch", "seq"), None),
        P(("batch", "seq")),
        P(),
        P(("batch", "seq"), None),
        P(("batch", "seq"), None),
        P(("batch", "seq")),
        P(),
        P(("batch", "seq"), None),
        P(("batch", "seq"), None),
        P(("batch", "seq")),
        P(),
        P(("batch", "seq"), None),
        P(),
        P(),
        P(),
        P(),
        P(),
        P(),
    )
    return jax.shard_map(body, mesh=mesh, in_specs=in_specs, out_specs=out_specs, check_vma=False)
```

```python
import functools

import jax
import jax.numpy as jnp
import numpy as np
from jax import lax
from jax.experimental import pallas as pl
from jax.experimental.pallas import tpu as pltpu
from jax.sharding import PartitionSpec as P

HEADS = 12
BLOCK = 512
STEP = 10

NEG_FILL = -8e9
NORM_EPS = 1e-06
TINY_SQUARE = 1e-30
RATE_MATRIX = 0.03
RATE_VECTOR = 0.2
LANES = 128
LOG2E = 1.4426950408889634

f32, bf16 = jnp.float32, jnp.bfloat16
NN = (((1,), (0,)), ((), ()))
NT = (((1,), (1,)), ((), ()))
TN = (((0,), (0,)), ((), ()))
SDS = jax.ShapeDtypeStruct


def bits_of(axis):
    size = lax.axis_size(axis)
    assert size & (size - 1) == 0
    return [(axis, 1 << k) for k in range(size.bit_length() - 1)]


def side_of(axis, bit):
    return (lax.axis_index(axis) // bit) % 2


def swapped(values, axis, bit):
    return lax.ppermute(values, axis, [(i, i ^ bit) for i in range(lax.axis_size(axis))])


def shifted(values, axis, distance):
    devices = range(lax.axis_size(axis))
    return lax.ppermute(values, axis, [(i, i + distance) for i in devices if i + distance in devices])


def summed(parts, bits):
    leaves, tree = jax.tree.flatten(parts)
    flat = jnp.concatenate([leaf.reshape(-1) for leaf in leaves])
    count = flat.shape[0]
    flat = jnp.pad(flat, (0, -count % 1024)).reshape(-1, LANES)
    for axis, bit in bits:
        flat = flat + swapped(flat, axis, bit)
    flat = flat.reshape(-1)
    out, place = [], 0
    for leaf in leaves:
        out.append(flat[place : place + leaf.size].reshape(leaf.shape))
        place += leaf.size
    return jax.tree.unflatten(tree, out)


def flipped(values, bits, flips):
    sizes = {axis: lax.axis_size(axis) for axis in ("batch", "seq")}
    change = {axis: sum(bit for n, (name, bit) in enumerate(bits) if name == axis and flips >> n & 1) for axis in sizes}
    route = [
        (b * sizes["seq"] + s, (b ^ change["batch"]) * sizes["seq"] + (s ^ change["seq"]))
        for b in range(sizes["batch"])
        for s in range(sizes["seq"])
    ]
    return lax.ppermute(values, ("batch", "seq"), route)


def mm(a, b, dims=NN):
    return lax.dot_general(a, b, dims, preferred_element_type=f32)


def limits(mib):
    return pltpu.CompilerParams(vmem_limit_bytes=mib * 2**20)


def cost(us):
    return pl.CostEstimate(flops=int(us * 1.15e9), bytes_accessed=1 << 20, transcendentals=0)


def whole(array):
    return pl.BlockSpec(array.shape, lambda *_: (0,) * array.ndim)


def following(kernel, inputs, after):
    return lambda *refs: kernel(*refs[:inputs], *refs[inputs + len(after) :])


def untouched(after):
    return [pl.BlockSpec(memory_space=pl.ANY)] * len(after)


def normalize(x):
    mean = jnp.mean(x, axis=1, keepdims=True)
    centred = x - mean
    rstd = lax.rsqrt(jnp.mean(centred * centred, axis=1, keepdims=True) + NORM_EPS)
    return centred * rstd, rstd


def norm_back(normalized, rstd, gain, grad):
    g = grad * gain
    inner = jnp.mean(g * normalized, axis=1, keepdims=True)
    return rstd * (g - jnp.mean(g, axis=1, keepdims=True) - normalized * inner)


def gelu_both(u):
    phi = 0.5 + 0.5 * lax.erf(u * 0.7071067811865476)
    density = jnp.exp2(u * u * (-0.5 * LOG2E)) * 0.3989422804014327
    return u * phi, phi + u * density


def head_part(values, head, size):
    lanes = lax.broadcasted_iota(jnp.int32, values.shape, 1)
    return jnp.where((lanes // size) == head, values, jnp.zeros_like(values))


def stage_kernel(side_ref, kept_ref, *refs, arrived, parts):
    for n in range(parts):
        at = side_ref[0] ^ n if parts > 1 else 0
        total = kept_ref[at].astype(f32)
        for ref in refs[:arrived]:
            total = total + ref[at].astype(f32)
        out = refs[arrived + n]
        out[...] = total.astype(out.dtype)


class Scatter:
    def __init__(self, sent, kept, stages):
        self.stages, self.parts, self.kept = list(stages), [sent], kept

    def step(self, after=()):
        bits = self.stages.pop(0)
        arrived = [flipped(part, bits[::-1], n + 1) for n, part in enumerate(self.parts)]
        bits = self.stages[0] if self.stages else []
        parts, columns = 1 << len(bits), self.kept.shape[-1]
        rows = self.kept.size // columns // parts
        block = columns if self.kept.size < 1 << 20 else columns // max(1, columns // 768)
        tall = 2 if columns == block and rows % 32 == 0 and self.kept.size > 1 << 19 else 1
        args = [a.reshape(parts, rows, columns) for a in [self.kept] + arrived]
        side = sum(side_of(*bit) << n for n, bit in enumerate(reversed(bits))) if bits else jnp.int32(0)
        spec = pl.BlockSpec((parts, rows // tall, block), lambda c, r: (0, r, c))
        out = pl.BlockSpec((rows // tall, block), lambda c, r: (r, c))
        after = list(after)
        self.kept, *self.parts = pl.pallas_call(
            following(functools.partial(stage_kernel, arrived=len(arrived), parts=parts), 1 + len(args), after),
            grid=(columns // block, tall),
            in_specs=[pl.BlockSpec(memory_space=pltpu.SMEM)] + [spec] * len(args) + untouched(after),
            out_specs=[out] * parts,
            out_shape=[SDS((rows, columns), bf16 if bits else f32)] + [SDS((rows, columns), bf16)] * (parts - 1),
            compiler_params=limits(60),
            cost_estimate=cost(2),
            name="sum_stage",
        )(side.reshape(1), *args, *after)
        return self.kept


def joint_kernel(side_ref, wk_ref, wa_ref, dk_ref, da_ref, sent_ref, kept_ref, total, *, chunk, starts):
    columns = wk_ref.shape[2]
    block = dk_ref.shape[2]
    for ref, flip in ((sent_ref, 1), (kept_ref, 0)):
        at = side_ref[0] ^ flip
        ref[:, :columns] = (wk_ref[at].astype(f32) + wa_ref[at].astype(f32)).astype(bf16)
        total[...] = dk_ref[at].astype(f32) + da_ref[at].astype(f32)
        for k, places in enumerate(starts):
            ref[:, columns + k * block : columns + (k + 1) * block] = gathered(total, places, chunk)


def joint_scatter(wide, down, stages, after=()):
    (bit,) = stages[0]
    args = []
    for scatter in (wide, down):
        bits = scatter.stages.pop(0)
        arrived = flipped(scatter.parts[0], bits, 1)
        args += [a.reshape(2, -1, a.shape[-1]) for a in (scatter.kept, arrived)]
    _, rows, columns = args[0].shape
    _, rows_down, block = args[2].shape
    owners = 1 << (len(stages) - 1)
    chunk = rows // owners
    groups = rows_down // rows
    starts = [[(n * groups + k) * chunk for n in range(owners)] for k in range(groups)]
    shape = SDS((rows, columns + groups * block), bf16)
    after = list(after)
    sent, kept = pl.pallas_call(
        following(functools.partial(joint_kernel, chunk=chunk, starts=starts), 5, after),
        in_specs=[pl.BlockSpec(memory_space=pltpu.SMEM)] + [whole(a) for a in args] + untouched(after),
        out_specs=[pl.BlockSpec(shape.shape, lambda: (0, 0))] * 2,
        out_shape=[shape, shape],
        scratch_shapes=[pltpu.VMEM((rows_down, block), f32)],
        compiler_params=limits(60),
        cost_estimate=cost(3),
        name="joint_stage",
    )(side_of(*bit).reshape(1), *args, *after)
    return Scatter(sent, kept, stages)


def row_places(width, stages):
    labels = bits_of("batch")[::-1] + bits_of("seq")[::-1]
    owners = np.arange(1 << len(labels)).reshape([2] * len(labels))
    owners = owners.transpose([labels.index(bit) for stage in stages for bit in stage]).reshape(2, -1)
    chunk = width // owners.size
    return tuple(int(owner) * chunk for owner in owners[0]), chunk, int(owners[1, 0] - owners[0, 0]) * chunk


def project_kernel(tok_ref, glob_ref, w_ref, vec_ref, qkv_ref, nt_ref, n_s):
    own = tok_ref.shape[0]

    @pl.when(pl.program_id(0) == 0)
    def _():
        for ref, rows in ((tok_ref, slice(0, own)), (glob_ref, slice(own, n_s.shape[0]))):
            n = normalize(ref[...].astype(f32))[0] * vec_ref[0:1, :] + vec_ref[1:2, :]
            n = n.astype(bf16)
            n_s[rows, :] = n
            nt_ref[:, rows] = n.T

    qkv_ref[...] = mm(n_s[...], w_ref[...]).astype(bf16)


def project(tok, glob, w, vec):
    width = tok.shape[1]
    rows = tok.shape[0] + glob.shape[0]
    return pl.pallas_call(
        project_kernel,
        grid=(w.shape[1] // width,),
        in_specs=[whole(tok), whole(glob), pl.BlockSpec((width, width), lambda c: (0, c)), whole(vec)],
        out_specs=[
            pl.BlockSpec((rows, width), lambda c: (0, c)),
            pl.BlockSpec((width, rows), lambda c: (0, 0)),
        ],
        out_shape=[SDS((rows, w.shape[1]), bf16), SDS((width, rows), bf16)],
        scratch_shapes=[pltpu.VMEM((rows, width), bf16)],
        compiler_params=limits(60),
        cost_estimate=cost(9),
        name="project",
    )(tok, glob, w, vec)


def halo_kernel(l_ref, r_ref, w_ref, vec_ref, lkv_ref, rkv_ref, nt_ref):
    half = l_ref.shape[0]
    for ref, out, at in ((l_ref, lkv_ref, 0), (r_ref, rkv_ref, half)):
        n = normalize(ref[...].astype(f32))[0] * vec_ref[0:1, :] + vec_ref[1:2, :]
        n = n.astype(bf16)
        nt_ref[:, at : at + half] = n.T
        out[...] = mm(n, w_ref[...]).astype(bf16)


def project_halos(left, right, w, vec):
    half, width = left.shape
    kv = pl.BlockSpec((half, width), lambda c: (0, c))
    return pl.pallas_call(
        halo_kernel,
        grid=(2,),
        in_specs=[whole(left), whole(right), pl.BlockSpec((width, width), lambda c: (0, c + 1)), whole(vec)],
        out_specs=[kv, kv, pl.BlockSpec((width, 2 * half), lambda c: (0, 0))],
        out_shape=[SDS((half, 2 * width), bf16)] * 2 + [SDS((width, 2 * half), bf16)],
        compiler_params=limits(60),
        cost_estimate=cost(3),
        name="project_halos",
    )(left, right, w, vec)


def attend(q, keys, values, coef):
    scores = mm(q, keys, NT) * coef
    top = jnp.max(scores, axis=1, keepdims=True)
    p = jnp.exp2(scores - top)
    return mm(p.astype(bf16), values), top, jnp.sum(p, axis=1, keepdims=True)


def mask_piece(kx_ref, name, low, rows, own, half):
    if name == "l":
        start = low
    elif name == "r":
        start = half + own + low
    else:
        start = half + low if low < own else 2 * half + low
    return kx_ref[start : start + rows, :]


def fill_inner(src, dst, own, half):
    for b in range(dst.shape[0]):
        low = half + b * 2 * half
        dst[b, : 2 * half, :LANES] = src[low : low + 2 * half]
        dst[b, 2 * half :, :LANES] = src[own:]


def fill_inner_masks(kx_ref, dst, own, half, glob):
    for b in range(dst.shape[0]):
        dst[b, : 2 * half, LANES:] = mask_piece(kx_ref, "o", half + b * 2 * half, 2 * half, own, half)
        dst[b, 2 * half :, LANES:] = mask_piece(kx_ref, "o", own, glob, own, half)


def fill_edges(src, l_ref, r_ref, dst, own, half):
    dst[0, :half, :LANES] = l_ref[...]
    dst[0, half : 2 * half, :LANES] = src[:half]
    dst[1, :half, :LANES] = src[own - half : own]
    dst[1, half : 2 * half, :LANES] = r_ref[...]
    for b in range(2):
        dst[b, 2 * half :, :LANES] = src[own:]


def fill_edge_masks(kx_ref, dst, own, half, glob):
    for at, name, low in ((0, "l", 0), (1, "o", 0), (2, "o", own - half), (3, "r", 0)):
        dst[at // 2, at % 2 * half : (at % 2 + 1) * half, LANES:] = mask_piece(kx_ref, name, low, half, own, half)
    for b in range(2):
        dst[b, 2 * half :, LANES:] = mask_piece(kx_ref, "o", own, glob, own, half)


def local_rows(q_ref, qx_ref, rows, k, v, lse, step, size, coef):
    lane = lax.broadcasted_iota(jnp.int32, (rows.stop - rows.start, LANES), 1)
    outs = []
    for h in range(2):
        q = jnp.concatenate([head_part(q_ref[rows, :], h, size), qx_ref[rows, :]], axis=1)
        o, top, total = attend(q, k, v, coef)
        outs.append(o * (1.0 / total))
        lse = jnp.where(lane == 2 * step + h, top + jnp.log2(total), lse)
    return jnp.where(lane < size, outs[0], outs[1]).astype(bf16), lse


def local_inner_kernel(q_ref, k_ref, v_ref, qx_ref, kx_ref, o_ref, lse_ref, ks, vs, *, size, coef, own, half):
    step = pl.program_id(0)
    glob = k_ref.shape[0] - own

    @pl.when(step == 0)
    def _():
        fill_inner_masks(kx_ref, ks, own, half, glob)
        lse_ref[...] = jnp.zeros_like(lse_ref)

    fill_inner(k_ref, ks, own, half)
    fill_inner(v_ref, vs, own, half)
    for j in range(own // half - 2):
        rows, there = slice((j + 1) * half, (j + 2) * half), slice(j * half, (j + 1) * half)
        o, lse = local_rows(q_ref, qx_ref, rows, ks[j // 2], vs[j // 2], lse_ref[there, :], step, size, coef)
        o_ref[there, :], lse_ref[there, :] = o, lse


def local_edge_kernel(q_ref, k_ref, v_ref, lk_ref, lv_ref, rk_ref, rv_ref, qx_ref, kx_ref, io_ref, ilse_ref, o_ref, lse_ref, ks, vs, *, size, coef):
    step = pl.program_id(0)
    own, half = q_ref.shape[0], lk_ref.shape[0]
    glob = k_ref.shape[0] - own

    @pl.when(step == 0)
    def _():
        fill_edge_masks(kx_ref, ks, own, half, glob)
        lse_ref[...] = jnp.zeros_like(lse_ref)
        lse_ref[half : own - half, :] = ilse_ref[...]

    fill_edges(k_ref, lk_ref, rk_ref, ks, own, half)
    fill_edges(v_ref, lv_ref, rv_ref, vs, own, half)
    o_ref[half : own - half, :] = io_ref[...]
    for b, rows in enumerate((slice(0, half), slice(own - half, own))):
        o_ref[rows, :], lse_ref[rows, :] = local_rows(q_ref, qx_ref, rows, ks[b], vs[b], lse_ref[rows, :], step, size, coef)


def local_inner(qkv, qx, kx, own, half, size, coef, after=()):
    rows, width = qkv.shape[0], qkv.shape[1] // 3
    pairs, inner = width // LANES, own - 2 * half
    blocks, span = own // (2 * half) - 1, 2 * half + rows - own

    def cols(n, off=0):
        return pl.BlockSpec((n, LANES), lambda p: (0, p + off))

    def fixed(n):
        return pl.BlockSpec((n, LANES), lambda p: (0, 0))

    return pl.pallas_call(
        following(functools.partial(local_inner_kernel, size=size, coef=coef, own=own, half=half), 5, after),
        grid=(pairs,),
        in_specs=[cols(own), cols(rows, pairs), cols(rows, 2 * pairs), fixed(own), whole(kx)] + untouched(after),
        out_specs=[cols(inner), fixed(inner)],
        out_shape=[SDS((inner, width), bf16), SDS((inner, LANES), f32)],
        scratch_shapes=[pltpu.VMEM((blocks, span, 2 * LANES), bf16), pltpu.VMEM((blocks, span, LANES), bf16)],
        compiler_params=limits(60),
        cost_estimate=cost(12),
        name="local_inner",
    )(qkv, qkv, qkv, qx, kx, *after)


def local_edge(qkv, left, right, qx, kx, io, ilse, own, half, size, coef, after=()):
    rows, width = qkv.shape[0], qkv.shape[1] // 3
    pairs, inner, span = width // LANES, own - 2 * half, 2 * half + rows - own

    def cols(n, off=0):
        return pl.BlockSpec((n, LANES), lambda p: (0, p + off))

    def fixed(n):
        return pl.BlockSpec((n, LANES), lambda p: (0, 0))

    return pl.pallas_call(
        following(functools.partial(local_edge_kernel, size=size, coef=coef), 11, after),
        grid=(pairs,),
        in_specs=[cols(own), cols(rows, pairs), cols(rows, 2 * pairs), cols(half), cols(half, pairs), cols(half), cols(half, pairs), fixed(own), whole(kx), cols(inner), fixed(inner)] + untouched(after),
        out_specs=[cols(own), fixed(own)],
        out_shape=[SDS((own, width), bf16), SDS((own, LANES), f32)],
        scratch_shapes=[pltpu.VMEM((2, span, 2 * LANES), bf16), pltpu.VMEM((2, span, LANES), bf16)],
        compiler_params=limits(60),
        cost_estimate=cost(12),
        name="local_edge",
    )(qkv, qkv, qkv, left, left, right, right, qx, kx, io, ilse, *after)


def to_thirds(lse):
    high = lse.astype(bf16).astype(f32)
    middle = (lse - high).astype(bf16).astype(f32)
    low = lse - high - middle
    lane = lax.broadcasted_iota(jnp.int32, lse.shape, 1)
    packed = jnp.where(lane < 16, high, jnp.where(lane < 32, pltpu.roll(middle, 16, 1), pltpu.roll(low, 32, 1)))
    return jnp.where(lane < 48, packed, 0.0).astype(bf16)


def from_thirds(packed):
    packed = packed.astype(f32)
    lane = lax.broadcasted_iota(jnp.int32, packed.shape, 1)
    total = packed + (pltpu.roll(packed, LANES - 16, 1) + pltpu.roll(packed, LANES - 32, 1))
    return jnp.where(lane < 16, total, 0.0)


def glob_kernel(q_ref, k_ref, v_ref, qx_ref, kx_ref, out_ref, ks, lse_ref, *, size, coef, half):
    step = pl.program_id(0)
    glob = q_ref.shape[0]
    own = k_ref.shape[0] - glob

    @pl.when(step == 0)
    def _():
        ks[:own, LANES:] = kx_ref[half : half + own, :]
        ks[own:, LANES:] = kx_ref[2 * half + own :, :]
        lse_ref[...] = jnp.zeros_like(lse_ref)

    ks[:, :LANES] = k_ref[...]
    lane = lax.broadcasted_iota(jnp.int32, q_ref.shape, 1)
    lse, outs = lse_ref[...], []
    for h in range(2):
        q = jnp.concatenate([head_part(q_ref[...], h, size), qx_ref[...]], axis=1)
        o, top, total = attend(q, ks[...], v_ref[...], coef)
        outs.append(o * (1.0 / total))
        lse = jnp.where(lane == 2 * step + h, top + jnp.log2(total), lse)
    lse_ref[...] = lse
    out_ref[:, pl.ds(pl.multiple_of(step * LANES, LANES), LANES)] = jnp.where(lane < size, outs[0], outs[1]).astype(bf16)

    @pl.when(step == pl.num_programs(0) - 1)
    def _():
        out_ref[:, out_ref.shape[1] - LANES :] = to_thirds(lse)


def glob_attention(qkv, qx, kx, own, half, size, coef):
    rows, width = qkv.shape[0], qkv.shape[1] // 3
    pairs, glob = width // LANES, rows - own
    at = own // glob

    def cols(off):
        return pl.BlockSpec((rows, LANES), lambda p: (0, p + off))

    return pl.pallas_call(
        functools.partial(glob_kernel, size=size, coef=coef, half=half),
        grid=(pairs,),
        in_specs=[pl.BlockSpec((glob, LANES), lambda p: (at, p)), cols(pairs), cols(2 * pairs), pl.BlockSpec((glob, LANES), lambda p: (at, 0)), whole(kx)],
        out_specs=pl.BlockSpec((glob, width + LANES), lambda p: (0, 0)),
        out_shape=SDS((glob, width + LANES), bf16),
        scratch_shapes=[pltpu.VMEM((rows, 2 * LANES), bf16), pltpu.VMEM((glob, LANES), f32)],
        compiler_params=limits(60),
        cost_estimate=cost(8),
        name="glob_attention",
    )(qkv, qkv, qkv, qx, kx)


def merge_kernel(upper_ref, own_ref, other_ref, out_ref, lse_ref, *, size):
    upper = upper_ref[0] == 1
    width = own_ref.shape[1] - LANES
    own_l, other_l = from_thirds(own_ref[:, width:]), from_thirds(other_ref[:, width:])
    first, second = jnp.where(upper, other_l, own_l), jnp.where(upper, own_l, other_l)
    top = jnp.maximum(first, second)
    wa, wb = jnp.exp2(first - top), jnp.exp2(second - top)
    total = wa + wb
    lse = top + jnp.log2(total)
    lane = lax.broadcasted_iota(jnp.int32, lse.shape, 1)
    lse = jnp.where(lane < 16, lse, 0.0)
    lse_ref[...] = lse
    out_ref[:, width:] = to_thirds(lse)
    wa, wb = wa / total, wb / total
    for p in range(width // LANES):
        at = slice(p * LANES, (p + 1) * LANES)
        own_o, other_o = own_ref[:, at].astype(f32), other_ref[:, at].astype(f32)
        a, b = jnp.where(upper, other_o, own_o), jnp.where(upper, own_o, other_o)
        ka = jnp.where(lane < size, wa[:, 2 * p : 2 * p + 1], wa[:, 2 * p + 1 : 2 * p + 2])
        kb = jnp.where(lane < size, wb[:, 2 * p : 2 * p + 1], wb[:, 2 * p + 1 : 2 * p + 2])
        out_ref[:, at] = (a * ka + b * kb).astype(bf16)


def merge_step(part, axis, bit, size, after=()):
    other = swapped(part, axis, bit)
    return pl.pallas_call(
        following(functools.partial(merge_kernel, size=size), 3, after),
        in_specs=[pl.BlockSpec(memory_space=pltpu.SMEM), whole(part), whole(part)] + untouched(after),
        out_specs=[whole(part), pl.BlockSpec((part.shape[0], LANES), lambda: (0, 0))],
        out_shape=[SDS(part.shape, bf16), SDS((part.shape[0], LANES), f32)],
        cost_estimate=cost(2),
        name="merge",
    )(side_of(axis, bit).reshape(1), part, other, *after)


def gathered(total, starts, chunk, shift=0):
    if chunk % 8 == 0:
        rows = [total[pl.ds(pl.multiple_of(start + shift, 8), chunk), :] for start in starts]
        return jnp.concatenate(rows, axis=0).astype(bf16)
    shape = (len(starts) * chunk, total.shape[0])
    place, row = lax.broadcasted_iota(jnp.int32, shape, 0), lax.broadcasted_iota(jnp.int32, shape, 1)
    wanted = place % chunk + shift
    for n, start in enumerate(starts):
        wanted = wanted + jnp.where(place // chunk == n, start, 0)
    return mm((wanted == row).astype(f32).astype(bf16), total[...].astype(bf16)).astype(bf16)


def split_rows(total, side, sent_ref, kept_ref, places):
    starts, chunk, apart = places
    sent_ref[...] = gathered(total, starts, chunk, (1 - side) * apart)
    kept_ref[...] = gathered(total, starts, chunk, side * apart)


def ffn_kernel(side_ref, flag_ref, att_ref, gatt_ref, tok_ref, glob_ref, wo_ref, up_ref, down_ref, vec_ref, bias_ref, br_tok_ref, br_glob_ref,
               out_tok_ref, out_glob_ref, mg_ref, hd_ref, wsent_ref, wkept_ref, dsent_ref, dkept_ref, vsum_ref, bsum_ref,
               att_s, n2s, n2t, br, act_s, hg_s, res_s, dn_s, total, *, places, tall_places, pieces):
    step, last = pl.program_id(0), pl.num_programs(0) - 1
    own, width = tok_ref.shape
    rows = br.shape[0]
    flag = flag_ref[0]
    side = side_ref[0]
    size, steps = rows // pieces, act_s.shape[0]

    def at(n):
        return pl.ds(pl.multiple_of(n * size, size), size)

    def counted(x):
        return (x.astype(f32) * flag).astype(bf16)

    @pl.when(step == 0)
    def _():
        br[:own] = br_tok_ref[...]
        br[own:] = br_glob_ref[...]
        att_s[:own] = att_ref[...]
        att_s[own:] = gatt_ref[:, :width]
        mg_ref[:own] = tok_ref[...].astype(f32)
        mg_ref[own:] = glob_ref[...].astype(f32)

        def block(n, _):
            here = at(n)
            mixed = mg_ref[here, :] + mm(att_s[here, :], wo_ref[...])
            mg_ref[here, :] = mixed
            n2 = (normalize(mixed)[0] * vec_ref[2:3, :] + vec_ref[3:4, :]).astype(bf16)
            n2s[here, :] = n2
            res_s[here, :] = mixed + vec_ref[4:5, :]
            return 0

        lax.fori_loop(0, pieces, block, 0)
        n2t[:, :own] = n2s[:own, :].T
        n2t[:, own:] = counted(n2s[own:, :]).T
        dn_s[...] = jnp.zeros_like(dn_s)

    @pl.when((step >= steps) & (step < last))
    def _():
        slot = step - steps
        total[...] = mm(n2t[...], hg_s[slot])
        split_rows(total, side, wsent_ref, wkept_ref, places)
        hg = hg_s[slot].astype(f32)
        bsum_ref[...] = jnp.sum(hg[:own], axis=0, keepdims=True) + flag * jnp.sum(hg[own:], axis=0, keepdims=True)
        act_s[slot, own:, :] = counted(act_s[slot, own:, :])
        total[...] = mm(act_s[slot], br[...], TN)
        starts, rows_each = tall_places
        grad = gathered(total, starts, rows_each)
        part_rows = dsent_ref.shape[2]
        mine = slot % 2 == side
        for ref, wanted in ((dkept_ref, mine), (dsent_ref, jnp.logical_not(mine))):

            @pl.when(wanted)
            def _():
                for n in range(ref.shape[0]):
                    ref[n, 0] = grad[n * part_rows : (n + 1) * part_rows]

    @pl.when(step < steps)
    def _():
        slot = step

        def block(n, _):
            here = at(n)
            hidden = mm(n2s[here, :], up_ref[...]) + bias_ref[...]
            d_active = mm(br[here, :], down_ref[...], NT)
            active, slope = gelu_both(hidden)
            active = active.astype(bf16)
            hg = (d_active * slope).astype(bf16)
            act_s[slot, here, :] = active
            hg_s[slot, here, :] = hg
            res_s[here, :] += mm(active, down_ref[...])
            dn_s[here, :] += mm(hg, up_ref[...], NT)
            return 0

        lax.fori_loop(0, pieces, block, 0)

    @pl.when(step == last)
    def _():
        def block(n, sums):
            here = at(n)
            normalized, rstd = normalize(mg_ref[here, :])
            dn = dn_s[here, :]
            bf = br[here, :].astype(f32)
            mg = bf + norm_back(normalized, rstd, vec_ref[2:3, :], dn)
            mg_ref[here, :] = mg
            ag = mg.astype(bf16)
            hd_ref[here, :] = mm(ag, wo_ref[...], NT).astype(bf16)
            row = lax.broadcasted_iota(jnp.int32, (size, 1), 0) + n * size
            keep = jnp.where(row < own, 1.0, flag)
            n2s[here, :] = (ag.astype(f32) * keep).astype(bf16)
            dn = dn * keep
            return tuple(total + jnp.sum(term, axis=0, keepdims=True) for total, term in zip(sums, (dn * normalized, dn, bf * keep)))

        zero = jnp.zeros((1, width), f32)
        sums = lax.fori_loop(0, pieces, block, (zero, zero, zero))
        vsum_ref[...] = jnp.concatenate(list(sums) + [jnp.zeros((5, width), f32)], axis=0)

        total[...] = mm(att_s[...], n2s[...], TN)
        split_rows(total, side, wsent_ref, wkept_ref, places)
        out_tok_ref[...] = res_s[:own, :].astype(bf16)
        out_glob_ref[...] = res_s[own:, :].astype(bf16)


def feed_forward(side, flag, att, gatt, tok, glob, wo, up, down, vec, bias, br_tok, br_glob, places, tall_places):
    own, width = tok.shape
    glob_rows = glob.shape[0]
    rows, units, chunk = own + glob_rows, up.shape[1], width
    steps = units // chunk
    pairs = lax.axis_size("batch") // 2
    assert steps == 2 * pairs

    def fixed(n):
        return pl.BlockSpec((n, width), lambda c: (0, 0))

    def once(array):
        return pl.BlockSpec(array.shape, lambda c: (0,) * array.ndim, pipeline_mode=pl.Buffered(1))

    def now(c):
        return jnp.minimum(c, steps - 1)

    def before(c):
        return jnp.clip(c - steps, 0, steps - 1)

    wide = pl.BlockSpec((width // 2, chunk), lambda c: (0, jnp.maximum(c - steps, 0)))
    parts = 2
    tall = pl.BlockSpec((parts, 1, chunk // parts, width), lambda c: (0, before(c) // 2, 0, 0))
    wide_shape = SDS((width // 2, units + width), bf16)
    tall_shape = SDS((parts, pairs, chunk // parts, width), bf16)
    smem = pl.BlockSpec(memory_space=pltpu.SMEM)
    low, full = pltpu.VMEM((rows, width), bf16), pltpu.VMEM((rows, width), f32)
    both = pltpu.VMEM((steps, rows, chunk), bf16)
    return pl.pallas_call(
        functools.partial(ffn_kernel, places=places, tall_places=tall_places, pieces=3),
        grid=(2 * steps + 1,),
        in_specs=[
            smem, smem, once(att), once(gatt), once(tok), once(glob), once(wo),
            pl.BlockSpec((width, chunk), lambda c: (0, now(c))), pl.BlockSpec((chunk, width), lambda c: (now(c), 0)), whole(vec),
            pl.BlockSpec((1, chunk), lambda c: (0, now(c))), once(br_tok), once(br_glob),
        ],
        out_specs=[
            fixed(own), fixed(glob_rows), fixed(rows), fixed(rows), wide, wide, tall, tall, fixed(8), pl.BlockSpec((1, chunk), lambda c: (0, before(c))),
        ],
        out_shape=[
            SDS((own, width), bf16), SDS((glob_rows, width), bf16), SDS((rows, width), f32), SDS((rows, width), bf16),
            wide_shape, wide_shape, tall_shape, tall_shape, SDS((8, width), f32), SDS((1, units), f32),
        ],
        scratch_shapes=[low, low, pltpu.VMEM((width, rows), bf16), low, both, both, full, full, pltpu.VMEM((width, width), f32)],
        compiler_params=limits(63),
        cost_estimate=cost(55),
        name="feed_forward",
    )(side, flag, att, gatt, tok, glob, wo, up, down, vec, bias, br_tok, br_glob)


def score_grads(k, v, q, do, lse_row, delta_row, coef):
    p = jnp.exp2(mm(k, q, NT) * coef - lse_row)
    ds = p * (mm(v, do, NT) - delta_row)
    return p.astype(bf16), ds.astype(bf16)


class Tile:
    def __init__(self, step, q_ref, qx_ref, do, lse_t, delta_t, size, coef, scale):
        self.q_ref, self.qx_ref, self.do = q_ref, qx_ref, do
        self.lse_t = [lse_t[pl.ds(2 * step + h, 1), :] for h in range(2)]
        self.delta_t, self.size, self.coef, self.scale = delta_t, size, coef, scale

    def __call__(self, rows, do_rows, k, v):
        kt = k[:, :LANES].T
        dqs, ps, dss, qs, dos = [], [], [], [], []
        for h in range(2):
            q = head_part(self.q_ref[rows, :], h, self.size)
            do = head_part(self.do[do_rows, :], h, self.size)
            p, ds = score_grads(k, v, jnp.concatenate([q, self.qx_ref[rows, :]], axis=1), do, self.lse_t[h][:, do_rows], self.delta_t[h][:, do_rows], self.coef)
            dqs.append(mm(kt[h * self.size : (h + 1) * self.size], ds))
            ps.append(p), dss.append(ds), qs.append(q), dos.append(do)
        dq = (jnp.concatenate(dqs, axis=0).T * self.scale).astype(bf16)
        dk = mm(jnp.concatenate(dss, axis=1), jnp.concatenate(qs, axis=0))
        dv = mm(jnp.concatenate(ps, axis=1), jnp.concatenate(dos, axis=0))
        return dq, dk, dv


def inner_rows(o, do, size):
    prod = (o.astype(f32) * do.astype(f32)).T
    return [jnp.sum(prod[h * size : (h + 1) * size], axis=0, keepdims=True) for h in range(2)]


def edge_kernel(q_ref, k_ref, v_ref, lk_ref, lv_ref, rk_ref, rv_ref, qx_ref, kx_ref, o_ref, do_ref, lse_ref,
                dq_ref, dkv_ref, dg_ref, dl_ref, dr_ref, ks, vs, lses, *, size, coef, scale, own):
    step = pl.program_id(0)
    half = lk_ref.shape[0]
    glob = k_ref.shape[0] - own
    low = own - half

    @pl.when(step == 0)
    def _():
        fill_edge_masks(kx_ref, ks, own, half, glob)
        lses[:, :half] = lse_ref[:half].T
        lses[:, half:] = lse_ref[low:].T

    fill_edges(k_ref, lk_ref, rk_ref, ks, own, half)
    fill_edges(v_ref, lv_ref, rv_ref, vs, own, half)
    do = jnp.concatenate([do_ref[:half], do_ref[low:own]], axis=0)
    o = jnp.concatenate([o_ref[:half], o_ref[low:own]], axis=0)
    tile = Tile(step, q_ref, qx_ref, do, lses, inner_rows(o, do, size), size, coef, scale)
    tails = []
    for b, rows in enumerate((slice(0, half), slice(low, own))):
        there = slice(b * half, (b + 1) * half)
        dq, dk, dv = tile(rows, there, ks[b], vs[b])
        dq_ref[there, :] = dq
        dk = dk * scale
        inside, outside = (slice(half, 2 * half), slice(0, half)) if b == 0 else (slice(0, half), slice(half, 2 * half))
        for n, part in enumerate((dk, dv)):
            dkv_ref[n, there, :] = part[inside]
            (dl_ref, dr_ref)[b][n] = part[outside].astype(bf16)
        tails.append((dk[2 * half :], dv[2 * half :]))
    for n in range(2):
        dg_ref[n] = tails[0][n] + tails[1][n]


def edge_backward(qkv, left, right, qx, kx, o, do, lse, own, size, coef, scale, after=()):
    rows, width = qkv.shape[0], qkv.shape[1] // 3
    pairs, half, glob = width // LANES, left.shape[0], rows - own

    def cols(n, off):
        return pl.BlockSpec((n, LANES), lambda p: (0, p + off))

    def both(n):
        return pl.BlockSpec((2, n, LANES), lambda p: (0, 0, p))

    fixed = pl.BlockSpec((own, LANES), lambda p: (0, 0))
    return pl.pallas_call(
        following(functools.partial(edge_kernel, size=size, coef=coef, scale=scale, own=own), 12, after),
        grid=(pairs,),
        in_specs=[
            cols(own, 0), cols(rows, pairs), cols(rows, 2 * pairs), cols(half, 0), cols(half, pairs), cols(half, 0), cols(half, pairs),
            fixed, whole(kx), cols(own, 0), cols(own, 0), fixed,
        ] + untouched(after),
        out_specs=[cols(2 * half, 0), both(2 * half), both(glob), both(half), both(half)],
        out_shape=[SDS((2 * half, width), bf16), SDS((2, 2 * half, width), f32), SDS((2, glob, width), f32)] + [SDS((2, half, width), bf16)] * 2,
        scratch_shapes=[
            pltpu.VMEM((2, 2 * half + glob, 2 * LANES), bf16), pltpu.VMEM((2, 2 * half + glob, LANES), bf16), pltpu.VMEM((LANES, 2 * half), f32),
        ],
        compiler_params=limits(60),
        cost_estimate=cost(17),
        name="edge_backward",
    )(qkv, qkv, qkv, left, left, right, right, qx, kx, o, do, lse, *after)


def inner_kernel(q_ref, k_ref, v_ref, qx_ref, kx_ref, o_ref, go_ref, do_ref, lse_ref, glse_ref, edq_ref, edkv_ref, edg_ref,
                 dq_ref, dkv_ref, ks, vs, lses, acc, *, size, coef, scale, own, half, first_pair):
    step = pl.program_id(0)
    rows = k_ref.shape[0]
    glob = rows - own
    blocks = ks.shape[0]
    pair = first_pair + step

    @pl.when(step == 0)
    def _():
        fill_inner_masks(kx_ref, ks, own, half, glob)
        lses[:, :own] = lse_ref[...].T
        lses[:, own:] = glse_ref[...].T

    fill_inner(k_ref, ks, own, half)
    fill_inner(v_ref, vs, own, half)
    o = jnp.concatenate([o_ref[...], go_ref[...]], axis=0)
    tile = Tile(pair, q_ref, qx_ref, do_ref, lses, inner_rows(o, do_ref[...], size), size, coef, scale)
    kx_own = jnp.concatenate([kx_ref[half : half + own, :], kx_ref[2 * half + own :, :]], axis=0)
    at = slice(own, rows)
    dq, dk, dv = tile(at, at, jnp.concatenate([k_ref[...], kx_own], axis=1), v_ref[...])
    dq_ref[at, :] = dq
    acc[0], acc[1] = dk * scale, dv
    for b in range(blocks):
        low = half + b * 2 * half
        for j in range(2):
            at = slice(low + j * half, low + (j + 1) * half)
            dq, dk, dv = tile(at, at, ks[b], vs[b])
            dq_ref[at, :] = dq
            dk = dk * scale
            for n, part in enumerate((dk, dv)):
                acc[n, low : low + 2 * half, :] += part[: 2 * half]
                acc[n, own:, :] += part[2 * half :]
    dq_ref[:half, :] = edq_ref[:half]
    dq_ref[own - half : own, :] = edq_ref[half:]
    for n in range(2):
        acc[n, :half, :] += edkv_ref[n, :half]
        acc[n, own - half : own, :] += edkv_ref[n, half:]
        acc[n, own:, :] += edg_ref[n]
    dkv_ref[...] = acc[...].astype(bf16)


def inner_backward(group, groups, qkv, qx, kx, o, go, do, lse, glse, edq, edkv, edg, own, half, size, coef, scale, after=()):
    rows, width = qkv.shape[0], qkv.shape[1] // 3
    pairs, glob = width // LANES, rows - own
    here = pairs // groups
    base = group * here
    blocks = own // (2 * half) - 1

    def cols(n, off=0):
        return pl.BlockSpec((n, LANES), lambda p: (0, base + p + off))

    def both(n):
        return pl.BlockSpec((2, n, LANES), lambda p: (0, 0, base + p))

    return pl.pallas_call(
        following(functools.partial(inner_kernel, size=size, coef=coef, scale=scale, own=own, half=half, first_pair=base), 13, after),
        grid=(here,),
        in_specs=[
            cols(rows), cols(rows, pairs), cols(rows, 2 * pairs), whole(qx), whole(kx), cols(own), cols(glob), cols(rows), whole(lse), whole(glse),
            cols(2 * half), both(2 * half), both(glob),
        ] + untouched(after),
        out_specs=[pl.BlockSpec((rows, LANES), lambda p: (0, p)), pl.BlockSpec((2, rows, LANES), lambda p: (0, 0, p))],
        out_shape=[SDS((rows, here * LANES), bf16), SDS((2, rows, here * LANES), bf16)],
        scratch_shapes=[
            pltpu.VMEM((blocks, 2 * half + glob, 2 * LANES), bf16), pltpu.VMEM((blocks, 2 * half + glob, LANES), bf16),
            pltpu.VMEM((LANES, rows), f32), pltpu.VMEM((2, rows, LANES), f32),
        ],
        compiler_params=limits(60),
        cost_estimate=cost(13),
        name="inner_backward",
    )(qkv, qkv, qkv, qx, kx, o, go, do, lse, glse, edq, edkv, edg, *after)


def weight_kernel(side_ref, nt_ref, ht_ref, dq_ref, dkv_ref, l_ref, r_ref, sent_ref, kept_ref, total, *, places):
    step = pl.program_id(0)

    @pl.when(step == 0)
    def _():
        total[...] = mm(nt_ref[...], dq_ref[...])

    @pl.when(step > 0)
    def _():
        total[...] = mm(nt_ref[...], dkv_ref[0]) + mm(ht_ref[...], jnp.concatenate([l_ref[0], r_ref[0]], axis=0))

    split_rows(total, side_ref[0], sent_ref, kept_ref, places)


def qkv_weight_grad(group, side, nt, ht, dq, dkv, dl, dr, places, after=()):
    width, rows = nt.shape
    cols, half = dq.shape[1], dl.shape[1]
    out = pl.BlockSpec((width // 2, cols), lambda c: (0, c))
    shape = SDS((width // 2, 3 * cols), bf16)
    halo = pl.BlockSpec((1, half, cols), lambda c: (jnp.maximum(c - 1, 0), 0, group))
    return pl.pallas_call(
        following(functools.partial(weight_kernel, places=places), 7, after),
        grid=(3,),
        in_specs=[
            pl.BlockSpec(memory_space=pltpu.SMEM), whole(nt), whole(ht), whole(dq),
            pl.BlockSpec((1, rows, cols), lambda c: (jnp.maximum(c - 1, 0), 0, 0)), halo, halo,
        ] + untouched(after),
        out_specs=[out, out],
        out_shape=[shape, shape],
        scratch_shapes=[pltpu.VMEM((width, cols), f32)],
        compiler_params=limits(60),
        cost_estimate=cost(5),
        name="qkv_weight_grad",
    )(side, nt, ht, dq, dkv, dl, dr, *after)


def norm_rows(x_ref, gain, dn):
    normalized, rstd = normalize(x_ref[...].astype(f32))
    sums = [jnp.sum(dn * normalized, axis=0, keepdims=True), jnp.sum(dn, axis=0, keepdims=True)]
    return norm_back(normalized, rstd, gain, dn), jnp.concatenate(sums + [jnp.zeros((6, dn.shape[1]), f32)], axis=0)


def halo_rows_kernel(lt_ref, rt_ref, vec_ref, w_ref, l_ref, r_ref, lout_ref, rout_ref, sums_ref):
    width = lt_ref.shape[1]
    sums = 0.0
    for x_ref, d_ref, out_ref in ((lt_ref, l_ref, lout_ref), (rt_ref, r_ref, rout_ref)):
        dn = mm(d_ref[0], w_ref[:, width : 2 * width], NT) + mm(d_ref[1], w_ref[:, 2 * width :], NT)
        back, part = norm_rows(x_ref, vec_ref[0:1, :], dn)
        out_ref[...] = back.astype(bf16)
        sums = sums + part
    sums_ref[...] = sums


def halo_rows(left, right, vec, w, dl, dr, after=()):
    args = (left, right, vec, w, dl, dr)
    half, width = left.shape
    return pl.pallas_call(
        following(halo_rows_kernel, len(args), after),
        in_specs=[whole(a) for a in args] + untouched(after),
        out_specs=[whole(left), whole(right), pl.BlockSpec((8, width), lambda: (0, 0))],
        out_shape=[SDS(left.shape, bf16), SDS(right.shape, bf16), SDS((8, width), f32)],
        compiler_params=limits(60),
        cost_estimate=cost(4),
        name="halo_rows",
    )(*args, *after)


def rows_kernel(flag_ref, x_ref, vec_ref, mg_ref, w_ref, *refs, groups, edges):
    width = x_ref.shape[1]
    step, last = pl.program_id(0), pl.num_programs(0) - 1
    out_ref, sums_ref = refs[-2:]
    cols = width // groups
    dn = 0.0
    for g in range(groups):
        dq_ref, dkv_ref = refs[2 * g : 2 * g + 2]
        for part, d in enumerate((dq_ref[...], dkv_ref[0], dkv_ref[1])):
            at = part * width + g * cols
            dn = dn + mm(d, w_ref[:, at : at + cols], NT)
    back, sums = norm_rows(x_ref, vec_ref[0:1, :], dn)
    out = mg_ref[...] * flag_ref[0] + back
    out_ref[...] = out.astype(out_ref.dtype)

    @pl.when(step == 0)
    def _():
        sums_ref[...] = sums

    @pl.when(step > 0)
    def _():
        sums_ref[...] += sums

    if edges:
        l_ref, r_ref = refs[2 * groups : 2 * groups + 2]

        @pl.when(step == 0)
        def _():
            out_ref[...] = out + l_ref[...].astype(f32)

        @pl.when(step == last)
        def _():
            out_ref[...] = out + r_ref[...].astype(f32)


def row_grads(flag, x, vec, mg, w, parts, start, block, dtype, edges=(), after=()):
    count, width = x.shape
    groups = len(parts)
    cols = width // groups
    base = start // block
    specs, args = [], []
    for dq, dkv in parts:
        specs += [pl.BlockSpec((block, cols), lambda r: (base + r, 0)), pl.BlockSpec((2, block, cols), lambda r: (0, base + r, 0))]
        args += [dq, dkv]
    here = pl.BlockSpec((block, width), lambda r: (r, 0))
    args = [flag, x, vec, mg, w] + args + list(edges)
    return pl.pallas_call(
        following(functools.partial(rows_kernel, groups=groups, edges=bool(edges)), len(args), after),
        grid=(count // block,),
        in_specs=[pl.BlockSpec(memory_space=pltpu.SMEM), here, whole(vec), pl.BlockSpec((block, width), lambda r: (base + r, 0)), whole(w)] + specs + [whole(e) for e in edges] + untouched(after),
        out_specs=[here, pl.BlockSpec((8, width), lambda r: (0, 0))],
        out_shape=[SDS(x.shape, dtype), SDS((8, width), f32)],
        compiler_params=limits(60),
        cost_estimate=cost(10 if edges else 1),
        name="row_grads",
    )(*args, *after)


def add_kernel(own_ref, other_ref, out_ref):
    out_ref[...] = (own_ref[...].astype(f32) + other_ref[...].astype(f32)).astype(out_ref.dtype)


def add_step(part, bit, dtype, after=()):
    return pl.pallas_call(
        following(add_kernel, 2, after),
        in_specs=[whole(part), whole(part)] + untouched(after),
        out_specs=whole(part),
        out_shape=SDS(part.shape, dtype),
        cost_estimate=cost(1),
        name="add_step",
    )(part, swapped(part, *bit), *after)


def as_column(row):
    n = row.shape[1]
    eye = lax.broadcasted_iota(jnp.int32, (n, n), 0) == lax.broadcasted_iota(jnp.int32, (n, n), 1)
    return jnp.sum(jnp.where(eye, row, 0.0), axis=1, keepdims=True)


def split_shards(qkv_ref, rest_ref, units, width):
    groups = (rest_ref.shape[1] - units - width) // width
    starts = [units + width * (k + 1) for k in range(groups)]
    return qkv_ref[...], rest_ref[:, units : units + width], rest_ref[:, :units], [rest_ref[:, at : at + width] for at in starts]


def pack_kernel(qkv_ref, rest_ref, rq_ref, ro_ref, ru_ref, rd_ref, vone_ref, vtwo_ref, bias_ref,
                stats_ref, gout_ref, gup_ref, gdown_ref, nq_ref, no_ref, nu_ref, nd_ref, cq_ref, co_ref, cu_ref, cd_ref, *, decay):
    units, width = bias_ref.shape[1], vone_ref.shape[1]
    g_qkv, g_out, g_up, g_down = split_shards(qkv_ref, rest_ref, units, width)
    rows = g_qkv.shape[0]
    gout_ref[...], gup_ref[...] = g_out, g_up
    at, totals = 0, []
    for g, old_ref, new_ref, col_ref in ((g_qkv, rq_ref, nq_ref, cq_ref), (g_out, ro_ref, no_ref, co_ref), (g_up, ru_ref, nu_ref, cu_ref), (g_down, rd_ref, nd_ref, cd_ref)):
        groups = g if isinstance(g, list) else [g]
        columns, total, means = 0.0, 0.0, []
        for k, part in enumerate(groups):
            square = part * part + TINY_SQUARE
            columns = columns + jnp.sum(square, axis=0, keepdims=True)
            means.append(jnp.mean(square, axis=1, keepdims=True))
            if len(groups) > 1:
                gdown_ref[k * rows : (k + 1) * rows, :] = part
        mean = means[0] if len(means) == 1 else jnp.concatenate(means, axis=0)
        new = decay * as_column(old_ref[...].reshape(1, -1)) + (1.0 - decay) * mean
        col_ref[...] = new
        new_ref[...] = jnp.sum(jnp.where(lax.broadcasted_iota(jnp.int32, (new.shape[0],) * 2, 0) == lax.broadcasted_iota(jnp.int32, (new.shape[0],) * 2, 1), new, 0.0), axis=0)
        totals.append(jnp.sum(new, axis=0, keepdims=True))
        stats_ref[:, at : at + columns.shape[1]] = columns
        at += columns.shape[1]
    for ref, count in ((vone_ref, 2), (vtwo_ref, 3)):
        for n in range(count):
            stats_ref[:, at : at + width] = ref[n : n + 1, :]
            at += width
    stats_ref[:, at : at + units] = bias_ref[...]
    at += units
    lane = lax.broadcasted_iota(jnp.int32, (1, LANES), 1)
    last = jnp.zeros((1, LANES), f32)
    for n, total in enumerate(totals):
        last = jnp.where(lane == n, total, last)
    stats_ref[:, at : at + LANES] = last


def pack(qkv, rest, row_olds, vec_one, vec_two, bias, decay):
    units, width, rows = bias.shape[1], vec_one.shape[1], qkv.shape[0]
    tall = rest.shape[1] // width - units // width - 1
    count = qkv.shape[1] + width + units + width + 5 * width + units + LANES
    shapes = [(1, count), (rows, width), (rows, units), (tall * rows, width)]
    shapes += [old.shape for old in row_olds] + [(old.shape[0], 1) for old in row_olds]
    args = (qkv, rest, *row_olds, vec_one, vec_two, bias)
    return pl.pallas_call(
        functools.partial(pack_kernel, decay=decay),
        out_shape=[SDS(shape, f32) for shape in shapes],
        compiler_params=limits(60),
        cost_estimate=cost(3),
        name="pack",
    )(*args)


def update_kernel(stats_ref, qkv_ref, rest_ref, rq_ref, ro_ref, ru_ref, rd_ref, mq_ref, mo_ref, mu_ref, md_ref, oq_ref, oo_ref, ou_ref, od_ref,
                  vec_ref, vstate_ref, bias_ref, bstate_ref,
                  nq_ref, no_ref, nu_ref, nd_ref, cq_ref, co_ref, cu_ref, cd_ref, vg_ref, vs_ref, vn_ref, bg_ref, bs_ref, bn_ref, *, decay, full_rows):
    width, units = vec_ref.shape[1], bias_ref.shape[0]
    shards = split_shards(qkv_ref, rest_ref, units, width)
    rows = qkv_ref.shape[0]
    stats = stats_ref[...]
    totals = stats[:, stats.shape[1] - LANES :]
    at = 0
    sets = zip(shards, (rq_ref, ro_ref, ru_ref, rd_ref), (mq_ref, mo_ref, mu_ref, md_ref), (oq_ref, oo_ref, ou_ref, od_ref), (nq_ref, no_ref, nu_ref, nd_ref), (cq_ref, co_ref, cu_ref, cd_ref), full_rows)
    for n, (shard, row_ref, master_ref, old_ref, new_ref, col_ref, count) in enumerate(sets):
        columns = old_ref.shape[0]
        col = decay * old_ref[...].reshape(1, columns) + (1.0 - decay) * (stats[:, at : at + columns] / count)
        at += columns
        col_ref[...] = col[0]
        row_mean = totals[:, n : n + 1] / count
        parts = shard if isinstance(shard, list) else [shard]
        master = master_ref[...].astype(f32)
        for k, part in enumerate(parts):
            here = slice(k * rows, (k + 1) * rows)
            estimate = row_ref[here, :] * col / row_mean
            new_ref[here, :] = master[here] - RATE_MATRIX * part * lax.rsqrt(estimate)
    grad = jnp.concatenate([stats[:, at + n * width : at + (n + 1) * width] for n in range(5)], axis=0)
    at += 5 * width
    vg_ref[...] = grad
    state = decay * vstate_ref[...] + (1.0 - decay) * (grad * grad + TINY_SQUARE)
    vs_ref[...] = state
    vn_ref[...] = vec_ref[...] - RATE_VECTOR * grad * lax.rsqrt(state)
    grad = stats[:, at : at + units]
    bg_ref[...] = grad[0]
    state = decay * bstate_ref[...].reshape(1, units) + (1.0 - decay) * (grad * grad + TINY_SQUARE)
    bs_ref[...] = state[0]
    bn_ref[...] = (bias_ref[...].reshape(1, units) - RATE_VECTOR * grad * lax.rsqrt(state))[0]


def update(stats, qkv, rest, row_columns, masters, col_olds, vec, vec_state, bias, bias_state, decay, full_rows):
    args = (stats, qkv, rest, *row_columns, *masters, *col_olds, vec, vec_state, bias, bias_state)
    shapes = [m.shape for m in masters] + [c.shape for c in col_olds] + [vec.shape] * 3 + [bias.shape] * 3
    return pl.pallas_call(
        functools.partial(update_kernel, decay=decay, full_rows=full_rows),
        out_shape=[SDS(shape, f32) for shape in shapes],
        compiler_params=limits(60),
        cost_estimate=cost(3),
        name="update",
    )(*args)


def mask_lanes(segments, valid, start, own, half, glob, first):
    count = own + 2 * half
    seg = lax.dynamic_slice_in_dim(jnp.pad(segments, half), start, count)[:, None]
    ok = lax.dynamic_slice_in_dim(jnp.pad(valid, half), start, count)[:, None] > 0
    lane = lax.broadcasted_iota(jnp.int32, (count, LANES), 1)
    seen = ok & ((seg == lane) | (lane == 4)) | (lane > 4)
    kx = jnp.where(seen, 0.0, NEG_FILL).astype(bf16)
    lane_g = lax.broadcasted_iota(jnp.int32, (glob, LANES), 1)
    kx_glob = jnp.where((lane_g == 4) & ~first, NEG_FILL, 0.0).astype(bf16)
    qx = (seg[half : half + own] == lane[:own]) & (lane[:own] < 4)
    qx = jnp.concatenate([qx, lane_g == 4], axis=0).astype(bf16)
    return qx, jnp.concatenate([kx, kx_glob], axis=0)


def body(
    tokens,
    glob_tokens,
    w_qkv,
    w_out,
    w_up,
    w_down,
    vec_params,
    hidden_bias,
    row_qkv,
    col_qkv,
    row_out,
    col_out,
    row_up,
    col_up,
    row_down,
    col_down,
    vec_state,
    bias_state,
    segments,
    valid_mask,
    out_cotangent,
    glob_cotangent,
):
    width = w_out.shape[0]
    size = width // HEADS
    assert 2 * size == LANES
    scale = size ** (-0.5)
    coef = scale * LOG2E
    half = BLOCK // 2
    tok, glob = tokens[0], glob_tokens[0]
    own, globs = tok.shape[0], glob.shape[0]
    seq_index = lax.axis_index("seq")
    first = seq_index == 0
    flag = first.astype(f32).reshape(1)
    bias_row = hidden_bias[None, :]
    batch_bits, seq_bits = bits_of("batch"), bits_of("seq")

    low, high = [batch_bits[:1]], [[bit] for bit in batch_bits[1:]]
    far = [seq_bits[1:][n : n + 2] for n in range(0, len(seq_bits) - 1, 2)]
    wide_stages = low + high + [seq_bits[:1]]
    tall_stages = low + [seq_bits[:1]] + high
    joint_stages = [[bit] for bit in seq_bits[1:]]
    pair_stages = low + [batch_bits[1:] + seq_bits[:1]] + far
    places = row_places(width, pair_stages)
    sequence = np.arange(1 << len(seq_bits)).reshape([2] * len(seq_bits)).transpose(
        [seq_bits[::-1].index(bit) for bit in seq_bits]
    ).reshape(-1)
    tall_chunk = w_down.shape[0] // lax.axis_size("batch") // sequence.size
    tall_places = tuple(int(n) * tall_chunk for n in sequence), tall_chunk
    halo_left, halo_right = shifted(tok[own - half :], "seq", 1), shifted(tok[:half], "seq", -1)
    qx, kx = mask_lanes(segments[0], valid_mask[0], seq_index * own, own, half, globs, first)
    qkv, normed_t = project(tok, glob, w_qkv, vec_params)
    part = glob_attention(qkv, qx, kx, own, half, size, coef)
    left, right, halo_t = project_halos(halo_left, halo_right, w_qkv, vec_params)
    part, glob_lse = merge_step(part, *seq_bits[0], size, after=[left])
    inner_att, inner_lse = local_inner(qkv, qx, kx, own, half, size, coef, after=[part])
    for bit in seq_bits[1:-1]:
        part, glob_lse = merge_step(part, *bit, size, after=[inner_lse])
    att, lse = local_edge(qkv, left, right, qx, kx, inner_att, inner_lse, own, half, size, coef, after=[part])
    part, glob_lse = merge_step(part, *seq_bits[-1], size, after=[lse])
    side = side_of(*batch_bits[0]).reshape(1)
    out_tok, out_glob, mixed_grad, heads_grad, *matrices, vec_two, bias_sum = feed_forward(
        side, flag, att, part, tok, glob, w_out, w_up, w_down, vec_params, bias_row, out_cotangent[0], glob_cotangent[0], places, tall_places
    )
    wide, down = Scatter(*matrices[:2], wide_stages), Scatter(*matrices[2:], tall_stages)
    edge = edge_backward(qkv, left, right, qx, kx, att, heads_grad, lse, own, size, coef, scale, after=wide.parts + down.parts)
    grad_left, grad_right = edge[3:]
    down.step(after=edge[:1])
    wide.step(after=down.parts)
    to_left, to_right, halo_sums = halo_rows(halo_left, halo_right, vec_params, w_qkv, grad_left, grad_right, after=wide.parts)
    edges = (shifted(to_right, "seq", 1), shifted(to_left, "seq", -1))
    shared = (qkv, qx, kx, att, part, heads_grad, lse, glob_lse, *edge[:3], own, half, size, coef, scale)
    parts = [inner_backward(0, 1, *shared, after=[to_left, to_right])]
    down.step(after=[parts[0][0], *edges])
    wide.step(after=down.parts)
    weight = Scatter(*qkv_weight_grad(0, side, normed_t, halo_t, *parts[0], grad_left, grad_right, places, after=wide.parts), pair_stages)
    glob_part, glob_sums = row_grads(flag, glob, vec_params, mixed_grad, w_qkv, parts, own, globs, bf16, after=weight.parts)
    joint = joint_scatter(wide, down, joint_stages, after=[glob_part])
    weight.step(after=joint.parts)
    glob_part = add_step(glob_part, seq_bits[0], bf16, after=weight.parts)
    tokens_grad, tok_sums = row_grads(
        jnp.ones((1,), f32), tok, vec_params, mixed_grad, w_qkv, parts, 0, half, f32, edges=edges, after=[glob_part]
    )
    joint.step(after=[tok_sums])
    weight.step(after=joint.parts)
    for bit in seq_bits[1:-1]:
        glob_part = add_step(glob_part, bit, bf16, after=weight.parts)
    while joint.stages:
        rest = joint.step(after=[glob_part])
    glob_part = add_step(glob_part, seq_bits[-1], f32, after=[rest])
    while weight.stages:
        shard_qkv = weight.step(after=[glob_part])
    decay = 1.0 - STEP ** (-0.8)
    units = w_up.shape[1]
    owner = lax.axis_index(("batch", "seq"))
    masters = []
    for matrix in (w_qkv, w_out, w_up, w_down):
        rows = matrix.shape[0] // lax.axis_size(("batch", "seq"))
        masters.append(lax.dynamic_slice_in_dim(matrix, owner * rows, rows, 0))
    stats, grad_out, grad_up, grad_down, *rows_new = pack(
        shard_qkv, rest, (row_qkv, row_out, row_up, row_down), halo_sums + glob_sums + tok_sums, vec_two, bias_sum, decay
    )
    for bit in batch_bits + seq_bits:
        stats = stats + swapped(stats, *bit)
    new_qkv, new_out, new_up, new_down, col_qkv_new, col_out_new, col_up_new, col_down_new, *vectors = update(
        stats, shard_qkv, rest, rows_new[4:], masters, (col_qkv, col_out, col_up, col_down), vec_params, vec_state, hidden_bias, bias_state,
        decay, (w_qkv.shape[0], w_out.shape[0], w_up.shape[0], w_down.shape[0]),
    )
    return (
        out_tok[None],
        out_glob[None],
        tokens_grad[None],
        glob_part[None],
        shard_qkv,
        rows_new[0],
        col_qkv_new,
        new_qkv,
        grad_out,
        rows_new[1],
        col_out_new,
        new_out,
        grad_up,
        rows_new[2],
        col_up_new,
        new_up,
        grad_down,
        rows_new[3],
        col_down_new,
        new_down,
        *vectors,
    )


def solution(mesh):
    in_specs = (
        P("batch", "seq", None),
        P("batch", None, None),
        P(),
        P(),
        P(),
        P(),
        P(),
        P(),
        P(("batch", "seq")),
        P(),
        P(("batch", "seq")),
        P(),
        P(("batch", "seq")),
        P(),
        P(("batch", "seq")),
        P(),
        P(),
        P(),
        P("batch", None),
        P("batch", None),
        P("batch", "seq", None),
        P("batch", None, None),
    )
    out_specs = (
        P("batch", "seq", None),
        P("batch", None, None),
        P("batch", "seq", None),
        P("batch", None, None),
        P(("batch", "seq"), None),
        P(("batch", "seq")),
        P(),
        P(("batch", "seq"), None),
        P(("batch", "seq"), None),
        P(("batch", "seq")),
        P(),
        P(("batch", "seq"), None),
        P(("batch", "seq"), None),
        P(("batch", "seq")),
        P(),
        P(("batch", "seq"), None),
        P(("batch", "seq"), None),
        P(("batch", "seq")),
        P(),
        P(("batch", "seq"), None),
        P(),
        P(),
        P(),
        P(),
        P(),
        P(),
    )
    return jax.shard_map(body, mesh=mesh, in_specs=in_specs, out_specs=out_specs, check_vma=False)
```

```python
import functools

import jax
import jax.numpy as jnp
import numpy as np
from jax import lax
from jax.experimental import pallas as pl
from jax.experimental.pallas import tpu as pltpu
from jax.sharding import PartitionSpec as P

HEADS = 12
BLOCK = 512
STEP = 10

NEG_FILL = -8e9
NORM_EPS = 1e-06
TINY_SQUARE = 1e-30
RATE_MATRIX = 0.03
RATE_VECTOR = 0.2
LANES = 128
LOG2E = 1.4426950408889634

f32, bf16 = jnp.float32, jnp.bfloat16
NN = (((1,), (0,)), ((), ()))
NT = (((1,), (1,)), ((), ()))
TN = (((0,), (0,)), ((), ()))
SDS = jax.ShapeDtypeStruct


def bits_of(axis):
    size = lax.axis_size(axis)
    assert size & (size - 1) == 0
    return [(axis, 1 << k) for k in range(size.bit_length() - 1)]


def side_of(axis, bit):
    return (lax.axis_index(axis) // bit) % 2


def swapped(values, axis, bit):
    return lax.ppermute(values, axis, [(i, i ^ bit) for i in range(lax.axis_size(axis))])


def shifted(values, axis, distance):
    devices = range(lax.axis_size(axis))
    return lax.ppermute(values, axis, [(i, i + distance) for i in devices if i + distance in devices])


def summed(parts, bits):
    leaves, tree = jax.tree.flatten(parts)
    flat = jnp.concatenate([leaf.reshape(-1) for leaf in leaves])
    count = flat.shape[0]
    flat = jnp.pad(flat, (0, -count % 1024)).reshape(-1, LANES)
    for axis, bit in bits:
        flat = flat + swapped(flat, axis, bit)
    flat = flat.reshape(-1)
    out, place = [], 0
    for leaf in leaves:
        out.append(flat[place : place + leaf.size].reshape(leaf.shape))
        place += leaf.size
    return jax.tree.unflatten(tree, out)


def flipped(values, bits, flips):
    sizes = {axis: lax.axis_size(axis) for axis in ("batch", "seq")}
    change = {axis: sum(bit for n, (name, bit) in enumerate(bits) if name == axis and flips >> n & 1) for axis in sizes}
    route = [
        (b * sizes["seq"] + s, (b ^ change["batch"]) * sizes["seq"] + (s ^ change["seq"]))
        for b in range(sizes["batch"])
        for s in range(sizes["seq"])
    ]
    return lax.ppermute(values, ("batch", "seq"), route)


def mm(a, b, dims=NN):
    return lax.dot_general(a, b, dims, preferred_element_type=f32)


def limits(mib):
    return pltpu.CompilerParams(vmem_limit_bytes=mib * 2**20)


def cost(us):
    return pl.CostEstimate(flops=int(us * 1.15e9), bytes_accessed=1 << 20, transcendentals=0)


def whole(array):
    return pl.BlockSpec(array.shape, lambda *_: (0,) * array.ndim)


def following(kernel, inputs, after):
    return lambda *refs: kernel(*refs[:inputs], *refs[inputs + len(after) :])


def untouched(after):
    return [pl.BlockSpec(memory_space=pl.ANY)] * len(after)


def normalize(x):
    mean = jnp.mean(x, axis=1, keepdims=True)
    centred = x - mean
    rstd = lax.rsqrt(jnp.mean(centred * centred, axis=1, keepdims=True) + NORM_EPS)
    return centred * rstd, rstd


def norm_back(normalized, rstd, gain, grad):
    g = grad * gain
    inner = jnp.mean(g * normalized, axis=1, keepdims=True)
    return rstd * (g - jnp.mean(g, axis=1, keepdims=True) - normalized * inner)


def gelu_both(u):
    phi = 0.5 + 0.5 * lax.erf(u * 0.7071067811865476)
    density = jnp.exp2(u * u * (-0.5 * LOG2E)) * 0.3989422804014327
    return u * phi, phi + u * density


def head_part(values, head, size):
    lanes = lax.broadcasted_iota(jnp.int32, values.shape, 1)
    return jnp.where((lanes // size) == head, values, jnp.zeros_like(values))


def stage_kernel(side_ref, kept_ref, *refs, arrived, parts):
    for n in range(parts):
        at = side_ref[0] ^ n if parts > 1 else 0
        total = kept_ref[at].astype(f32)
        for ref in refs[:arrived]:
            total = total + ref[at].astype(f32)
        out = refs[arrived + n]
        out[...] = total.astype(out.dtype)


class Scatter:
    def __init__(self, sent, kept, stages):
        self.stages, self.parts, self.kept = list(stages), [sent], kept

    def step(self, after=()):
        bits = self.stages.pop(0)
        arrived = [flipped(part, bits[::-1], n + 1) for n, part in enumerate(self.parts)]
        bits = self.stages[0] if self.stages else []
        parts, columns = 1 << len(bits), self.kept.shape[-1]
        rows = self.kept.size // columns // parts
        block = columns if self.kept.size < 1 << 20 else columns // max(1, columns // 768)
        tall = 2 if columns == block and rows % 32 == 0 and self.kept.size > 1 << 19 else 1
        args = [a.reshape(parts, rows, columns) for a in [self.kept] + arrived]
        side = sum(side_of(*bit) << n for n, bit in enumerate(reversed(bits))) if bits else jnp.int32(0)
        spec = pl.BlockSpec((parts, rows // tall, block), lambda c, r: (0, r, c))
        out = pl.BlockSpec((rows // tall, block), lambda c, r: (r, c))
        after = list(after)
        self.kept, *self.parts = pl.pallas_call(
            following(functools.partial(stage_kernel, arrived=len(arrived), parts=parts), 1 + len(args), after),
            grid=(columns // block, tall),
            in_specs=[pl.BlockSpec(memory_space=pltpu.SMEM)] + [spec] * len(args) + untouched(after),
            out_specs=[out] * parts,
            out_shape=[SDS((rows, columns), bf16 if bits else f32)] + [SDS((rows, columns), bf16)] * (parts - 1),
            compiler_params=limits(60),
            cost_estimate=cost(2),
            name="sum_stage",
        )(side.reshape(1), *args, *after)
        return self.kept


def joint_kernel(side_ref, wk_ref, wa_ref, dk_ref, da_ref, sent_ref, kept_ref, total, *, chunk, starts):
    columns = wk_ref.shape[2]
    block = dk_ref.shape[2]
    for ref, flip in ((sent_ref, 1), (kept_ref, 0)):
        at = side_ref[0] ^ flip
        ref[:, :columns] = (wk_ref[at].astype(f32) + wa_ref[at].astype(f32)).astype(bf16)
        total[...] = dk_ref[at].astype(f32) + da_ref[at].astype(f32)
        for k, places in enumerate(starts):
            ref[:, columns + k * block : columns + (k + 1) * block] = gathered(total, places, chunk)


def joint_scatter(wide, down, stages, after=()):
    (bit,) = stages[0]
    args = []
    for scatter in (wide, down):
        bits = scatter.stages.pop(0)
        arrived = flipped(scatter.parts[0], bits, 1)
        args += [a.reshape(2, -1, a.shape[-1]) for a in (scatter.kept, arrived)]
    _, rows, columns = args[0].shape
    _, rows_down, block = args[2].shape
    owners = 1 << (len(stages) - 1)
    chunk = rows // owners
    groups = rows_down // rows
    starts = [[(n * groups + k) * chunk for n in range(owners)] for k in range(groups)]
    shape = SDS((rows, columns + groups * block), bf16)
    after = list(after)
    sent, kept = pl.pallas_call(
        following(functools.partial(joint_kernel, chunk=chunk, starts=starts), 5, after),
        in_specs=[pl.BlockSpec(memory_space=pltpu.SMEM)] + [whole(a) for a in args] + untouched(after),
        out_specs=[pl.BlockSpec(shape.shape, lambda: (0, 0))] * 2,
        out_shape=[shape, shape],
        scratch_shapes=[pltpu.VMEM((rows_down, block), f32)],
        compiler_params=limits(60),
        cost_estimate=cost(100),
        name="joint_stage",
    )(side_of(*bit).reshape(1), *args, *after)
    return Scatter(sent, kept, stages)


def row_places(width, stages):
    labels = bits_of("batch")[::-1] + bits_of("seq")[::-1]
    owners = np.arange(1 << len(labels)).reshape([2] * len(labels))
    owners = owners.transpose([labels.index(bit) for stage in stages for bit in stage]).reshape(2, -1)
    chunk = width // owners.size
    return tuple(int(owner) * chunk for owner in owners[0]), chunk, int(owners[1, 0] - owners[0, 0]) * chunk


def project_kernel(tok_ref, glob_ref, w_ref, vec_ref, qkv_ref, nt_ref, n_s):
    own = tok_ref.shape[0]

    @pl.when(pl.program_id(0) == 0)
    def _():
        for ref, rows in ((tok_ref, slice(0, own)), (glob_ref, slice(own, n_s.shape[0]))):
            n = normalize(ref[...].astype(f32))[0] * vec_ref[0:1, :] + vec_ref[1:2, :]
            n = n.astype(bf16)
            n_s[rows, :] = n
            nt_ref[:, rows] = n.T

    qkv_ref[...] = mm(n_s[...], w_ref[...]).astype(bf16)


def project(tok, glob, w, vec):
    width = tok.shape[1]
    rows = tok.shape[0] + glob.shape[0]
    return pl.pallas_call(
        project_kernel,
        grid=(w.shape[1] // width,),
        in_specs=[whole(tok), whole(glob), pl.BlockSpec((width, width), lambda c: (0, c)), whole(vec)],
        out_specs=[
            pl.BlockSpec((rows, width), lambda c: (0, c)),
            pl.BlockSpec((width, rows), lambda c: (0, 0)),
        ],
        out_shape=[SDS((rows, w.shape[1]), bf16), SDS((width, rows), bf16)],
        scratch_shapes=[pltpu.VMEM((rows, width), bf16)],
        compiler_params=limits(60),
        cost_estimate=cost(9),
        name="project",
    )(tok, glob, w, vec)


def halo_kernel(l_ref, r_ref, w_ref, vec_ref, lkv_ref, rkv_ref, nt_ref):
    half = l_ref.shape[0]
    for ref, out, at in ((l_ref, lkv_ref, 0), (r_ref, rkv_ref, half)):
        n = normalize(ref[...].astype(f32))[0] * vec_ref[0:1, :] + vec_ref[1:2, :]
        n = n.astype(bf16)
        nt_ref[:, at : at + half] = n.T
        out[...] = mm(n, w_ref[...]).astype(bf16)


def project_halos(left, right, w, vec):
    half, width = left.shape
    kv = pl.BlockSpec((half, width), lambda c: (0, c))
    return pl.pallas_call(
        halo_kernel,
        grid=(2,),
        in_specs=[whole(left), whole(right), pl.BlockSpec((width, width), lambda c: (0, c + 1)), whole(vec)],
        out_specs=[kv, kv, pl.BlockSpec((width, 2 * half), lambda c: (0, 0))],
        out_shape=[SDS((half, 2 * width), bf16)] * 2 + [SDS((width, 2 * half), bf16)],
        compiler_params=limits(60),
        cost_estimate=cost(3),
        name="project_halos",
    )(left, right, w, vec)


def attend_pairs(tiles, lse_rows, step, size, coef):
    scores = []
    for q, qx, keys, _ in tiles:
        for h in range(2):
            scores.append(mm(keys, jnp.concatenate([head_part(q, h, size), qx], axis=1), NT))
    tops = [jnp.max(s, axis=0, keepdims=True) * coef for s in scores]
    weights = [jnp.exp2(s * coef - top) for s, top in zip(scores, tops)]
    totals = [jnp.sum(p, axis=0, keepdims=True) for p in weights]
    outs = []
    for n, p in enumerate(weights):
        h = n % 2
        values_t = tiles[n // 2][3].T[h * size : (h + 1) * size]
        outs.append(mm(values_t, p.astype(bf16)) * (1.0 / totals[n]))
    results = []
    for n, lse in enumerate(lse_rows):
        row = lax.broadcasted_iota(jnp.int32, lse.shape, 0)
        for h in range(2):
            lse = jnp.where(row == 2 * step + h, tops[2 * n + h] + jnp.log2(totals[2 * n + h]), lse)
        results.append((jnp.concatenate(outs[2 * n : 2 * n + 2], axis=0).T.astype(bf16), lse))
    return results


def mask_piece(kx_ref, name, low, rows, own, half):
    if name == "l":
        start = low
    elif name == "r":
        start = half + own + low
    else:
        start = half + low if low < own else 2 * half + low
    return kx_ref[start : start + rows, :]


def fill_inner(src, dst, own, half):
    for b in range(dst.shape[0]):
        low = half + b * 2 * half
        dst[b, : 2 * half, :LANES] = src[low : low + 2 * half]
        dst[b, 2 * half :, :LANES] = src[own:]


def fill_inner_masks(kx_ref, dst, own, half, glob):
    for b in range(dst.shape[0]):
        dst[b, : 2 * half, LANES:] = mask_piece(kx_ref, "o", half + b * 2 * half, 2 * half, own, half)
        dst[b, 2 * half :, LANES:] = mask_piece(kx_ref, "o", own, glob, own, half)


def fill_edges(src, l_ref, r_ref, dst, own, half):
    dst[0, :half, :LANES] = l_ref[...]
    dst[0, half : 2 * half, :LANES] = src[:half]
    dst[1, :half, :LANES] = src[own - half : own]
    dst[1, half : 2 * half, :LANES] = r_ref[...]
    for b in range(2):
        dst[b, 2 * half :, :LANES] = src[own:]


def fill_edge_masks(kx_ref, dst, own, half, glob):
    for at, name, low in ((0, "l", 0), (1, "o", 0), (2, "o", own - half), (3, "r", 0)):
        dst[at // 2, at % 2 * half : (at % 2 + 1) * half, LANES:] = mask_piece(kx_ref, name, low, half, own, half)
    for b in range(2):
        dst[b, 2 * half :, LANES:] = mask_piece(kx_ref, "o", own, glob, own, half)


def local_inner_kernel(q_ref, k_ref, v_ref, qx_ref, kx_ref, o_ref, lse_ref, ks, vs, *, size, coef, own, half):
    step = pl.program_id(0)
    glob = k_ref.shape[0] - own

    @pl.when(step == 0)
    def _():
        fill_inner_masks(kx_ref, ks, own, half, glob)
        lse_ref[...] = jnp.zeros_like(lse_ref)

    fill_inner(k_ref, ks, own, half)
    fill_inner(v_ref, vs, own, half)
    places = [slice(j * half, (j + 1) * half) for j in range(own // half - 2)]
    tiles = []
    for j, there in enumerate(places):
        rows = slice(there.start + half, there.stop + half)
        tiles.append((q_ref[rows, :], qx_ref[rows, :], ks[j // 2], vs[j // 2]))
    for there, (o, lse) in zip(places, attend_pairs(tiles, [lse_ref[:, there] for there in places], step, size, coef)):
        o_ref[there, :], lse_ref[:, there] = o, lse


def local_edge_kernel(q_ref, k_ref, v_ref, lk_ref, lv_ref, rk_ref, rv_ref, qx_ref, kx_ref, io_ref, ilse_ref, o_ref, lse_ref, ks, vs, *, size, coef):
    step = pl.program_id(0)
    own, half = q_ref.shape[0], lk_ref.shape[0]
    glob = k_ref.shape[0] - own

    @pl.when(step == 0)
    def _():
        fill_edge_masks(kx_ref, ks, own, half, glob)
        lse_ref[...] = jnp.zeros_like(lse_ref)
        lse_ref[:, half : own - half] = ilse_ref[...]

    fill_edges(k_ref, lk_ref, rk_ref, ks, own, half)
    fill_edges(v_ref, lv_ref, rv_ref, vs, own, half)
    o_ref[half : own - half, :] = io_ref[...]
    places = [slice(0, half), slice(own - half, own)]
    tiles = [(q_ref[rows, :], qx_ref[rows, :], ks[b], vs[b]) for b, rows in enumerate(places)]
    for rows, (o, lse) in zip(places, attend_pairs(tiles, [lse_ref[:, rows] for rows in places], step, size, coef)):
        o_ref[rows, :], lse_ref[:, rows] = o, lse


def local_inner(qkv, qx, kx, own, half, size, coef, after=()):
    rows, width = qkv.shape[0], qkv.shape[1] // 3
    pairs, inner = width // LANES, own - 2 * half
    blocks, span = own // (2 * half) - 1, 2 * half + rows - own

    def cols(n, off=0):
        return pl.BlockSpec((n, LANES), lambda p: (0, p + off))

    def fixed(n):
        return pl.BlockSpec((n, LANES), lambda p: (0, 0))

    return pl.pallas_call(
        following(functools.partial(local_inner_kernel, size=size, coef=coef, own=own, half=half), 5, after),
        grid=(pairs,),
        in_specs=[cols(own), cols(rows, pairs), cols(rows, 2 * pairs), fixed(own), whole(kx)] + untouched(after),
        out_specs=[cols(inner), pl.BlockSpec((16, inner), lambda p: (0, 0))],
        out_shape=[SDS((inner, width), bf16), SDS((16, inner), f32)],
        scratch_shapes=[pltpu.VMEM((blocks, span, 2 * LANES), bf16), pltpu.VMEM((blocks, span, LANES), bf16)],
        compiler_params=limits(60),
        cost_estimate=cost(12),
        name="local_inner",
    )(qkv, qkv, qkv, qx, kx, *after)


def local_edge(qkv, left, right, qx, kx, io, ilse, own, half, size, coef, after=()):
    rows, width = qkv.shape[0], qkv.shape[1] // 3
    pairs, inner, span = width // LANES, own - 2 * half, 2 * half + rows - own

    def cols(n, off=0):
        return pl.BlockSpec((n, LANES), lambda p: (0, p + off))

    def fixed(n):
        return pl.BlockSpec((n, LANES), lambda p: (0, 0))

    return pl.pallas_call(
        following(functools.partial(local_edge_kernel, size=size, coef=coef), 11, after),
        grid=(pairs,),
        in_specs=[cols(own), cols(rows, pairs), cols(rows, 2 * pairs), cols(half), cols(half, pairs), cols(half), cols(half, pairs), fixed(own), whole(kx), cols(inner), whole(ilse)] + untouched(after),
        out_specs=[cols(own), pl.BlockSpec((16, own), lambda p: (0, 0))],
        out_shape=[SDS((own, width), bf16), SDS((16, own), f32)],
        scratch_shapes=[pltpu.VMEM((2, span, 2 * LANES), bf16), pltpu.VMEM((2, span, LANES), bf16)],
        compiler_params=limits(60),
        cost_estimate=cost(12),
        name="local_edge",
    )(qkv, qkv, qkv, left, left, right, right, qx, kx, io, ilse, *after)


def to_thirds(lse):
    high = lse.astype(bf16).astype(f32)
    middle = (lse - high).astype(bf16).astype(f32)
    low = lse - high - middle
    lane = lax.broadcasted_iota(jnp.int32, lse.shape, 1)
    packed = jnp.where(lane < 16, high, jnp.where(lane < 32, pltpu.roll(middle, 16, 1), pltpu.roll(low, 32, 1)))
    return jnp.where(lane < 48, packed, 0.0).astype(bf16)


def from_thirds(packed):
    packed = packed.astype(f32)
    lane = lax.broadcasted_iota(jnp.int32, packed.shape, 1)
    total = packed + (pltpu.roll(packed, LANES - 16, 1) + pltpu.roll(packed, LANES - 32, 1))
    return jnp.where(lane < 16, total, 0.0)


def glob_kernel(q_ref, k_ref, v_ref, qx_ref, kx_ref, out_ref, ks, lse_ref, *, size, coef, half):
    step = pl.program_id(0)
    glob = q_ref.shape[0]
    own = k_ref.shape[0] - glob

    @pl.when(step == 0)
    def _():
        ks[:own, LANES:] = kx_ref[half : half + own, :]
        ks[own:, LANES:] = kx_ref[2 * half + own :, :]
        lse_ref[...] = jnp.zeros_like(lse_ref)

    ks[:, :LANES] = k_ref[...]
    ((o, lse),) = attend_pairs([(q_ref[...], qx_ref[...], ks[...], v_ref[...])], [lse_ref[...]], step, size, coef)
    lse_ref[...] = lse
    out_ref[:, pl.ds(pl.multiple_of(step * LANES, LANES), LANES)] = o

    @pl.when(step == pl.num_programs(0) - 1)
    def _():
        out_ref[:, out_ref.shape[1] - LANES :] = to_thirds(lse.T)


def glob_attention(qkv, qx, kx, own, half, size, coef):
    rows, width = qkv.shape[0], qkv.shape[1] // 3
    pairs, glob = width // LANES, rows - own
    at = own // glob

    def cols(off):
        return pl.BlockSpec((rows, LANES), lambda p: (0, p + off))

    return pl.pallas_call(
        functools.partial(glob_kernel, size=size, coef=coef, half=half),
        grid=(pairs,),
        in_specs=[pl.BlockSpec((glob, LANES), lambda p: (at, p)), cols(pairs), cols(2 * pairs), pl.BlockSpec((glob, LANES), lambda p: (at, 0)), whole(kx)],
        out_specs=pl.BlockSpec((glob, width + LANES), lambda p: (0, 0)),
        out_shape=SDS((glob, width + LANES), bf16),
        scratch_shapes=[pltpu.VMEM((rows, 2 * LANES), bf16), pltpu.VMEM((LANES, glob), f32)],
        compiler_params=limits(60),
        cost_estimate=cost(8),
        name="glob_attention",
    )(qkv, qkv, qkv, qx, kx)


def merge_kernel(upper_ref, own_ref, other_ref, out_ref, lse_ref, *, size):
    upper = upper_ref[0] == 1
    width = own_ref.shape[1] - LANES
    own_l, other_l = from_thirds(own_ref[:, width:]), from_thirds(other_ref[:, width:])
    first, second = jnp.where(upper, other_l, own_l), jnp.where(upper, own_l, other_l)
    top = jnp.maximum(first, second)
    wa, wb = jnp.exp2(first - top), jnp.exp2(second - top)
    total = wa + wb
    lse = top + jnp.log2(total)
    lane = lax.broadcasted_iota(jnp.int32, lse.shape, 1)
    lse = jnp.where(lane < 16, lse, 0.0)
    lse_ref[...] = lse
    out_ref[:, width:] = to_thirds(lse)
    wa, wb = wa / total, wb / total
    for p in range(width // LANES):
        at = slice(p * LANES, (p + 1) * LANES)
        own_o, other_o = own_ref[:, at].astype(f32), other_ref[:, at].astype(f32)
        a, b = jnp.where(upper, other_o, own_o), jnp.where(upper, own_o, other_o)
        ka = jnp.where(lane < size, wa[:, 2 * p : 2 * p + 1], wa[:, 2 * p + 1 : 2 * p + 2])
        kb = jnp.where(lane < size, wb[:, 2 * p : 2 * p + 1], wb[:, 2 * p + 1 : 2 * p + 2])
        out_ref[:, at] = (a * ka + b * kb).astype(bf16)


def merge_step(part, axis, bit, size, after=()):
    other = swapped(part, axis, bit)
    return pl.pallas_call(
        following(functools.partial(merge_kernel, size=size), 3, after),
        in_specs=[pl.BlockSpec(memory_space=pltpu.SMEM), whole(part), whole(part)] + untouched(after),
        out_specs=[whole(part), pl.BlockSpec((part.shape[0], LANES), lambda: (0, 0))],
        out_shape=[SDS(part.shape, bf16), SDS((part.shape[0], LANES), f32)],
        cost_estimate=cost(2),
        name="merge",
    )(side_of(axis, bit).reshape(1), part, other, *after)


def gathered(total, starts, chunk, shift=0):
    if chunk % 8 == 0:
        rows = [total[pl.ds(pl.multiple_of(start + shift, 8), chunk), :] for start in starts]
        return jnp.concatenate(rows, axis=0).astype(bf16)
    shape = (len(starts) * chunk, total.shape[0])
    place, row = lax.broadcasted_iota(jnp.int32, shape, 0), lax.broadcasted_iota(jnp.int32, shape, 1)
    wanted = place % chunk + shift
    for n, start in enumerate(starts):
        wanted = wanted + jnp.where(place // chunk == n, start, 0)
    return mm((wanted == row).astype(f32).astype(bf16), total[...].astype(bf16)).astype(bf16)


def split_rows(total, side, sent_ref, kept_ref, places):
    starts, chunk, apart = places
    sent_ref[...] = gathered(total, starts, chunk, (1 - side) * apart)
    kept_ref[...] = gathered(total, starts, chunk, side * apart)


def ffn_kernel(side_ref, flag_ref, att_ref, gatt_ref, tok_ref, glob_ref, wo_ref, up_ref, down_ref, vec_ref, bias_ref, br_tok_ref, br_glob_ref,
               out_tok_ref, out_glob_ref, mg_ref, hd_ref, wsent_ref, wkept_ref, dsent_ref, dkept_ref, vsum_ref, bsum_ref,
               att_s, n2s, n2t, br, act_s, hg_s, mixed_s, res_s, dn_s, sums_s, total, *, places, tall_places, pieces):
    step, last = pl.program_id(0), pl.num_programs(0) - 1
    own, width = tok_ref.shape
    rows = br.shape[0]
    flag = flag_ref[0]
    side = side_ref[0]
    size, steps = rows // pieces, act_s.shape[0]

    def at(n):
        return pl.ds(pl.multiple_of(n * size, size), size)

    def counted(x):
        return (x.astype(f32) * flag).astype(bf16)

    @pl.when(step == 0)
    def _():
        br[:own] = br_tok_ref[...]
        br[own:] = br_glob_ref[...]
        att_s[:own] = att_ref[...]
        att_s[own:] = gatt_ref[:, :width]
        mixed_s[:own] = tok_ref[...].astype(f32)
        mixed_s[own:] = glob_ref[...].astype(f32)

        def block(n, _):
            here = at(n)
            mixed = mixed_s[here, :] + mm(att_s[here, :], wo_ref[...])
            mixed_s[here, :] = mixed
            n2 = (normalize(mixed)[0] * vec_ref[2:3, :] + vec_ref[3:4, :]).astype(bf16)
            n2s[here, :] = n2
            res_s[here, :] = mixed + vec_ref[4:5, :]
            return 0

        lax.fori_loop(0, pieces, block, 0)
        n2t[:, :own] = n2s[:own, :].T
        n2t[:, own:] = counted(n2s[own:, :]).T
        dn_s[...] = jnp.zeros_like(dn_s)

    @pl.when((step >= steps) & (step < last))
    def _():
        slot = step - steps
        count = out_tok_ref.shape[0]
        out_tok_ref[...] = res_s[pl.ds(pl.multiple_of(slot * count, 16), count), :].astype(bf16)
        count = hd_ref.shape[0]
        here = pl.ds(pl.multiple_of(slot * count, 16), count)
        normalized, rstd = normalize(mixed_s[here, :])
        dn = dn_s[here, :]
        bf = br[here, :].astype(f32)
        ag = (bf + norm_back(normalized, rstd, vec_ref[2:3, :], dn)).astype(bf16)
        mg_ref[...] = ag
        hd_ref[...] = mm(ag, wo_ref[...], NT).astype(bf16)
        row = lax.broadcasted_iota(jnp.int32, (count, 1), 0) + slot * count
        keep = jnp.where(row < own, 1.0, flag)
        n2s[here, :] = (ag.astype(f32) * keep).astype(bf16)
        dn = dn * keep
        terms = [jnp.sum(term, axis=0, keepdims=True) for term in (dn * normalized, dn, bf * keep)]
        terms = jnp.concatenate(terms + [jnp.zeros((5, width), f32)], axis=0)
        sums_s[...] = terms + jnp.where(slot == 0, 0.0, sums_s[...])
        total[...] = mm(n2t[...], hg_s[slot])
        split_rows(total, side, wsent_ref, wkept_ref, places)
        hg = hg_s[slot].astype(f32)
        bsum_ref[...] = jnp.sum(hg[:own], axis=0, keepdims=True) + flag * jnp.sum(hg[own:], axis=0, keepdims=True)
        act_s[slot, own:, :] = counted(act_s[slot, own:, :])
        total[...] = mm(act_s[slot], br[...], TN)
        starts, rows_each = tall_places
        grad = gathered(total, starts, rows_each)
        part_rows = dsent_ref.shape[2]
        mine = slot % 2 == side
        for ref, wanted in ((dkept_ref, mine), (dsent_ref, jnp.logical_not(mine))):

            @pl.when(wanted)
            def _():
                for n in range(ref.shape[0]):
                    ref[n, 0] = grad[n * part_rows : (n + 1) * part_rows]

    @pl.when(step < steps)
    def _():
        slot = step

        def block(n, _):
            here = at(n)
            hidden = mm(n2s[here, :], up_ref[...]) + bias_ref[...]
            d_active = mm(br[here, :], down_ref[...], NT)
            active, slope = gelu_both(hidden)
            active = active.astype(bf16)
            hg = (d_active * slope).astype(bf16)
            act_s[slot, here, :] = active
            hg_s[slot, here, :] = hg
            res_s[here, :] += mm(active, down_ref[...])
            dn_s[here, :] += mm(hg, up_ref[...], NT)
            return 0

        lax.fori_loop(0, pieces, block, 0)

    @pl.when(step == last)
    def _():
        total[...] = mm(att_s[...], n2s[...], TN)
        split_rows(total, side, wsent_ref, wkept_ref, places)
        vsum_ref[...] = sums_s[...]
        out_glob_ref[...] = res_s[own:, :].astype(bf16)


def feed_forward(side, flag, att, gatt, tok, glob, wo, up, down, vec, bias, br_tok, br_glob, places, tall_places):
    own, width = tok.shape
    glob_rows = glob.shape[0]
    rows, units, chunk = own + glob_rows, up.shape[1], width
    steps = units // chunk
    pairs = lax.axis_size("batch") // 2
    assert steps == 2 * pairs

    def fixed(n):
        return pl.BlockSpec((n, width), lambda c: (0, 0))

    def once(array):
        return pl.BlockSpec(array.shape, lambda c: (0,) * array.ndim, pipeline_mode=pl.Buffered(1))

    def now(c):
        return jnp.minimum(c, steps - 1)

    def before(c):
        return jnp.clip(c - steps, 0, steps - 1)

    def by_part(n):
        assert n % (16 * steps) == 0
        return pl.BlockSpec((n // steps, width), lambda c: (before(c), 0))

    wide = pl.BlockSpec((width // 2, chunk), lambda c: (0, jnp.maximum(c - steps, 0)))
    parts = 2
    tall = pl.BlockSpec((parts, 1, chunk // parts, width), lambda c: (0, before(c) // 2, 0, 0))
    wide_shape = SDS((width // 2, units + width), bf16)
    tall_shape = SDS((parts, pairs, chunk // parts, width), bf16)
    smem = pl.BlockSpec(memory_space=pltpu.SMEM)
    low, full = pltpu.VMEM((rows, width), bf16), pltpu.VMEM((rows, width), f32)
    both = pltpu.VMEM((steps, rows, chunk), bf16)
    return pl.pallas_call(
        functools.partial(ffn_kernel, places=places, tall_places=tall_places, pieces=3),
        grid=(2 * steps + 1,),
        in_specs=[
            smem, smem, once(att), once(gatt), once(tok), once(glob), once(wo),
            pl.BlockSpec((width, chunk), lambda c: (0, now(c))), pl.BlockSpec((chunk, width), lambda c: (now(c), 0)), whole(vec),
            pl.BlockSpec((1, chunk), lambda c: (0, now(c))), once(br_tok), once(br_glob),
        ],
        out_specs=[
            by_part(own), fixed(glob_rows), by_part(rows), by_part(rows), wide, wide, tall, tall, fixed(8), pl.BlockSpec((1, chunk), lambda c: (0, before(c))),
        ],
        out_shape=[
            SDS((own, width), bf16), SDS((glob_rows, width), bf16), SDS((rows, width), bf16), SDS((rows, width), bf16),
            wide_shape, wide_shape, tall_shape, tall_shape, SDS((8, width), f32), SDS((1, units), f32),
        ],
        scratch_shapes=[low, low, pltpu.VMEM((width, rows), bf16), low, both, both, full, full, full, pltpu.VMEM((8, width), f32), pltpu.VMEM((width, width), f32)],
        compiler_params=limits(63),
        cost_estimate=cost(55),
        name="feed_forward",
    )(side, flag, att, gatt, tok, glob, wo, up, down, vec, bias, br_tok, br_glob)


def pair_backward(blocks, lse_rows, delta_rows, size, coef, scale):
    units = []
    for keys, values, tiles in blocks:
        for q, qx, do, at in tiles:
            for h in range(2):
                units.append((keys, values, head_part(q, h, size), qx, head_part(do, h, size), lse_rows[h][:, at], delta_rows[h][:, at]))
    scores = [mm(keys, jnp.concatenate([q, qx], axis=1), NT) for keys, _, q, qx, _, _, _ in units]
    dps = [mm(values, do, NT) for _, values, _, _, do, _, _ in units]
    weights = [jnp.exp2(s * coef - unit[5]) for s, unit in zip(scores, units)]
    dss = [(p * (dp - unit[6])).astype(bf16) for p, dp, unit in zip(weights, dps, units)]
    weights = [p.astype(bf16) for p in weights]
    results, first = [], 0
    for keys, _, tiles in blocks:
        here = range(first, first + 2 * len(tiles))
        first += 2 * len(tiles)
        keys_t = keys[:, :LANES].T
        dqs = []
        for n in here[::2]:
            parts = [mm(keys_t[h * size : (h + 1) * size], dss[n + h]) for h in range(2)]
            dqs.append((jnp.concatenate(parts, axis=0).T * scale).astype(bf16))
        dk = mm(jnp.concatenate([dss[n] for n in here], axis=1), jnp.concatenate([units[n][2] for n in here], axis=0)) * scale
        dv = mm(jnp.concatenate([weights[n] for n in here], axis=1), jnp.concatenate([units[n][4] for n in here], axis=0))
        results.append((dqs, dk, dv))
    return results


def inner_rows(o, do, size):
    prod = (o.astype(f32) * do.astype(f32)).T
    return [jnp.sum(prod[h * size : (h + 1) * size], axis=0, keepdims=True) for h in range(2)]


def edge_kernel(q_ref, k_ref, v_ref, lk_ref, lv_ref, rk_ref, rv_ref, qx_ref, kx_ref, o_ref, do_ref, lse_ref,
                dq_ref, dkv_ref, dg_ref, dl_ref, dr_ref, ks, vs, lses, *, size, coef, scale, own):
    step = pl.program_id(0)
    half = lk_ref.shape[0]
    glob = k_ref.shape[0] - own
    low = own - half

    @pl.when(step == 0)
    def _():
        fill_edge_masks(kx_ref, ks, own, half, glob)
        lses[:, :half] = lse_ref[:, :half]
        lses[:, half:] = lse_ref[:, low:]

    fill_edges(k_ref, lk_ref, rk_ref, ks, own, half)
    fill_edges(v_ref, lv_ref, rv_ref, vs, own, half)
    do = jnp.concatenate([do_ref[:half], do_ref[low:own]], axis=0)
    o = jnp.concatenate([o_ref[:half], o_ref[low:own]], axis=0)
    lse_rows = [lses[pl.ds(2 * step + h, 1), :] for h in range(2)]
    blocks = []
    for b, rows in enumerate((slice(0, half), slice(low, own))):
        there = slice(b * half, (b + 1) * half)
        blocks.append((ks[b], vs[b], [(q_ref[rows, :], qx_ref[rows, :], do[there], there)]))
    tails = []
    for b, (dqs, dk, dv) in enumerate(pair_backward(blocks, lse_rows, inner_rows(o, do, size), size, coef, scale)):
        there = slice(b * half, (b + 1) * half)
        dq_ref[there, :] = dqs[0]
        inside, outside = (slice(half, 2 * half), slice(0, half)) if b == 0 else (slice(0, half), slice(half, 2 * half))
        for n, part in enumerate((dk, dv)):
            dkv_ref[n, there, :] = part[inside]
            (dl_ref, dr_ref)[b][n] = part[outside].astype(bf16)
        tails.append((dk[2 * half :], dv[2 * half :]))
    for n in range(2):
        dg_ref[n] = tails[0][n] + tails[1][n]


def edge_backward(qkv, left, right, qx, kx, o, do, lse, own, size, coef, scale, after=()):
    rows, width = qkv.shape[0], qkv.shape[1] // 3
    pairs, half, glob = width // LANES, left.shape[0], rows - own

    def cols(n, off):
        return pl.BlockSpec((n, LANES), lambda p: (0, p + off))

    def both(n):
        return pl.BlockSpec((2, n, LANES), lambda p: (0, 0, p))

    fixed = pl.BlockSpec((own, LANES), lambda p: (0, 0))
    return pl.pallas_call(
        following(functools.partial(edge_kernel, size=size, coef=coef, scale=scale, own=own), 12, after),
        grid=(pairs,),
        in_specs=[
            cols(own, 0), cols(rows, pairs), cols(rows, 2 * pairs), cols(half, 0), cols(half, pairs), cols(half, 0), cols(half, pairs),
            fixed, whole(kx), cols(own, 0), cols(own, 0), whole(lse),
        ] + untouched(after),
        out_specs=[cols(2 * half, 0), both(2 * half), both(glob), both(half), both(half)],
        out_shape=[SDS((2 * half, width), bf16), SDS((2, 2 * half, width), f32), SDS((2, glob, width), f32)] + [SDS((2, half, width), bf16)] * 2,
        scratch_shapes=[
            pltpu.VMEM((2, 2 * half + glob, 2 * LANES), bf16), pltpu.VMEM((2, 2 * half + glob, LANES), bf16), pltpu.VMEM((16, 2 * half), f32),
        ],
        compiler_params=limits(60),
        cost_estimate=cost(17),
        name="edge_backward",
    )(qkv, qkv, qkv, left, left, right, right, qx, kx, o, do, lse, *after)


def inner_kernel(q_ref, k_ref, v_ref, qx_ref, kx_ref, o_ref, go_ref, do_ref, lse_ref, glse_ref, edq_ref, edkv_ref, edg_ref,
                 dq_ref, dkv_ref, ks, vs, lses, acc, *, size, coef, scale, own, half, first_pair):
    step = pl.program_id(0)
    rows = k_ref.shape[0]
    glob = rows - own
    blocks = ks.shape[0]
    pair = first_pair + step

    @pl.when(step == 0)
    def _():
        fill_inner_masks(kx_ref, ks, own, half, glob)
        lses[:, :own] = lse_ref[...]
        lses[:, own:] = glse_ref[...].T[:16]

    fill_inner(k_ref, ks, own, half)
    fill_inner(v_ref, vs, own, half)
    o = jnp.concatenate([o_ref[...], go_ref[...]], axis=0)
    lse_rows = [lses[pl.ds(2 * pair + h, 1), :] for h in range(2)]
    deltas = inner_rows(o, do_ref[...], size)
    kx_own = jnp.concatenate([kx_ref[half : half + own, :], kx_ref[2 * half + own :, :]], axis=0)

    def tile(at):
        return q_ref[at, :], qx_ref[at, :], do_ref[at, :], at

    every = [(jnp.concatenate([k_ref[...], kx_own], axis=1), v_ref[...], [tile(slice(own, rows))])]
    for b in range(blocks):
        low = half + b * 2 * half
        every.append((ks[b], vs[b], [tile(slice(low + j * half, low + (j + 1) * half)) for j in range(2)]))
    for b, (dqs, dk, dv) in enumerate(pair_backward(every, lse_rows, deltas, size, coef, scale)):
        for dq, (_, _, _, at) in zip(dqs, every[b][2]):
            dq_ref[at, :] = dq
        low = half + (b - 1) * 2 * half
        for n, part in enumerate((dk, dv)):
            if b == 0:
                acc[n] = part
            else:
                acc[n, low : low + 2 * half, :] += part[: 2 * half]
                acc[n, own:, :] += part[2 * half :]
    dq_ref[:half, :] = edq_ref[:half]
    dq_ref[own - half : own, :] = edq_ref[half:]
    for n in range(2):
        acc[n, :half, :] += edkv_ref[n, :half]
        acc[n, own - half : own, :] += edkv_ref[n, half:]
        acc[n, own:, :] += edg_ref[n]
    dkv_ref[...] = acc[...].astype(bf16)


def inner_backward(group, groups, qkv, qx, kx, o, go, do, lse, glse, edq, edkv, edg, own, half, size, coef, scale, after=()):
    rows, width = qkv.shape[0], qkv.shape[1] // 3
    pairs, glob = width // LANES, rows - own
    here = pairs // groups
    base = group * here
    blocks = own // (2 * half) - 1

    def cols(n, off=0):
        return pl.BlockSpec((n, LANES), lambda p: (0, base + p + off))

    def both(n):
        return pl.BlockSpec((2, n, LANES), lambda p: (0, 0, base + p))

    return pl.pallas_call(
        following(functools.partial(inner_kernel, size=size, coef=coef, scale=scale, own=own, half=half, first_pair=base), 13, after),
        grid=(here,),
        in_specs=[
            cols(rows), cols(rows, pairs), cols(rows, 2 * pairs), whole(qx), whole(kx), cols(own), cols(glob), cols(rows), whole(lse), whole(glse),
            cols(2 * half), both(2 * half), both(glob),
        ] + untouched(after),
        out_specs=[pl.BlockSpec((rows, LANES), lambda p: (0, p)), pl.BlockSpec((2, rows, LANES), lambda p: (0, 0, p))],
        out_shape=[SDS((rows, here * LANES), bf16), SDS((2, rows, here * LANES), bf16)],
        scratch_shapes=[
            pltpu.VMEM((blocks, 2 * half + glob, 2 * LANES), bf16), pltpu.VMEM((blocks, 2 * half + glob, LANES), bf16),
            pltpu.VMEM((16, rows), f32), pltpu.VMEM((2, rows, LANES), f32),
        ],
        compiler_params=limits(60),
        cost_estimate=cost(13),
        name="inner_backward",
    )(qkv, qkv, qkv, qx, kx, o, go, do, lse, glse, edq, edkv, edg, *after)


def weight_kernel(side_ref, nt_ref, ht_ref, dq_ref, dkv_ref, l_ref, r_ref, sent_ref, kept_ref, total, *, places):
    step = pl.program_id(0)

    @pl.when(step == 0)
    def _():
        total[...] = mm(nt_ref[...], dq_ref[...])

    @pl.when(step > 0)
    def _():
        total[...] = mm(nt_ref[...], dkv_ref[0]) + mm(ht_ref[...], jnp.concatenate([l_ref[0], r_ref[0]], axis=0))

    split_rows(total, side_ref[0], sent_ref, kept_ref, places)


def qkv_weight_grad(group, side, nt, ht, dq, dkv, dl, dr, places, after=()):
    width, rows = nt.shape
    cols, half = dq.shape[1], dl.shape[1]
    out = pl.BlockSpec((width // 2, cols), lambda c: (0, c))
    shape = SDS((width // 2, 3 * cols), bf16)
    halo = pl.BlockSpec((1, half, cols), lambda c: (jnp.maximum(c - 1, 0), 0, group))
    return pl.pallas_call(
        following(functools.partial(weight_kernel, places=places), 7, after),
        grid=(3,),
        in_specs=[
            pl.BlockSpec(memory_space=pltpu.SMEM), whole(nt), whole(ht), whole(dq),
            pl.BlockSpec((1, rows, cols), lambda c: (jnp.maximum(c - 1, 0), 0, 0)), halo, halo,
        ] + untouched(after),
        out_specs=[out, out],
        out_shape=[shape, shape],
        scratch_shapes=[pltpu.VMEM((width, cols), f32)],
        compiler_params=limits(60),
        cost_estimate=cost(0.1),
        name="qkv_weight_grad",
    )(side, nt, ht, dq, dkv, dl, dr, *after)


def norm_rows(x_ref, gain, dn):
    normalized, rstd = normalize(x_ref[...].astype(f32))
    sums = [jnp.sum(dn * normalized, axis=0, keepdims=True), jnp.sum(dn, axis=0, keepdims=True)]
    return norm_back(normalized, rstd, gain, dn), jnp.concatenate(sums + [jnp.zeros((6, dn.shape[1]), f32)], axis=0)


def halo_rows_kernel(lt_ref, rt_ref, vec_ref, w_ref, l_ref, r_ref, lout_ref, rout_ref, sums_ref):
    width = lt_ref.shape[1]
    sums = 0.0
    for x_ref, d_ref, out_ref in ((lt_ref, l_ref, lout_ref), (rt_ref, r_ref, rout_ref)):
        dn = mm(d_ref[0], w_ref[:, width : 2 * width], NT) + mm(d_ref[1], w_ref[:, 2 * width :], NT)
        back, part = norm_rows(x_ref, vec_ref[0:1, :], dn)
        out_ref[...] = back.astype(bf16)
        sums = sums + part
    sums_ref[...] = sums


def halo_rows(left, right, vec, w, dl, dr, after=()):
    args = (left, right, vec, w, dl, dr)
    half, width = left.shape
    return pl.pallas_call(
        following(halo_rows_kernel, len(args), after),
        in_specs=[whole(a) for a in args] + untouched(after),
        out_specs=[whole(left), whole(right), pl.BlockSpec((8, width), lambda: (0, 0))],
        out_shape=[SDS(left.shape, bf16), SDS(right.shape, bf16), SDS((8, width), f32)],
        compiler_params=limits(60),
        cost_estimate=cost(4),
        name="halo_rows",
    )(*args, *after)


def rows_kernel(flag_ref, x_ref, vec_ref, mg_ref, w_ref, *refs, groups, edges):
    width = x_ref.shape[1]
    step, last = pl.program_id(0), pl.num_programs(0) - 1
    out_ref, sums_ref = refs[-2:]
    cols = width // groups
    dn = 0.0
    for g in range(groups):
        dq_ref, dkv_ref = refs[2 * g : 2 * g + 2]
        for part, d in enumerate((dq_ref[...], dkv_ref[0], dkv_ref[1])):
            at = part * width + g * cols
            dn = dn + mm(d, w_ref[:, at : at + cols], NT)
    back, sums = norm_rows(x_ref, vec_ref[0:1, :], dn)
    out = mg_ref[...].astype(f32) * flag_ref[0] + back
    out_ref[...] = out.astype(out_ref.dtype)

    @pl.when(step == 0)
    def _():
        sums_ref[...] = sums

    @pl.when(step > 0)
    def _():
        sums_ref[...] += sums

    if edges:
        l_ref, r_ref = refs[2 * groups : 2 * groups + 2]

        @pl.when(step == 0)
        def _():
            out_ref[...] = out + l_ref[...].astype(f32)

        @pl.when(step == last)
        def _():
            out_ref[...] = out + r_ref[...].astype(f32)


def row_grads(flag, x, vec, mg, w, parts, start, block, dtype, edges=(), after=()):
    count, width = x.shape
    groups = len(parts)
    cols = width // groups
    base = start // block
    specs, args = [], []
    for dq, dkv in parts:
        specs += [pl.BlockSpec((block, cols), lambda r: (base + r, 0)), pl.BlockSpec((2, block, cols), lambda r: (0, base + r, 0))]
        args += [dq, dkv]
    here = pl.BlockSpec((block, width), lambda r: (r, 0))
    args = [flag, x, vec, mg, w] + args + list(edges)
    return pl.pallas_call(
        following(functools.partial(rows_kernel, groups=groups, edges=bool(edges)), len(args), after),
        grid=(count // block,),
        in_specs=[pl.BlockSpec(memory_space=pltpu.SMEM), here, whole(vec), pl.BlockSpec((block, width), lambda r: (base + r, 0)), whole(w)] + specs + [whole(e) for e in edges] + untouched(after),
        out_specs=[here, pl.BlockSpec((8, width), lambda r: (0, 0))],
        out_shape=[SDS(x.shape, dtype), SDS((8, width), f32)],
        compiler_params=limits(60),
        cost_estimate=cost(10 if edges else 0.1),
        name="row_grads",
    )(*args, *after)


def add_kernel(own_ref, other_ref, out_ref):
    out_ref[...] = (own_ref[...].astype(f32) + other_ref[...].astype(f32)).astype(out_ref.dtype)


def add_step(part, bit, dtype, after=()):
    return pl.pallas_call(
        following(add_kernel, 2, after),
        in_specs=[whole(part), whole(part)] + untouched(after),
        out_specs=whole(part),
        out_shape=SDS(part.shape, dtype),
        cost_estimate=cost(1),
        name="add_step",
    )(part, swapped(part, *bit), *after)


def as_column(row):
    n = row.shape[1]
    eye = lax.broadcasted_iota(jnp.int32, (n, n), 0) == lax.broadcasted_iota(jnp.int32, (n, n), 1)
    return jnp.sum(jnp.where(eye, row, 0.0), axis=1, keepdims=True)


def split_shards(qkv_ref, rest_ref, units, width):
    groups = (rest_ref.shape[1] - units - width) // width
    starts = [units + width * (k + 1) for k in range(groups)]
    return qkv_ref[...], rest_ref[:, units : units + width], rest_ref[:, :units], [rest_ref[:, at : at + width] for at in starts]


def pack_kernel(qkv_ref, rest_ref, rq_ref, ro_ref, ru_ref, rd_ref, vone_ref, vtwo_ref, bias_ref,
                stats_ref, gout_ref, gup_ref, gdown_ref, nq_ref, no_ref, nu_ref, nd_ref, cq_ref, co_ref, cu_ref, cd_ref, *, decay):
    units, width = bias_ref.shape[1], vone_ref.shape[1]
    g_qkv, g_out, g_up, g_down = split_shards(qkv_ref, rest_ref, units, width)
    rows = g_qkv.shape[0]
    gout_ref[...], gup_ref[...] = g_out, g_up
    at, totals = 0, []
    for g, old_ref, new_ref, col_ref in ((g_qkv, rq_ref, nq_ref, cq_ref), (g_out, ro_ref, no_ref, co_ref), (g_up, ru_ref, nu_ref, cu_ref), (g_down, rd_ref, nd_ref, cd_ref)):
        groups = g if isinstance(g, list) else [g]
        columns, total, means = 0.0, 0.0, []
        for k, part in enumerate(groups):
            square = part * part + TINY_SQUARE
            columns = columns + jnp.sum(square, axis=0, keepdims=True)
            means.append(jnp.mean(square, axis=1, keepdims=True))
            if len(groups) > 1:
                gdown_ref[k * rows : (k + 1) * rows, :] = part
        mean = means[0] if len(means) == 1 else jnp.concatenate(means, axis=0)
        new = decay * as_column(old_ref[...].reshape(1, -1)) + (1.0 - decay) * mean
        col_ref[...] = new
        new_ref[...] = jnp.sum(jnp.where(lax.broadcasted_iota(jnp.int32, (new.shape[0],) * 2, 0) == lax.broadcasted_iota(jnp.int32, (new.shape[0],) * 2, 1), new, 0.0), axis=0)
        totals.append(jnp.sum(new, axis=0, keepdims=True))
        stats_ref[:, at : at + columns.shape[1]] = columns
        at += columns.shape[1]
    for ref, count in ((vone_ref, 2), (vtwo_ref, 3)):
        for n in range(count):
            stats_ref[:, at : at + width] = ref[n : n + 1, :]
            at += width
    stats_ref[:, at : at + units] = bias_ref[...]
    at += units
    lane = lax.broadcasted_iota(jnp.int32, (1, LANES), 1)
    last = jnp.zeros((1, LANES), f32)
    for n, total in enumerate(totals):
        last = jnp.where(lane == n, total, last)
    stats_ref[:, at : at + LANES] = last


def pack(qkv, rest, row_olds, vec_one, vec_two, bias, decay):
    units, width, rows = bias.shape[1], vec_one.shape[1], qkv.shape[0]
    tall = rest.shape[1] // width - units // width - 1
    count = qkv.shape[1] + width + units + width + 5 * width + units + LANES
    shapes = [(1, count), (rows, width), (rows, units), (tall * rows, width)]
    shapes += [old.shape for old in row_olds] + [(old.shape[0], 1) for old in row_olds]
    args = (qkv, rest, *row_olds, vec_one, vec_two, bias)
    return pl.pallas_call(
        functools.partial(pack_kernel, decay=decay),
        out_shape=[SDS(shape, f32) for shape in shapes],
        compiler_params=limits(60),
        cost_estimate=cost(3),
        name="pack",
    )(*args)


def update_kernel(stats_ref, qkv_ref, rest_ref, rq_ref, ro_ref, ru_ref, rd_ref, mq_ref, mo_ref, mu_ref, md_ref, oq_ref, oo_ref, ou_ref, od_ref,
                  vec_ref, vstate_ref, bias_ref, bstate_ref,
                  nq_ref, no_ref, nu_ref, nd_ref, cq_ref, co_ref, cu_ref, cd_ref, vg_ref, vs_ref, vn_ref, bg_ref, bs_ref, bn_ref, *, decay, full_rows):
    width, units = vec_ref.shape[1], bias_ref.shape[0]
    shards = split_shards(qkv_ref, rest_ref, units, width)
    rows = qkv_ref.shape[0]
    stats = stats_ref[...]
    totals = stats[:, stats.shape[1] - LANES :]
    at = 0
    sets = zip(shards, (rq_ref, ro_ref, ru_ref, rd_ref), (mq_ref, mo_ref, mu_ref, md_ref), (oq_ref, oo_ref, ou_ref, od_ref), (nq_ref, no_ref, nu_ref, nd_ref), (cq_ref, co_ref, cu_ref, cd_ref), full_rows)
    for n, (shard, row_ref, master_ref, old_ref, new_ref, col_ref, count) in enumerate(sets):
        columns = old_ref.shape[0]
        col = decay * old_ref[...].reshape(1, columns) + (1.0 - decay) * (stats[:, at : at + columns] / count)
        at += columns
        col_ref[...] = col[0]
        row_mean = totals[:, n : n + 1] / count
        parts = shard if isinstance(shard, list) else [shard]
        master = master_ref[...].astype(f32)
        for k, part in enumerate(parts):
            here = slice(k * rows, (k + 1) * rows)
            estimate = row_ref[here, :] * col / row_mean
            new_ref[here, :] = master[here] - RATE_MATRIX * part * lax.rsqrt(estimate)
    grad = jnp.concatenate([stats[:, at + n * width : at + (n + 1) * width] for n in range(5)], axis=0)
    at += 5 * width
    vg_ref[...] = grad
    state = decay * vstate_ref[...] + (1.0 - decay) * (grad * grad + TINY_SQUARE)
    vs_ref[...] = state
    vn_ref[...] = vec_ref[...] - RATE_VECTOR * grad * lax.rsqrt(state)
    grad = stats[:, at : at + units]
    bg_ref[...] = grad[0]
    state = decay * bstate_ref[...].reshape(1, units) + (1.0 - decay) * (grad * grad + TINY_SQUARE)
    bs_ref[...] = state[0]
    bn_ref[...] = (bias_ref[...].reshape(1, units) - RATE_VECTOR * grad * lax.rsqrt(state))[0]


def update(stats, qkv, rest, row_columns, masters, col_olds, vec, vec_state, bias, bias_state, decay, full_rows):
    args = (stats, qkv, rest, *row_columns, *masters, *col_olds, vec, vec_state, bias, bias_state)
    shapes = [m.shape for m in masters] + [c.shape for c in col_olds] + [vec.shape] * 3 + [bias.shape] * 3
    return pl.pallas_call(
        functools.partial(update_kernel, decay=decay, full_rows=full_rows),
        out_shape=[SDS(shape, f32) for shape in shapes],
        compiler_params=limits(60),
        cost_estimate=cost(3),
        name="update",
    )(*args)


def mask_lanes(segments, valid, start, own, half, glob, first):
    count = own + 2 * half
    seg = lax.dynamic_slice_in_dim(jnp.pad(segments, half), start, count)[:, None]
    ok = lax.dynamic_slice_in_dim(jnp.pad(valid, half), start, count)[:, None] > 0
    lane = lax.broadcasted_iota(jnp.int32, (count, LANES), 1)
    seen = ok & ((seg == lane) | (lane == 4)) | (lane > 4)
    kx = jnp.where(seen, 0.0, NEG_FILL).astype(bf16)
    lane_g = lax.broadcasted_iota(jnp.int32, (glob, LANES), 1)
    kx_glob = jnp.where((lane_g == 4) & ~first, NEG_FILL, 0.0).astype(bf16)
    qx = (seg[half : half + own] == lane[:own]) & (lane[:own] < 4)
    qx = jnp.concatenate([qx, lane_g == 4], axis=0).astype(bf16)
    return qx, jnp.concatenate([kx, kx_glob], axis=0)


def body(
    tokens,
    glob_tokens,
    w_qkv,
    w_out,
    w_up,
    w_down,
    vec_params,
    hidden_bias,
    row_qkv,
    col_qkv,
    row_out,
    col_out,
    row_up,
    col_up,
    row_down,
    col_down,
    vec_state,
    bias_state,
    segments,
    valid_mask,
    out_cotangent,
    glob_cotangent,
):
    width = w_out.shape[0]
    size = width // HEADS
    assert 2 * size == LANES
    scale = size ** (-0.5)
    coef = scale * LOG2E
    half = BLOCK // 2
    tok, glob = tokens[0], glob_tokens[0]
    own, globs = tok.shape[0], glob.shape[0]
    seq_index = lax.axis_index("seq")
    first = seq_index == 0
    flag = first.astype(f32).reshape(1)
    bias_row = hidden_bias[None, :]
    batch_bits, seq_bits = bits_of("batch"), bits_of("seq")

    low, high = [batch_bits[:1]], [[bit] for bit in batch_bits[1:]]
    far = [seq_bits[1:][n : n + 2] for n in range(0, len(seq_bits) - 1, 2)]
    wide_stages = low + high + [seq_bits[:1]]
    tall_stages = low + [seq_bits[:1]] + high
    joint_stages = [[bit] for bit in seq_bits[1:]]
    pair_stages = low + [batch_bits[1:] + seq_bits[:1]] + far
    places = row_places(width, pair_stages)
    sequence = np.arange(1 << len(seq_bits)).reshape([2] * len(seq_bits)).transpose(
        [seq_bits[::-1].index(bit) for bit in seq_bits]
    ).reshape(-1)
    tall_chunk = w_down.shape[0] // lax.axis_size("batch") // sequence.size
    tall_places = tuple(int(n) * tall_chunk for n in sequence), tall_chunk
    halo_left, halo_right = shifted(tok[own - half :], "seq", 1), shifted(tok[:half], "seq", -1)
    qx, kx = mask_lanes(segments[0], valid_mask[0], seq_index * own, own, half, globs, first)
    qkv, normed_t = project(tok, glob, w_qkv, vec_params)
    part = glob_attention(qkv, qx, kx, own, half, size, coef)
    left, right, halo_t = project_halos(halo_left, halo_right, w_qkv, vec_params)
    part, glob_lse = merge_step(part, *seq_bits[0], size, after=[left])
    inner_att, inner_lse = local_inner(qkv, qx, kx, own, half, size, coef, after=[part])
    for bit in seq_bits[1:-1]:
        part, glob_lse = merge_step(part, *bit, size, after=[inner_lse])
    att, lse = local_edge(qkv, left, right, qx, kx, inner_att, inner_lse, own, half, size, coef, after=[part])
    part, glob_lse = merge_step(part, *seq_bits[-1], size, after=[lse])
    side = side_of(*batch_bits[0]).reshape(1)
    out_tok, out_glob, mixed_grad, heads_grad, *matrices, vec_two, bias_sum = feed_forward(
        side, flag, att, part, tok, glob, w_out, w_up, w_down, vec_params, bias_row, out_cotangent[0], glob_cotangent[0], places, tall_places
    )
    wide, down = Scatter(*matrices[:2], wide_stages), Scatter(*matrices[2:], tall_stages)
    edge = edge_backward(qkv, left, right, qx, kx, att, heads_grad, lse, own, size, coef, scale, after=wide.parts + down.parts)
    grad_left, grad_right = edge[3:]
    down.step(after=edge[:1])
    wide.step(after=down.parts)
    to_left, to_right, halo_sums = halo_rows(halo_left, halo_right, vec_params, w_qkv, grad_left, grad_right, after=wide.parts)
    edges = (shifted(to_right, "seq", 1), shifted(to_left, "seq", -1))
    shared = (qkv, qx, kx, att, part, heads_grad, lse, glob_lse, *edge[:3], own, half, size, coef, scale)
    parts = [inner_backward(0, 1, *shared, after=[to_left, to_right])]
    down.step(after=[parts[0][0], *edges])
    wide.step(after=down.parts)
    glob_part, glob_sums = row_grads(flag, glob, vec_params, mixed_grad, w_qkv, parts, own, globs, bf16, after=wide.parts)
    weight = Scatter(*qkv_weight_grad(0, side, normed_t, halo_t, *parts[0], grad_left, grad_right, places, after=[glob_part]), pair_stages)
    glob_part = add_step(glob_part, seq_bits[0], bf16, after=weight.parts)
    joint = joint_scatter(wide, down, joint_stages, after=[glob_part])
    weight.step(after=joint.parts)
    for bit in seq_bits[1:-1]:
        glob_part = add_step(glob_part, bit, bf16, after=weight.parts)
    tokens_grad, tok_sums = row_grads(
        jnp.ones((1,), f32), tok, vec_params, mixed_grad, w_qkv, parts, 0, half, f32, edges=edges, after=[glob_part]
    )
    joint.step(after=[tok_sums])
    weight.step(after=joint.parts)
    glob_part = add_step(glob_part, seq_bits[-1], f32, after=weight.parts)
    while joint.stages:
        rest = joint.step(after=[glob_part])
    while weight.stages:
        shard_qkv = weight.step(after=[rest])
    decay = 1.0 - STEP ** (-0.8)
    units = w_up.shape[1]
    owner = lax.axis_index(("batch", "seq"))
    masters = []
    for matrix in (w_qkv, w_out, w_up, w_down):
        rows = matrix.shape[0] // lax.axis_size(("batch", "seq"))
        masters.append(lax.dynamic_slice_in_dim(matrix, owner * rows, rows, 0))
    stats, grad_out, grad_up, grad_down, *rows_new = pack(
        shard_qkv, rest, (row_qkv, row_out, row_up, row_down), halo_sums + glob_sums + tok_sums, vec_two, bias_sum, decay
    )
    for bit in batch_bits + seq_bits:
        stats = stats + swapped(stats, *bit)
    new_qkv, new_out, new_up, new_down, col_qkv_new, col_out_new, col_up_new, col_down_new, *vectors = update(
        stats, shard_qkv, rest, rows_new[4:], masters, (col_qkv, col_out, col_up, col_down), vec_params, vec_state, hidden_bias, bias_state,
        decay, (w_qkv.shape[0], w_out.shape[0], w_up.shape[0], w_down.shape[0]),
    )
    return (
        out_tok[None],
        out_glob[None],
        tokens_grad[None],
        glob_part[None],
        shard_qkv,
        rows_new[0],
        col_qkv_new,
        new_qkv,
        grad_out,
        rows_new[1],
        col_out_new,
        new_out,
        grad_up,
        rows_new[2],
        col_up_new,
        new_up,
        grad_down,
        rows_new[3],
        col_down_new,
        new_down,
        *vectors,
    )


def solution(mesh):
    in_specs = (
        P("batch", "seq", None),
        P("batch", None, None),
        P(),
        P(),
        P(),
        P(),
        P(),
        P(),
        P(("batch", "seq")),
        P(),
        P(("batch", "seq")),
        P(),
        P(("batch", "seq")),
        P(),
        P(("batch", "seq")),
        P(),
        P(),
        P(),
        P("batch", None),
        P("batch", None),
        P("batch", "seq", None),
        P("batch", None, None),
    )
    out_specs = (
        P("batch", "seq", None),
        P("batch", None, None),
        P("batch", "seq", None),
        P("batch", None, None),
        P(("batch", "seq"), None),
        P(("batch", "seq")),
        P(),
        P(("batch", "seq"), None),
        P(("batch", "seq"), None),
        P(("batch", "seq")),
        P(),
        P(("batch", "seq"), None),
        P(("batch", "seq"), None),
        P(("batch", "seq")),
        P(),
        P(("batch", "seq"), None),
        P(("batch", "seq"), None),
        P(("batch", "seq")),
        P(),
        P(("batch", "seq"), None),
        P(),
        P(),
        P(),
        P(),
        P(),
        P(),
    )
    return jax.shard_map(body, mesh=mesh, in_specs=in_specs, out_specs=out_specs, check_vma=False)
```

```python
import functools

import jax
import jax.numpy as jnp
import numpy as np
from jax import lax
from jax.experimental import pallas as pl
from jax.experimental.pallas import tpu as pltpu
from jax.sharding import PartitionSpec as P

HEADS = 12
BLOCK = 512
STEP = 10

NEG_FILL = -8e9
NORM_EPS = 1e-06
TINY_SQUARE = 1e-30
RATE_MATRIX = 0.03
RATE_VECTOR = 0.2
LANES = 128
LOG2E = 1.4426950408889634

f32, bf16 = jnp.float32, jnp.bfloat16
NN = (((1,), (0,)), ((), ()))
NT = (((1,), (1,)), ((), ()))
TN = (((0,), (0,)), ((), ()))
SDS = jax.ShapeDtypeStruct


def bits_of(axis):
    size = lax.axis_size(axis)
    assert size & (size - 1) == 0
    return [(axis, 1 << k) for k in range(size.bit_length() - 1)]


def side_of(axis, bit):
    return (lax.axis_index(axis) // bit) % 2


def swapped(values, axis, bit):
    return lax.ppermute(values, axis, [(i, i ^ bit) for i in range(lax.axis_size(axis))])


def shifted(values, axis, distance):
    devices = range(lax.axis_size(axis))
    return lax.ppermute(values, axis, [(i, i + distance) for i in devices if i + distance in devices])


def summed(parts, bits):
    leaves, tree = jax.tree.flatten(parts)
    flat = jnp.concatenate([leaf.reshape(-1) for leaf in leaves])
    count = flat.shape[0]
    flat = jnp.pad(flat, (0, -count % 1024)).reshape(-1, LANES)
    for axis, bit in bits:
        flat = flat + swapped(flat, axis, bit)
    flat = flat.reshape(-1)
    out, place = [], 0
    for leaf in leaves:
        out.append(flat[place : place + leaf.size].reshape(leaf.shape))
        place += leaf.size
    return jax.tree.unflatten(tree, out)


def flipped(values, bits, flips):
    sizes = {axis: lax.axis_size(axis) for axis in ("batch", "seq")}
    change = {axis: sum(bit for n, (name, bit) in enumerate(bits) if name == axis and flips >> n & 1) for axis in sizes}
    route = [
        (b * sizes["seq"] + s, (b ^ change["batch"]) * sizes["seq"] + (s ^ change["seq"]))
        for b in range(sizes["batch"])
        for s in range(sizes["seq"])
    ]
    return lax.ppermute(values, ("batch", "seq"), route)


def mm(a, b, dims=NN):
    return lax.dot_general(a, b, dims, preferred_element_type=f32)


def limits(mib):
    return pltpu.CompilerParams(vmem_limit_bytes=mib * 2**20)


def cost(us):
    return pl.CostEstimate(flops=int(us * 1.15e9), bytes_accessed=1 << 20, transcendentals=0)


def whole(array):
    return pl.BlockSpec(array.shape, lambda *_: (0,) * array.ndim)


def following(kernel, inputs, after):
    return lambda *refs: kernel(*refs[:inputs], *refs[inputs + len(after) :])


def untouched(after):
    return [pl.BlockSpec(memory_space=pl.ANY)] * len(after)


def normalize(x):
    mean = jnp.mean(x, axis=1, keepdims=True)
    centred = x - mean
    rstd = lax.rsqrt(jnp.mean(centred * centred, axis=1, keepdims=True) + NORM_EPS)
    return centred * rstd, rstd


def norm_back(normalized, rstd, gain, grad):
    g = grad * gain
    inner = jnp.mean(g * normalized, axis=1, keepdims=True)
    return rstd * (g - jnp.mean(g, axis=1, keepdims=True) - normalized * inner)


def gelu_both(u):
    phi = 0.5 + 0.5 * lax.erf(u * 0.7071067811865476)
    density = jnp.exp2(u * u * (-0.5 * LOG2E)) * 0.3989422804014327
    return u * phi, phi + u * density


def head_part(values, head, size):
    lanes = lax.broadcasted_iota(jnp.int32, values.shape, 1)
    return jnp.where((lanes // size) == head, values, jnp.zeros_like(values))


def stage_kernel(side_ref, kept_ref, *refs, arrived, parts):
    for n in range(parts):
        at = side_ref[0] ^ n if parts > 1 else 0
        total = kept_ref[at].astype(f32)
        for ref in refs[:arrived]:
            total = total + ref[at].astype(f32)
        out = refs[arrived + n]
        out[...] = total.astype(out.dtype)


class Scatter:
    def __init__(self, sent, kept, stages):
        self.stages, self.parts, self.kept = list(stages), [sent], kept

    def step(self, after=(), us=2):
        bits = self.stages.pop(0)
        arrived = [flipped(part, bits[::-1], n + 1) for n, part in enumerate(self.parts)]
        bits = self.stages[0] if self.stages else []
        parts, columns = 1 << len(bits), self.kept.shape[-1]
        rows = self.kept.size // columns // parts
        block = columns if self.kept.size < 1 << 20 else columns // 3 if columns % 1152 == 0 or columns % 3840 == 0 else columns
        tall = 2 if columns == block and rows % 32 == 0 and self.kept.size > 1 << 19 else 1
        args = [a.reshape(parts, rows, columns) for a in [self.kept] + arrived]
        side = sum(side_of(*bit) << n for n, bit in enumerate(reversed(bits))) if bits else jnp.int32(0)
        spec = pl.BlockSpec((parts, rows // tall, block), lambda c, r: (0, r, c))
        out = pl.BlockSpec((rows // tall, block), lambda c, r: (r, c))
        after = list(after)
        self.kept, *self.parts = pl.pallas_call(
            following(functools.partial(stage_kernel, arrived=len(arrived), parts=parts), 1 + len(args), after),
            grid=(columns // block, tall),
            in_specs=[pl.BlockSpec(memory_space=pltpu.SMEM)] + [spec] * len(args) + untouched(after),
            out_specs=[out] * parts,
            out_shape=[SDS((rows, columns), bf16 if bits else f32)] + [SDS((rows, columns), bf16)] * (parts - 1),
            compiler_params=limits(60),
            cost_estimate=cost(us),
            name="sum_stage",
        )(side.reshape(1), *args, *after)
        return self.kept


def joint_kernel(side_ref, wk_ref, wa_ref, dk_ref, da_ref, sent_ref, kept_ref, total, *, chunk, starts):
    columns = wk_ref.shape[2]
    block = dk_ref.shape[2]
    for ref, flip in ((sent_ref, 1), (kept_ref, 0)):
        at = side_ref[0] ^ flip
        ref[:, :columns] = (wk_ref[at].astype(f32) + wa_ref[at].astype(f32)).astype(bf16)
        total[...] = dk_ref[at].astype(f32) + da_ref[at].astype(f32)
        for k, places in enumerate(starts):
            ref[:, columns + k * block : columns + (k + 1) * block] = gathered(total, places, chunk)


def joint_scatter(wide, down, stages, after=()):
    (bit,) = stages[0]
    args = []
    for scatter in (wide, down):
        bits = scatter.stages.pop(0)
        arrived = flipped(scatter.parts[0], bits, 1)
        args += [a.reshape(2, -1, a.shape[-1]) for a in (scatter.kept, arrived)]
    _, rows, columns = args[0].shape
    _, rows_down, block = args[2].shape
    owners = 1 << (len(stages) - 1)
    chunk = rows // owners
    groups = rows_down // rows
    starts = [[(n * groups + k) * chunk for n in range(owners)] for k in range(groups)]
    shape = SDS((rows, columns + groups * block), bf16)
    after = list(after)
    sent, kept = pl.pallas_call(
        following(functools.partial(joint_kernel, chunk=chunk, starts=starts), 5, after),
        in_specs=[pl.BlockSpec(memory_space=pltpu.SMEM)] + [whole(a) for a in args] + untouched(after),
        out_specs=[pl.BlockSpec(shape.shape, lambda: (0, 0))] * 2,
        out_shape=[shape, shape],
        scratch_shapes=[pltpu.VMEM((rows_down, block), f32)],
        compiler_params=limits(60),
        cost_estimate=cost(100),
        name="joint_stage",
    )(side_of(*bit).reshape(1), *args, *after)
    return Scatter(sent, kept, stages)


def row_places(width, stages):
    labels = bits_of("batch")[::-1] + bits_of("seq")[::-1]
    owners = np.arange(1 << len(labels)).reshape([2] * len(labels))
    owners = owners.transpose([labels.index(bit) for stage in stages for bit in stage]).reshape(2, -1)
    chunk = width // owners.size
    return tuple(int(owner) * chunk for owner in owners[0]), chunk, int(owners[1, 0] - owners[0, 0]) * chunk


def project_kernel(tok_ref, glob_ref, w_ref, vec_ref, qkv_ref, nt_ref, n_s):
    own = tok_ref.shape[0]

    @pl.when(pl.program_id(0) == 0)
    def _():
        for ref, rows in ((tok_ref, slice(0, own)), (glob_ref, slice(own, n_s.shape[0]))):
            n = normalize(ref[...].astype(f32))[0] * vec_ref[0:1, :] + vec_ref[1:2, :]
            n = n.astype(bf16)
            n_s[rows, :] = n
            nt_ref[:, rows] = n.T

    qkv_ref[...] = mm(n_s[...], w_ref[...]).astype(bf16)


def project(tok, glob, w, vec):
    width = tok.shape[1]
    rows = tok.shape[0] + glob.shape[0]
    return pl.pallas_call(
        project_kernel,
        grid=(w.shape[1] // width,),
        in_specs=[whole(tok), whole(glob), pl.BlockSpec((width, width), lambda c: (0, c)), whole(vec)],
        out_specs=[
            pl.BlockSpec((rows, width), lambda c: (0, c)),
            pl.BlockSpec((width, rows), lambda c: (0, 0)),
        ],
        out_shape=[SDS((rows, w.shape[1]), bf16), SDS((width, rows), bf16)],
        scratch_shapes=[pltpu.VMEM((rows, width), bf16)],
        compiler_params=limits(60),
        cost_estimate=cost(9),
        name="project",
    )(tok, glob, w, vec)


def halo_kernel(l_ref, r_ref, w_ref, vec_ref, lkv_ref, rkv_ref, nt_ref):
    half = l_ref.shape[0]
    for ref, out, at in ((l_ref, lkv_ref, 0), (r_ref, rkv_ref, half)):
        n = normalize(ref[...].astype(f32))[0] * vec_ref[0:1, :] + vec_ref[1:2, :]
        n = n.astype(bf16)
        nt_ref[:, at : at + half] = n.T
        out[...] = mm(n, w_ref[...]).astype(bf16)


def project_halos(left, right, w, vec):
    half, width = left.shape
    kv = pl.BlockSpec((half, width), lambda c: (0, c))
    return pl.pallas_call(
        halo_kernel,
        grid=(2,),
        in_specs=[whole(left), whole(right), pl.BlockSpec((width, width), lambda c: (0, c + 1)), whole(vec)],
        out_specs=[kv, kv, pl.BlockSpec((width, 2 * half), lambda c: (0, 0))],
        out_shape=[SDS((half, 2 * width), bf16)] * 2 + [SDS((width, 2 * half), bf16)],
        compiler_params=limits(60),
        cost_estimate=cost(3),
        name="project_halos",
    )(left, right, w, vec)


def attend_pairs(tiles, lse_rows, step, size, coef):
    scores = []
    for q, qx, keys, _ in tiles:
        for h in range(2):
            scores.append(mm(keys, jnp.concatenate([head_part(q, h, size), qx], axis=1), NT))
    tops = [jnp.max(s, axis=0, keepdims=True) * coef for s in scores]
    weights = [jnp.exp2(s * coef - top) for s, top in zip(scores, tops)]
    totals = [jnp.sum(p, axis=0, keepdims=True) for p in weights]
    outs = []
    for n, p in enumerate(weights):
        h = n % 2
        values_t = tiles[n // 2][3].T[h * size : (h + 1) * size]
        outs.append(mm(values_t, p.astype(bf16)) * (1.0 / totals[n]))
    results = []
    for n, lse in enumerate(lse_rows):
        row = lax.broadcasted_iota(jnp.int32, lse.shape, 0)
        for h in range(2):
            lse = jnp.where(row == 2 * step + h, tops[2 * n + h] + jnp.log2(totals[2 * n + h]), lse)
        results.append((jnp.concatenate(outs[2 * n : 2 * n + 2], axis=0).T.astype(bf16), lse))
    return results


def mask_piece(kx_ref, name, low, rows, own, half):
    if name == "l":
        start = low
    elif name == "r":
        start = half + own + low
    else:
        start = half + low if low < own else 2 * half + low
    return kx_ref[start : start + rows, :]


def fill_inner(src, dst, own, half):
    for b in range(dst.shape[0]):
        low = half + b * 2 * half
        dst[b, : 2 * half, :LANES] = src[low : low + 2 * half]
        dst[b, 2 * half :, :LANES] = src[own:]


def fill_inner_masks(kx_ref, dst, own, half, glob):
    for b in range(dst.shape[0]):
        dst[b, : 2 * half, LANES:] = mask_piece(kx_ref, "o", half + b * 2 * half, 2 * half, own, half)
        dst[b, 2 * half :, LANES:] = mask_piece(kx_ref, "o", own, glob, own, half)


def fill_edges(src, l_ref, r_ref, dst, own, half):
    dst[0, :half, :LANES] = l_ref[...]
    dst[0, half : 2 * half, :LANES] = src[:half]
    dst[1, :half, :LANES] = src[own - half : own]
    dst[1, half : 2 * half, :LANES] = r_ref[...]
    for b in range(2):
        dst[b, 2 * half :, :LANES] = src[own:]


def fill_edge_masks(kx_ref, dst, own, half, glob):
    for at, name, low in ((0, "l", 0), (1, "o", 0), (2, "o", own - half), (3, "r", 0)):
        dst[at // 2, at % 2 * half : (at % 2 + 1) * half, LANES:] = mask_piece(kx_ref, name, low, half, own, half)
    for b in range(2):
        dst[b, 2 * half :, LANES:] = mask_piece(kx_ref, "o", own, glob, own, half)


def local_inner_kernel(q_ref, k_ref, v_ref, qx_ref, kx_ref, o_ref, lse_ref, ks, vs, *, size, coef, own, half):
    step = pl.program_id(0)
    glob = k_ref.shape[0] - own

    @pl.when(step == 0)
    def _():
        fill_inner_masks(kx_ref, ks, own, half, glob)
        lse_ref[...] = jnp.zeros_like(lse_ref)

    fill_inner(k_ref, ks, own, half)
    fill_inner(v_ref, vs, own, half)
    places = [slice(j * half, (j + 1) * half) for j in range(own // half - 2)]
    tiles = []
    for j, there in enumerate(places):
        rows = slice(there.start + half, there.stop + half)
        tiles.append((q_ref[rows, :], qx_ref[rows, :], ks[j // 2], vs[j // 2]))
    for there, (o, lse) in zip(places, attend_pairs(tiles, [lse_ref[:, there] for there in places], step, size, coef)):
        o_ref[there, :], lse_ref[:, there] = o, lse


def local_edge_kernel(q_ref, k_ref, v_ref, lk_ref, lv_ref, rk_ref, rv_ref, qx_ref, kx_ref, io_ref, ilse_ref, o_ref, lse_ref, ks, vs, *, size, coef):
    step = pl.program_id(0)
    own, half = q_ref.shape[0], lk_ref.shape[0]
    glob = k_ref.shape[0] - own

    @pl.when(step == 0)
    def _():
        fill_edge_masks(kx_ref, ks, own, half, glob)
        lse_ref[...] = jnp.zeros_like(lse_ref)
        lse_ref[:, half : own - half] = ilse_ref[...]

    fill_edges(k_ref, lk_ref, rk_ref, ks, own, half)
    fill_edges(v_ref, lv_ref, rv_ref, vs, own, half)
    o_ref[half : own - half, :] = io_ref[...]
    places = [slice(0, half), slice(own - half, own)]
    tiles = [(q_ref[rows, :], qx_ref[rows, :], ks[b], vs[b]) for b, rows in enumerate(places)]
    for rows, (o, lse) in zip(places, attend_pairs(tiles, [lse_ref[:, rows] for rows in places], step, size, coef)):
        o_ref[rows, :], lse_ref[:, rows] = o, lse


def local_inner(qkv, qx, kx, own, half, size, coef, after=()):
    rows, width = qkv.shape[0], qkv.shape[1] // 3
    pairs, inner = width // LANES, own - 2 * half
    blocks, span = own // (2 * half) - 1, 2 * half + rows - own

    def cols(n, off=0):
        return pl.BlockSpec((n, LANES), lambda p: (0, p + off))

    def fixed(n):
        return pl.BlockSpec((n, LANES), lambda p: (0, 0))

    return pl.pallas_call(
        following(functools.partial(local_inner_kernel, size=size, coef=coef, own=own, half=half), 5, after),
        grid=(pairs,),
        in_specs=[cols(own), cols(rows, pairs), cols(rows, 2 * pairs), fixed(own), whole(kx)] + untouched(after),
        out_specs=[cols(inner), pl.BlockSpec((16, inner), lambda p: (0, 0))],
        out_shape=[SDS((inner, width), bf16), SDS((16, inner), f32)],
        scratch_shapes=[pltpu.VMEM((blocks, span, 2 * LANES), bf16), pltpu.VMEM((blocks, span, LANES), bf16)],
        compiler_params=limits(60),
        cost_estimate=cost(12),
        name="local_inner",
    )(qkv, qkv, qkv, qx, kx, *after)


def local_edge(qkv, left, right, qx, kx, io, ilse, own, half, size, coef, after=()):
    rows, width = qkv.shape[0], qkv.shape[1] // 3
    pairs, inner, span = width // LANES, own - 2 * half, 2 * half + rows - own

    def cols(n, off=0):
        return pl.BlockSpec((n, LANES), lambda p: (0, p + off))

    def fixed(n):
        return pl.BlockSpec((n, LANES), lambda p: (0, 0))

    return pl.pallas_call(
        following(functools.partial(local_edge_kernel, size=size, coef=coef), 11, after),
        grid=(pairs,),
        in_specs=[cols(own), cols(rows, pairs), cols(rows, 2 * pairs), cols(half), cols(half, pairs), cols(half), cols(half, pairs), fixed(own), whole(kx), cols(inner), whole(ilse)] + untouched(after),
        out_specs=[cols(own), pl.BlockSpec((16, own), lambda p: (0, 0))],
        out_shape=[SDS((own, width), bf16), SDS((16, own), f32)],
        scratch_shapes=[pltpu.VMEM((2, span, 2 * LANES), bf16), pltpu.VMEM((2, span, LANES), bf16)],
        compiler_params=limits(60),
        cost_estimate=cost(12),
        name="local_edge",
    )(qkv, qkv, qkv, left, left, right, right, qx, kx, io, ilse, *after)


def to_thirds(lse):
    high = lse.astype(bf16).astype(f32)
    middle = (lse - high).astype(bf16).astype(f32)
    low = lse - high - middle
    lane = lax.broadcasted_iota(jnp.int32, lse.shape, 1)
    packed = jnp.where(lane < 16, high, jnp.where(lane < 32, pltpu.roll(middle, 16, 1), pltpu.roll(low, 32, 1)))
    return jnp.where(lane < 48, packed, 0.0).astype(bf16)


def from_thirds(packed):
    packed = packed.astype(f32)
    lane = lax.broadcasted_iota(jnp.int32, packed.shape, 1)
    total = packed + (pltpu.roll(packed, LANES - 16, 1) + pltpu.roll(packed, LANES - 32, 1))
    return jnp.where(lane < 16, total, 0.0)


def glob_kernel(q_ref, k_ref, v_ref, qx_ref, kx_ref, out_ref, ks, lse_ref, *, size, coef, half):
    step = pl.program_id(0)
    glob = q_ref.shape[0]
    own = k_ref.shape[0] - glob

    @pl.when(step == 0)
    def _():
        ks[:own, LANES:] = kx_ref[half : half + own, :]
        ks[own:, LANES:] = kx_ref[2 * half + own :, :]
        lse_ref[...] = jnp.zeros_like(lse_ref)

    ks[:, :LANES] = k_ref[...]
    ((o, lse),) = attend_pairs([(q_ref[...], qx_ref[...], ks[...], v_ref[...])], [lse_ref[...]], step, size, coef)
    lse_ref[...] = lse
    out_ref[:, pl.ds(pl.multiple_of(step * LANES, LANES), LANES)] = o

    @pl.when(step == pl.num_programs(0) - 1)
    def _():
        out_ref[:, out_ref.shape[1] - LANES :] = to_thirds(lse.T)


def glob_attention(qkv, qx, kx, own, half, size, coef):
    rows, width = qkv.shape[0], qkv.shape[1] // 3
    pairs, glob = width // LANES, rows - own
    at = own // glob

    def cols(off):
        return pl.BlockSpec((rows, LANES), lambda p: (0, p + off))

    return pl.pallas_call(
        functools.partial(glob_kernel, size=size, coef=coef, half=half),
        grid=(pairs,),
        in_specs=[pl.BlockSpec((glob, LANES), lambda p: (at, p)), cols(pairs), cols(2 * pairs), pl.BlockSpec((glob, LANES), lambda p: (at, 0)), whole(kx)],
        out_specs=pl.BlockSpec((glob, width + LANES), lambda p: (0, 0)),
        out_shape=SDS((glob, width + LANES), bf16),
        scratch_shapes=[pltpu.VMEM((rows, 2 * LANES), bf16), pltpu.VMEM((LANES, glob), f32)],
        compiler_params=limits(60),
        cost_estimate=cost(8),
        name="glob_attention",
    )(qkv, qkv, qkv, qx, kx)


def merge_kernel(upper_ref, own_ref, other_ref, out_ref, lse_ref, *, size):
    upper = upper_ref[0] == 1
    width = own_ref.shape[1] - LANES
    own_l, other_l = from_thirds(own_ref[:, width:]), from_thirds(other_ref[:, width:])
    first, second = jnp.where(upper, other_l, own_l), jnp.where(upper, own_l, other_l)
    top = jnp.maximum(first, second)
    wa, wb = jnp.exp2(first - top), jnp.exp2(second - top)
    total = wa + wb
    lse = top + jnp.log2(total)
    lane = lax.broadcasted_iota(jnp.int32, lse.shape, 1)
    lse = jnp.where(lane < 16, lse, 0.0)
    lse_ref[...] = lse
    out_ref[:, width:] = to_thirds(lse)
    wa, wb = wa / total, wb / total
    for p in range(width // LANES):
        at = slice(p * LANES, (p + 1) * LANES)
        own_o, other_o = own_ref[:, at].astype(f32), other_ref[:, at].astype(f32)
        a, b = jnp.where(upper, other_o, own_o), jnp.where(upper, own_o, other_o)
        ka = jnp.where(lane < size, wa[:, 2 * p : 2 * p + 1], wa[:, 2 * p + 1 : 2 * p + 2])
        kb = jnp.where(lane < size, wb[:, 2 * p : 2 * p + 1], wb[:, 2 * p + 1 : 2 * p + 2])
        out_ref[:, at] = (a * ka + b * kb).astype(bf16)


def merge_step(part, axis, bit, size, after=()):
    other = swapped(part, axis, bit)
    return pl.pallas_call(
        following(functools.partial(merge_kernel, size=size), 3, after),
        in_specs=[pl.BlockSpec(memory_space=pltpu.SMEM), whole(part), whole(part)] + untouched(after),
        out_specs=[whole(part), pl.BlockSpec((part.shape[0], LANES), lambda: (0, 0))],
        out_shape=[SDS(part.shape, bf16), SDS((part.shape[0], LANES), f32)],
        cost_estimate=cost(2),
        name="merge",
    )(side_of(axis, bit).reshape(1), part, other, *after)


def gathered(total, starts, chunk, shift=0):
    if chunk % 8 == 0:
        rows = [total[pl.ds(pl.multiple_of(start + shift, 8), chunk), :] for start in starts]
        return jnp.concatenate(rows, axis=0).astype(bf16)
    shape = (len(starts) * chunk, total.shape[0])
    place, row = lax.broadcasted_iota(jnp.int32, shape, 0), lax.broadcasted_iota(jnp.int32, shape, 1)
    wanted = place % chunk + shift
    for n, start in enumerate(starts):
        wanted = wanted + jnp.where(place // chunk == n, start, 0)
    return mm((wanted == row).astype(f32).astype(bf16), total[...].astype(bf16)).astype(bf16)


def split_rows(total, side, sent_ref, kept_ref, places):
    starts, chunk, apart = places
    sent_ref[...] = gathered(total, starts, chunk, (1 - side) * apart)
    kept_ref[...] = gathered(total, starts, chunk, side * apart)


def ffn_kernel(side_ref, flag_ref, att_ref, gatt_ref, tok_ref, glob_ref, wo_ref, up_ref, down_ref, vec_ref, bias_ref, br_tok_ref, br_glob_ref,
               out_tok_ref, out_glob_ref, mg_ref, hd_ref, wsent_ref, wkept_ref, dsent_ref, dkept_ref, vsum_ref, bsum_ref,
               att_s, n2s, n2t, br, act_s, hg_s, mixed_s, res_s, dn_s, sums_s, total, *, places, tall_places, pieces):
    step, last = pl.program_id(0), pl.num_programs(0) - 1
    own, width = tok_ref.shape
    rows = br.shape[0]
    flag = flag_ref[0]
    side = side_ref[0]
    size, steps = rows // pieces, act_s.shape[0]

    def at(n):
        return pl.ds(pl.multiple_of(n * size, size), size)

    def counted(x):
        return (x.astype(f32) * flag).astype(bf16)

    @pl.when(step == 0)
    def _():
        br[:own] = br_tok_ref[...]
        br[own:] = br_glob_ref[...]
        att_s[:own] = att_ref[...]
        att_s[own:] = gatt_ref[:, :width]
        mixed_s[:own] = tok_ref[...].astype(f32)
        mixed_s[own:] = glob_ref[...].astype(f32)

        def block(n, _):
            here = at(n)
            mixed = mixed_s[here, :] + mm(att_s[here, :], wo_ref[...])
            mixed_s[here, :] = mixed
            n2 = (normalize(mixed)[0] * vec_ref[2:3, :] + vec_ref[3:4, :]).astype(bf16)
            n2s[here, :] = n2
            res_s[here, :] = mixed + vec_ref[4:5, :]
            return 0

        lax.fori_loop(0, pieces, block, 0)
        n2t[:, :own] = n2s[:own, :].T
        n2t[:, own:] = counted(n2s[own:, :]).T
        dn_s[...] = jnp.zeros_like(dn_s)

    @pl.when((step >= steps) & (step < last))
    def _():
        slot = step - steps
        count = out_tok_ref.shape[0]
        out_tok_ref[...] = res_s[pl.ds(pl.multiple_of(slot * count, 16), count), :].astype(bf16)
        count = hd_ref.shape[0]
        here = pl.ds(pl.multiple_of(slot * count, 16), count)
        normalized, rstd = normalize(mixed_s[here, :])
        dn = dn_s[here, :]
        bf = br[here, :].astype(f32)
        ag = (bf + norm_back(normalized, rstd, vec_ref[2:3, :], dn)).astype(bf16)
        mg_ref[...] = ag
        hd_ref[...] = mm(ag, wo_ref[...], NT).astype(bf16)
        row = lax.broadcasted_iota(jnp.int32, (count, 1), 0) + slot * count
        keep = jnp.where(row < own, 1.0, flag)
        n2s[here, :] = (ag.astype(f32) * keep).astype(bf16)
        dn = dn * keep
        terms = [jnp.sum(term, axis=0, keepdims=True) for term in (dn * normalized, dn, bf * keep)]
        terms = jnp.concatenate(terms + [jnp.zeros((5, width), f32)], axis=0)
        sums_s[...] = terms + jnp.where(slot == 0, 0.0, sums_s[...])
        total[...] = mm(n2t[...], hg_s[slot])
        split_rows(total, side, wsent_ref, wkept_ref, places)
        hg = hg_s[slot].astype(f32)
        bsum_ref[...] = jnp.sum(hg[:own], axis=0, keepdims=True) + flag * jnp.sum(hg[own:], axis=0, keepdims=True)
        act_s[slot, own:, :] = counted(act_s[slot, own:, :])
        total[...] = mm(act_s[slot], br[...], TN)
        starts, rows_each = tall_places
        grad = gathered(total, starts, rows_each)
        part_rows = dsent_ref.shape[2]
        mine = slot % 2 == side
        for ref, wanted in ((dkept_ref, mine), (dsent_ref, jnp.logical_not(mine))):

            @pl.when(wanted)
            def _():
                for n in range(ref.shape[0]):
                    ref[n, 0] = grad[n * part_rows : (n + 1) * part_rows]

    @pl.when(step < steps)
    def _():
        slot = step

        def block(n, _):
            here = at(n)
            hidden = mm(n2s[here, :], up_ref[...]) + bias_ref[...]
            d_active = mm(br[here, :], down_ref[...], NT)
            active, slope = gelu_both(hidden)
            active = active.astype(bf16)
            hg = (d_active * slope).astype(bf16)
            act_s[slot, here, :] = active
            hg_s[slot, here, :] = hg
            res_s[here, :] += mm(active, down_ref[...])
            dn_s[here, :] += mm(hg, up_ref[...], NT)
            return 0

        lax.fori_loop(0, pieces, block, 0)

    @pl.when(step == last)
    def _():
        total[...] = mm(att_s[...], n2s[...], TN)
        split_rows(total, side, wsent_ref, wkept_ref, places)
        vsum_ref[...] = sums_s[...]
        out_glob_ref[...] = res_s[own:, :].astype(bf16)


def feed_forward(side, flag, att, gatt, tok, glob, wo, up, down, vec, bias, br_tok, br_glob, places, tall_places):
    own, width = tok.shape
    glob_rows = glob.shape[0]
    rows, units, chunk = own + glob_rows, up.shape[1], width
    steps = units // chunk
    pairs = lax.axis_size("batch") // 2
    assert steps == 2 * pairs

    def fixed(n):
        return pl.BlockSpec((n, width), lambda c: (0, 0))

    def once(array):
        return pl.BlockSpec(array.shape, lambda c: (0,) * array.ndim, pipeline_mode=pl.Buffered(1))

    def now(c):
        return jnp.minimum(c, steps - 1)

    def before(c):
        return jnp.clip(c - steps, 0, steps - 1)

    def by_part(n):
        assert n % (16 * steps) == 0
        return pl.BlockSpec((n // steps, width), lambda c: (before(c), 0))

    wide = pl.BlockSpec((width // 2, chunk), lambda c: (0, jnp.maximum(c - steps, 0)))
    parts = 2
    tall = pl.BlockSpec((parts, 1, chunk // parts, width), lambda c: (0, before(c) // 2, 0, 0))
    wide_shape = SDS((width // 2, units + width), bf16)
    tall_shape = SDS((parts, pairs, chunk // parts, width), bf16)
    smem = pl.BlockSpec(memory_space=pltpu.SMEM)
    low, full = pltpu.VMEM((rows, width), bf16), pltpu.VMEM((rows, width), f32)
    both = pltpu.VMEM((steps, rows, chunk), bf16)
    return pl.pallas_call(
        functools.partial(ffn_kernel, places=places, tall_places=tall_places, pieces=4),
        grid=(2 * steps + 1,),
        in_specs=[
            smem, smem, once(att), once(gatt), once(tok), once(glob), once(wo),
            pl.BlockSpec((width, chunk), lambda c: (0, now(c))), pl.BlockSpec((chunk, width), lambda c: (now(c), 0)), whole(vec),
            pl.BlockSpec((1, chunk), lambda c: (0, now(c))), once(br_tok), once(br_glob),
        ],
        out_specs=[
            by_part(own), fixed(glob_rows), by_part(rows), by_part(rows), wide, wide, tall, tall, fixed(8), pl.BlockSpec((1, chunk), lambda c: (0, before(c))),
        ],
        out_shape=[
            SDS((own, width), bf16), SDS((glob_rows, width), bf16), SDS((rows, width), bf16), SDS((rows, width), bf16),
            wide_shape, wide_shape, tall_shape, tall_shape, SDS((8, width), f32), SDS((1, units), f32),
        ],
        scratch_shapes=[low, low, pltpu.VMEM((width, rows), bf16), low, both, both, full, full, full, pltpu.VMEM((8, width), f32), pltpu.VMEM((width, width), f32)],
        compiler_params=limits(63),
        cost_estimate=cost(55),
        name="feed_forward",
    )(side, flag, att, gatt, tok, glob, wo, up, down, vec, bias, br_tok, br_glob)


def norm_rows(x_ref, gain, dn):
    normalized, rstd = normalize(x_ref[...].astype(f32))
    sums = [jnp.sum(dn * normalized, axis=0, keepdims=True), jnp.sum(dn, axis=0, keepdims=True)]
    return norm_back(normalized, rstd, gain, dn), jnp.concatenate(sums + [jnp.zeros((6, dn.shape[1]), f32)], axis=0)


def pair_backward(blocks, lse_rows, delta_rows, size, coef, scale):
    units = []
    for keys, values, tiles in blocks:
        for q, qx, do, at in tiles:
            for h in range(2):
                units.append((keys, values, head_part(q, h, size), qx, head_part(do, h, size), lse_rows[h][:, at], delta_rows[h][:, at]))
    scores = [mm(keys, jnp.concatenate([q, qx], axis=1), NT) for keys, _, q, qx, _, _, _ in units]
    dps = [mm(values, do, NT) for _, values, _, _, do, _, _ in units]
    weights = [jnp.exp2(s * coef - unit[5]) for s, unit in zip(scores, units)]
    dss = [(p * (dp - unit[6])).astype(bf16) for p, dp, unit in zip(weights, dps, units)]
    weights = [p.astype(bf16) for p in weights]
    results, first = [], 0
    for keys, _, tiles in blocks:
        here = range(first, first + 2 * len(tiles))
        first += 2 * len(tiles)
        keys_t = keys[:, :LANES].T
        dqs = []
        for n in here[::2]:
            parts = [mm(keys_t[h * size : (h + 1) * size], dss[n + h]) for h in range(2)]
            dqs.append((jnp.concatenate(parts, axis=0).T * scale).astype(bf16))
        dk = mm(jnp.concatenate([dss[n] for n in here], axis=1), jnp.concatenate([units[n][2] for n in here], axis=0)) * scale
        dv = mm(jnp.concatenate([weights[n] for n in here], axis=1), jnp.concatenate([units[n][4] for n in here], axis=0))
        results.append((dqs, dk, dv))
    return results


def inner_rows(o, do, size):
    prod = (o.astype(f32) * do.astype(f32)).T
    return [jnp.sum(prod[h * size : (h + 1) * size], axis=0, keepdims=True) for h in range(2)]


def edge_kernel(q_ref, k_ref, v_ref, lk_ref, lv_ref, rk_ref, rv_ref, qx_ref, kx_ref, o_ref, do_ref, lse_ref,
                dq_ref, dkv_ref, dg_ref, dl_ref, dr_ref, ks, vs, lses, *, size, coef, scale, own):
    step = pl.program_id(0)
    half = lk_ref.shape[0]
    glob = k_ref.shape[0] - own
    low = own - half

    @pl.when(step == 0)
    def _():
        fill_edge_masks(kx_ref, ks, own, half, glob)
        lses[:, :half] = lse_ref[:, :half]
        lses[:, half:] = lse_ref[:, low:]

    fill_edges(k_ref, lk_ref, rk_ref, ks, own, half)
    fill_edges(v_ref, lv_ref, rv_ref, vs, own, half)
    do = jnp.concatenate([do_ref[:half], do_ref[low:own]], axis=0)
    o = jnp.concatenate([o_ref[:half], o_ref[low:own]], axis=0)
    lse_rows = [lses[pl.ds(2 * step + h, 1), :] for h in range(2)]
    blocks = []
    for b, rows in enumerate((slice(0, half), slice(low, own))):
        there = slice(b * half, (b + 1) * half)
        blocks.append((ks[b], vs[b], [(q_ref[rows, :], qx_ref[rows, :], do[there], there)]))
    tails = []
    for b, (dqs, dk, dv) in enumerate(pair_backward(blocks, lse_rows, inner_rows(o, do, size), size, coef, scale)):
        there = slice(b * half, (b + 1) * half)
        dq_ref[there, :] = dqs[0]
        inside, outside = (slice(half, 2 * half), slice(0, half)) if b == 0 else (slice(0, half), slice(half, 2 * half))
        for n, part in enumerate((dk, dv)):
            dkv_ref[n, there, :] = part[inside]
            (dl_ref, dr_ref)[b][n] = part[outside].astype(bf16)
        tails.append((dk[2 * half :], dv[2 * half :]))
    for n in range(2):
        dg_ref[n] = tails[0][n] + tails[1][n]


def edge_backward(qkv, left, right, qx, kx, o, do, lse, own, size, coef, scale, after=()):
    rows, width = qkv.shape[0], qkv.shape[1] // 3
    pairs, half, glob = width // LANES, left.shape[0], rows - own

    def cols(n, off):
        return pl.BlockSpec((n, LANES), lambda p: (0, p + off))

    def both(n):
        return pl.BlockSpec((2, n, LANES), lambda p: (0, 0, p))

    fixed = pl.BlockSpec((own, LANES), lambda p: (0, 0))
    return pl.pallas_call(
        following(functools.partial(edge_kernel, size=size, coef=coef, scale=scale, own=own), 12, after),
        grid=(pairs,),
        in_specs=[
            cols(own, 0), cols(rows, pairs), cols(rows, 2 * pairs), cols(half, 0), cols(half, pairs), cols(half, 0), cols(half, pairs),
            fixed, whole(kx), cols(own, 0), cols(own, 0), whole(lse),
        ] + untouched(after),
        out_specs=[cols(2 * half, 0), both(2 * half), both(glob), both(half), both(half)],
        out_shape=[SDS((2 * half, width), bf16), SDS((2, 2 * half, width), f32), SDS((2, glob, width), f32)] + [SDS((2, half, width), bf16)] * 2,
        scratch_shapes=[
            pltpu.VMEM((2, 2 * half + glob, 2 * LANES), bf16), pltpu.VMEM((2, 2 * half + glob, LANES), bf16), pltpu.VMEM((16, 2 * half), f32),
        ],
        compiler_params=limits(60),
        cost_estimate=cost(17),
        name="edge_backward",
    )(qkv, qkv, qkv, left, left, right, right, qx, kx, o, do, lse, *after)


def inner_kernel(q_ref, k_ref, v_ref, qx_ref, kx_ref, o_ref, go_ref, do_ref, lse_ref, glse_ref, edq_ref, edkv_ref, edg_ref,
                 flag_ref, x_ref, vec_ref, mg_ref, wq_ref, wk_ref, wv_ref, dq_ref, dkv_ref, out_ref, sums_ref, ks, vs, lses, acc, dn_s, *, size, coef, scale, own, half):
    step = pl.program_id(0)
    rows = k_ref.shape[0]
    glob = rows - own
    blocks = ks.shape[0]

    @pl.when(step == 0)
    def _():
        fill_inner_masks(kx_ref, ks, own, half, glob)
        lses[:, :own] = lse_ref[...]
        lses[:, own:] = glse_ref[...].T[:16]

    fill_inner(k_ref, ks, own, half)
    fill_inner(v_ref, vs, own, half)
    o = jnp.concatenate([o_ref[...], go_ref[...]], axis=0)
    lse_rows = [lses[pl.ds(2 * step + h, 1), :] for h in range(2)]
    deltas = inner_rows(o, do_ref[...], size)
    kx_own = jnp.concatenate([kx_ref[half : half + own, :], kx_ref[2 * half + own :, :]], axis=0)

    def tile(at):
        return q_ref[at, :], qx_ref[at, :], do_ref[at, :], at

    every = [(jnp.concatenate([k_ref[...], kx_own], axis=1), v_ref[...], [tile(slice(own, rows))])]
    for b in range(blocks):
        low = half + b * 2 * half
        every.append((ks[b], vs[b], [tile(slice(low + j * half, low + (j + 1) * half)) for j in range(2)]))
    for b, (dqs, dk, dv) in enumerate(pair_backward(every, lse_rows, deltas, size, coef, scale)):
        for dq, (_, _, _, at) in zip(dqs, every[b][2]):
            dq_ref[at, :] = dq
        low = half + (b - 1) * 2 * half
        for n, part in enumerate((dk, dv)):
            if b == 0:
                acc[n] = part
            else:
                acc[n, low : low + 2 * half, :] += part[: 2 * half]
                acc[n, own:, :] += part[2 * half :]
    dq_ref[:half, :] = edq_ref[:half]
    dq_ref[own - half : own, :] = edq_ref[half:]
    for n in range(2):
        acc[n, :half, :] += edkv_ref[n, :half]
        acc[n, own - half : own, :] += edkv_ref[n, half:]
        acc[n, own:, :] += edg_ref[n]
    dkv_ref[...] = acc[...].astype(bf16)
    to_rows = mm(dq_ref[own:, :], wq_ref[...], NT) + mm(acc[0, own:, :].astype(bf16), wk_ref[...], NT) + mm(acc[1, own:, :].astype(bf16), wv_ref[...], NT)
    dn_s[...] = to_rows + jnp.where(step == 0, 0.0, dn_s[...])

    @pl.when(step == pl.num_programs(0) - 1)
    def _():
        back, sums = norm_rows(x_ref, vec_ref[0:1, :], dn_s[...])
        out_ref[...] = (mg_ref[...].astype(f32) * flag_ref[0] + back).astype(bf16)
        sums_ref[...] = sums


def inner_backward(qkv, qx, kx, o, go, do, lse, glse, edq, edkv, edg, flag, x, vec, mg, w, own, half, size, coef, scale, after=()):
    rows, width = qkv.shape[0], qkv.shape[1] // 3
    pairs, glob = width // LANES, rows - own
    blocks = own // (2 * half) - 1

    def cols(n, off=0):
        return pl.BlockSpec((n, LANES), lambda p: (0, p + off))

    def both(n):
        return pl.BlockSpec((2, n, LANES), lambda p: (0, 0, p))

    return pl.pallas_call(
        following(functools.partial(inner_kernel, size=size, coef=coef, scale=scale, own=own, half=half), 20, after),
        grid=(pairs,),
        in_specs=[
            cols(rows), cols(rows, pairs), cols(rows, 2 * pairs), whole(qx), whole(kx), cols(own), cols(glob), cols(rows), whole(lse), whole(glse),
            cols(2 * half), both(2 * half), both(glob), pl.BlockSpec(memory_space=pltpu.SMEM), whole(x), whole(vec),
            pl.BlockSpec((glob, width), lambda p: (own // glob, 0)), cols(width), cols(width, pairs), cols(width, 2 * pairs),
        ] + untouched(after),
        out_specs=[pl.BlockSpec((rows, LANES), lambda p: (0, p)), pl.BlockSpec((2, rows, LANES), lambda p: (0, 0, p)), whole(x), pl.BlockSpec((8, width), lambda p: (0, 0))],
        out_shape=[SDS((rows, width), bf16), SDS((2, rows, width), bf16), SDS(x.shape, bf16), SDS((8, width), f32)],
        scratch_shapes=[
            pltpu.VMEM((blocks, 2 * half + glob, 2 * LANES), bf16), pltpu.VMEM((blocks, 2 * half + glob, LANES), bf16),
            pltpu.VMEM((16, rows), f32), pltpu.VMEM((2, rows, LANES), f32), pltpu.VMEM((glob, width), f32),
        ],
        compiler_params=limits(60),
        cost_estimate=cost(13),
        name="inner_backward",
    )(qkv, qkv, qkv, qx, kx, o, go, do, lse, glse, edq, edkv, edg, flag, x, vec, mg, w, w, w, *after)


def weight_kernel(side_ref, nt_ref, ht_ref, dq_ref, dkv_ref, l_ref, r_ref, sent_ref, kept_ref, total, *, places):
    step = pl.program_id(0)

    @pl.when(step == 0)
    def _():
        total[...] = mm(nt_ref[...], dq_ref[...])

    @pl.when(step > 0)
    def _():
        total[...] = mm(nt_ref[...], dkv_ref[0]) + mm(ht_ref[...], jnp.concatenate([l_ref[0], r_ref[0]], axis=0))

    split_rows(total, side_ref[0], sent_ref, kept_ref, places)


def qkv_weight_grad(group, side, nt, ht, dq, dkv, dl, dr, places, after=()):
    width, rows = nt.shape
    cols, half = dq.shape[1], dl.shape[1]
    out = pl.BlockSpec((width // 2, cols), lambda c: (0, c))
    shape = SDS((width // 2, 3 * cols), bf16)
    halo = pl.BlockSpec((1, half, cols), lambda c: (jnp.maximum(c - 1, 0), 0, group))
    return pl.pallas_call(
        following(functools.partial(weight_kernel, places=places), 7, after),
        grid=(3,),
        in_specs=[
            pl.BlockSpec(memory_space=pltpu.SMEM), whole(nt), whole(ht), whole(dq),
            pl.BlockSpec((1, rows, cols), lambda c: (jnp.maximum(c - 1, 0), 0, 0)), halo, halo,
        ] + untouched(after),
        out_specs=[out, out],
        out_shape=[shape, shape],
        scratch_shapes=[pltpu.VMEM((width, cols), f32)],
        compiler_params=limits(60),
        cost_estimate=cost(0.1),
        name="qkv_weight_grad",
    )(side, nt, ht, dq, dkv, dl, dr, *after)


def halo_rows_kernel(lt_ref, rt_ref, vec_ref, w_ref, l_ref, r_ref, lout_ref, rout_ref, sums_ref):
    width = lt_ref.shape[1]
    sums = 0.0
    for x_ref, d_ref, out_ref in ((lt_ref, l_ref, lout_ref), (rt_ref, r_ref, rout_ref)):
        dn = mm(d_ref[0], w_ref[:, width : 2 * width], NT) + mm(d_ref[1], w_ref[:, 2 * width :], NT)
        back, part = norm_rows(x_ref, vec_ref[0:1, :], dn)
        out_ref[...] = back.astype(bf16)
        sums = sums + part
    sums_ref[...] = sums


def halo_rows(left, right, vec, w, dl, dr, after=()):
    args = (left, right, vec, w, dl, dr)
    half, width = left.shape
    return pl.pallas_call(
        following(halo_rows_kernel, len(args), after),
        in_specs=[whole(a) for a in args] + untouched(after),
        out_specs=[whole(left), whole(right), pl.BlockSpec((8, width), lambda: (0, 0))],
        out_shape=[SDS(left.shape, bf16), SDS(right.shape, bf16), SDS((8, width), f32)],
        compiler_params=limits(60),
        cost_estimate=cost(4),
        name="halo_rows",
    )(*args, *after)


def rows_kernel(flag_ref, x_ref, vec_ref, mg_ref, w_ref, *refs, groups, first, last):
    step = pl.program_id(0)
    assert groups == 1
    out_ref, sums_ref = refs[-2:]
    dq_ref, dkv_ref = refs[:2]
    dn = mm(jnp.concatenate([dq_ref[...], dkv_ref[0], dkv_ref[1]], axis=1), w_ref[...], NT)
    back, sums = norm_rows(x_ref, vec_ref[0:1, :], dn)
    out = mg_ref[...].astype(f32) * flag_ref[0] + back
    out_ref[...] = out.astype(out_ref.dtype)

    @pl.when(step == 0)
    def _():
        sums_ref[...] = sums

    @pl.when(step > 0)
    def _():
        sums_ref[...] += sums

    for ref, place in zip(refs[2:-2], (first, last)):
        if place is not None:

            @pl.when(step == place)
            def _():
                out_ref[...] = out + ref[...].astype(f32)


def row_grads(flag, x, vec, mg, w, parts, start, block, dtype, edges=(), after=(), share=(0, 1), into=None):
    count, width = x.shape
    groups = len(parts)
    cols = width // groups
    steps = count // block // share[1]
    ahead = share[0] * steps
    base = start // block + ahead
    after = ([] if into is None else [into]) + list(after)
    specs, args = [], []
    for dq, dkv in parts:
        specs += [pl.BlockSpec((block, cols), lambda r: (base + r, 0)), pl.BlockSpec((2, block, cols), lambda r: (0, base + r, 0))]
        args += [dq, dkv]
    here = pl.BlockSpec((block, width), lambda r: (ahead + r, 0))
    args = [flag, x, vec, mg, w] + args + list(edges)
    return pl.pallas_call(
        following(functools.partial(rows_kernel, groups=groups, first=0 if share[0] == 0 else None, last=steps - 1 if share[0] == share[1] - 1 else None), len(args), after),
        grid=(steps,),
        input_output_aliases={} if into is None else {len(args): 0},
        in_specs=[pl.BlockSpec(memory_space=pltpu.SMEM), here, whole(vec), pl.BlockSpec((block, width), lambda r: (base + r, 0)), whole(w)] + specs + [whole(e) for e in edges] + untouched(after),
        out_specs=[here, pl.BlockSpec((8, width), lambda r: (0, 0))],
        out_shape=[SDS(x.shape, dtype), SDS((8, width), f32)],
        compiler_params=limits(60),
        cost_estimate=cost(10 if edges else 0.1),
        name="row_grads",
    )(*args, *after)


def add_kernel(own_ref, other_ref, out_ref):
    out_ref[...] = (own_ref[...].astype(f32) + other_ref[...].astype(f32)).astype(out_ref.dtype)


def add_step(part, bit, dtype, after=()):
    return pl.pallas_call(
        following(add_kernel, 2, after),
        in_specs=[whole(part), whole(part)] + untouched(after),
        out_specs=whole(part),
        out_shape=SDS(part.shape, dtype),
        cost_estimate=cost(1),
        name="add_step",
    )(part, swapped(part, *bit), *after)


def as_column(row):
    n = row.shape[1]
    eye = lax.broadcasted_iota(jnp.int32, (n, n), 0) == lax.broadcasted_iota(jnp.int32, (n, n), 1)
    return jnp.sum(jnp.where(eye, row, 0.0), axis=1, keepdims=True)


def split_shards(qkv_ref, rest_ref, units, width):
    groups = (rest_ref.shape[1] - units - width) // width
    starts = [units + width * (k + 1) for k in range(groups)]
    return qkv_ref[...], rest_ref[:, units : units + width], rest_ref[:, :units], [rest_ref[:, at : at + width] for at in starts]


def pack_kernel(qkv_ref, rest_ref, rq_ref, ro_ref, ru_ref, rd_ref, vone_ref, vtwo_ref, bias_ref,
                stats_ref, gout_ref, gup_ref, gdown_ref, nq_ref, no_ref, nu_ref, nd_ref, cq_ref, co_ref, cu_ref, cd_ref, *, decay):
    units, width = bias_ref.shape[1], vone_ref.shape[1]
    g_qkv, g_out, g_up, g_down = split_shards(qkv_ref, rest_ref, units, width)
    rows = g_qkv.shape[0]
    gout_ref[...], gup_ref[...] = g_out, g_up
    at, totals = 0, []
    for g, old_ref, new_ref, col_ref in ((g_qkv, rq_ref, nq_ref, cq_ref), (g_out, ro_ref, no_ref, co_ref), (g_up, ru_ref, nu_ref, cu_ref), (g_down, rd_ref, nd_ref, cd_ref)):
        groups = g if isinstance(g, list) else [g]
        columns, total, means = 0.0, 0.0, []
        for k, part in enumerate(groups):
            square = part * part + TINY_SQUARE
            columns = columns + jnp.sum(square, axis=0, keepdims=True)
            means.append(jnp.mean(square, axis=1, keepdims=True))
            if len(groups) > 1:
                gdown_ref[k * rows : (k + 1) * rows, :] = part
        mean = means[0] if len(means) == 1 else jnp.concatenate(means, axis=0)
        new = decay * as_column(old_ref[...].reshape(1, -1)) + (1.0 - decay) * mean
        col_ref[...] = new
        new_ref[...] = jnp.sum(jnp.where(lax.broadcasted_iota(jnp.int32, (new.shape[0],) * 2, 0) == lax.broadcasted_iota(jnp.int32, (new.shape[0],) * 2, 1), new, 0.0), axis=0)
        totals.append(jnp.sum(new, axis=0, keepdims=True))
        stats_ref[:, at : at + columns.shape[1]] = columns
        at += columns.shape[1]
    for ref, count in ((vone_ref, 2), (vtwo_ref, 3)):
        for n in range(count):
            stats_ref[:, at : at + width] = ref[n : n + 1, :]
            at += width
    stats_ref[:, at : at + units] = bias_ref[...]
    at += units
    lane = lax.broadcasted_iota(jnp.int32, (1, LANES), 1)
    last = jnp.zeros((1, LANES), f32)
    for n, total in enumerate(totals):
        last = jnp.where(lane == n, total, last)
    stats_ref[:, at : at + LANES] = last


def pack(qkv, rest, row_olds, vec_one, vec_two, bias, decay):
    units, width, rows = bias.shape[1], vec_one.shape[1], qkv.shape[0]
    tall = rest.shape[1] // width - units // width - 1
    count = qkv.shape[1] + width + units + width + 5 * width + units + LANES
    shapes = [(1, count), (rows, width), (rows, units), (tall * rows, width)]
    shapes += [old.shape for old in row_olds] + [(old.shape[0], 1) for old in row_olds]
    args = (qkv, rest, *row_olds, vec_one, vec_two, bias)
    return pl.pallas_call(
        functools.partial(pack_kernel, decay=decay),
        out_shape=[SDS(shape, f32) for shape in shapes],
        compiler_params=limits(60),
        cost_estimate=cost(3),
        name="pack",
    )(*args)


def update_kernel(stats_ref, qkv_ref, rest_ref, rq_ref, ro_ref, ru_ref, rd_ref, mq_ref, mo_ref, mu_ref, md_ref, oq_ref, oo_ref, ou_ref, od_ref,
                  vec_ref, vstate_ref, bias_ref, bstate_ref,
                  nq_ref, no_ref, nu_ref, nd_ref, cq_ref, co_ref, cu_ref, cd_ref, vg_ref, vs_ref, vn_ref, bg_ref, bs_ref, bn_ref, *, decay, full_rows):
    width, units = vec_ref.shape[1], bias_ref.shape[0]
    shards = split_shards(qkv_ref, rest_ref, units, width)
    rows = qkv_ref.shape[0]
    stats = stats_ref[...]
    totals = stats[:, stats.shape[1] - LANES :]
    at = 0
    sets = zip(shards, (rq_ref, ro_ref, ru_ref, rd_ref), (mq_ref, mo_ref, mu_ref, md_ref), (oq_ref, oo_ref, ou_ref, od_ref), (nq_ref, no_ref, nu_ref, nd_ref), (cq_ref, co_ref, cu_ref, cd_ref), full_rows)
    for n, (shard, row_ref, master_ref, old_ref, new_ref, col_ref, count) in enumerate(sets):
        columns = old_ref.shape[0]
        col = decay * old_ref[...].reshape(1, columns) + (1.0 - decay) * (stats[:, at : at + columns] / count)
        at += columns
        col_ref[...] = col[0]
        row_mean = totals[:, n : n + 1] / count
        parts = shard if isinstance(shard, list) else [shard]
        master = master_ref[...].astype(f32)
        for k, part in enumerate(parts):
            here = slice(k * rows, (k + 1) * rows)
            estimate = row_ref[here, :] * col / row_mean
            new_ref[here, :] = master[here] - RATE_MATRIX * part * lax.rsqrt(estimate)
    grad = jnp.concatenate([stats[:, at + n * width : at + (n + 1) * width] for n in range(5)], axis=0)
    at += 5 * width
    vg_ref[...] = grad
    state = decay * vstate_ref[...] + (1.0 - decay) * (grad * grad + TINY_SQUARE)
    vs_ref[...] = state
    vn_ref[...] = vec_ref[...] - RATE_VECTOR * grad * lax.rsqrt(state)
    grad = stats[:, at : at + units]
    bg_ref[...] = grad[0]
    state = decay * bstate_ref[...].reshape(1, units) + (1.0 - decay) * (grad * grad + TINY_SQUARE)
    bs_ref[...] = state[0]
    bn_ref[...] = (bias_ref[...].reshape(1, units) - RATE_VECTOR * grad * lax.rsqrt(state))[0]


def update(stats, qkv, rest, row_columns, masters, col_olds, vec, vec_state, bias, bias_state, decay, full_rows):
    args = (stats, qkv, rest, *row_columns, *masters, *col_olds, vec, vec_state, bias, bias_state)
    shapes = [m.shape for m in masters] + [c.shape for c in col_olds] + [vec.shape] * 3 + [bias.shape] * 3
    return pl.pallas_call(
        functools.partial(update_kernel, decay=decay, full_rows=full_rows),
        out_shape=[SDS(shape, f32) for shape in shapes],
        compiler_params=limits(60),
        cost_estimate=cost(3),
        name="update",
    )(*args)


def mask_kernel(info_ref, seg_ref, ok_ref, qx_ref, kx_ref, *, half, glob):
    lead, total = half // LANES, seg_ref.shape[1] // LANES
    own = qx_ref.shape[0] - glob
    lane = lax.broadcasted_iota(jnp.int32, (LANES, LANES), 1).astype(f32)
    for n in range(own // LANES + 2 * lead):
        block = info_ref[0] - lead + n
        at = pl.ds(pl.multiple_of(jnp.clip(block, 0, total - 1) * LANES, LANES), LANES)
        code = (seg_ref[:, at] + jnp.where(ok_ref[:, at] > 0, 8, 0)).astype(f32)
        code = jnp.broadcast_to(code, (LANES, LANES)).T
        valid = (code >= 8.0) & (block >= 0) & (block < total)
        document = jnp.where(code >= 8.0, code - 8.0, code) == lane
        seen = ((document | (lane == 4.0)) & valid) | (lane > 4.0)
        kx_ref[n * LANES : (n + 1) * LANES, :] = jnp.where(seen, 0.0, NEG_FILL).astype(bf16)
        if lead <= n < lead + own // LANES:
            qx_ref[(n - lead) * LANES : (n - lead + 1) * LANES, :] = jnp.where(document, 1.0, 0.0).astype(bf16)
    lane = lax.broadcasted_iota(jnp.int32, (glob, LANES), 1)
    kx_ref[own + 2 * half :, :] = jnp.where((lane == 4) & (info_ref[1] == 0), NEG_FILL, 0.0).astype(bf16)
    qx_ref[own:, :] = jnp.where(lane == 4, 1.0, 0.0).astype(bf16)


def mask_lanes(segments, valid, start, own, half, glob, first):
    info = jnp.stack([start // LANES, first.astype(jnp.int32)])
    return pl.pallas_call(
        functools.partial(mask_kernel, half=half, glob=glob),
        in_specs=[pl.BlockSpec(memory_space=pltpu.SMEM), whole(segments), whole(valid)],
        out_specs=[pl.BlockSpec((own + glob, LANES), lambda: (0, 0)), pl.BlockSpec((own + 2 * half + glob, LANES), lambda: (0, 0))],
        out_shape=[SDS((own + glob, LANES), bf16), SDS((own + 2 * half + glob, LANES), bf16)],
        compiler_params=limits(60),
        cost_estimate=cost(2),
        name="mask_lanes",
    )(info, segments, valid)


def body(
    tokens,
    glob_tokens,
    w_qkv,
    w_out,
    w_up,
    w_down,
    vec_params,
    hidden_bias,
    row_qkv,
    col_qkv,
    row_out,
    col_out,
    row_up,
    col_up,
    row_down,
    col_down,
    vec_state,
    bias_state,
    segments,
    valid_mask,
    out_cotangent,
    glob_cotangent,
):
    width = w_out.shape[0]
    size = width // HEADS
    assert 2 * size == LANES
    scale = size ** (-0.5)
    coef = scale * LOG2E
    half = BLOCK // 2
    tok, glob = tokens[0], glob_tokens[0]
    own, globs = tok.shape[0], glob.shape[0]
    seq_index = lax.axis_index("seq")
    first = seq_index == 0
    flag = first.astype(f32).reshape(1)
    bias_row = hidden_bias[None, :]
    batch_bits, seq_bits = bits_of("batch"), bits_of("seq")

    low, high = [batch_bits[:1]], [[bit] for bit in batch_bits[1:]]
    far = [seq_bits[1:][n : n + 2] for n in range(0, len(seq_bits) - 1, 2)]
    wide_stages = low + high + [seq_bits[:1]]
    tall_stages = low + [seq_bits[:1]] + high
    joint_stages = [[bit] for bit in seq_bits[1:]]
    pair_stages = low + [batch_bits[1:] + seq_bits[:1]] + far
    places = row_places(width, pair_stages)
    sequence = np.arange(1 << len(seq_bits)).reshape([2] * len(seq_bits)).transpose(
        [seq_bits[::-1].index(bit) for bit in seq_bits]
    ).reshape(-1)
    tall_chunk = w_down.shape[0] // lax.axis_size("batch") // sequence.size
    tall_places = tuple(int(n) * tall_chunk for n in sequence), tall_chunk
    halo_left, halo_right = shifted(tok[own - half :], "seq", 1), shifted(tok[:half], "seq", -1)
    qx, kx = mask_lanes(segments, valid_mask, seq_index * own, own, half, globs, first)
    qkv, normed_t = project(tok, glob, w_qkv, vec_params)
    part = glob_attention(qkv, qx, kx, own, half, size, coef)
    left, right, halo_t = project_halos(halo_left, halo_right, w_qkv, vec_params)
    part, glob_lse = merge_step(part, *seq_bits[0], size, after=[left])
    inner_att, inner_lse = local_inner(qkv, qx, kx, own, half, size, coef, after=[part])
    for bit in seq_bits[1:-1]:
        part, glob_lse = merge_step(part, *bit, size, after=[inner_lse])
    att, lse = local_edge(qkv, left, right, qx, kx, inner_att, inner_lse, own, half, size, coef, after=[part])
    part, glob_lse = merge_step(part, *seq_bits[-1], size, after=[lse])
    side = side_of(*batch_bits[0]).reshape(1)
    out_tok, out_glob, mixed_grad, heads_grad, *matrices, vec_two, bias_sum = feed_forward(
        side, flag, att, part, tok, glob, w_out, w_up, w_down, vec_params, bias_row, out_cotangent[0], glob_cotangent[0], places, tall_places
    )
    wide, down = Scatter(*matrices[:2], wide_stages), Scatter(*matrices[2:], tall_stages)
    edge = edge_backward(qkv, left, right, qx, kx, att, heads_grad, lse, own, size, coef, scale, after=wide.parts + down.parts)
    grad_left, grad_right = edge[3:]
    down.step(after=edge[:1])
    wide.step(after=down.parts)
    to_left, to_right, halo_sums = halo_rows(halo_left, halo_right, vec_params, w_qkv, grad_left, grad_right, after=wide.parts)
    edges = (shifted(to_right, "seq", 1), shifted(to_left, "seq", -1))
    dq, dkv, glob_part, glob_sums = inner_backward(
        qkv, qx, kx, att, part, heads_grad, lse, glob_lse, *edge[:3], flag, glob, vec_params, mixed_grad, w_qkv, own, half, size, coef, scale,
        after=[to_left, to_right],
    )
    parts = [(dq, dkv)]
    down.step(after=[parts[0][0]], us=0.01)
    wide.step(after=[*down.parts, *edges], us=0.01)
    weight = Scatter(*qkv_weight_grad(0, side, normed_t, halo_t, dq, dkv, grad_left, grad_right, places, after=wide.parts), pair_stages)
    glob_bits = seq_bits[1:] + seq_bits[:1]
    glob_part = add_step(glob_part, glob_bits[0], bf16, after=weight.parts)
    joint = joint_scatter(wide, down, joint_stages, after=[glob_part])
    weight.step(after=joint.parts)
    for bit in glob_bits[1:-1]:
        glob_part = add_step(glob_part, bit, bf16, after=weight.parts)
    ones = jnp.ones((1,), f32)
    row_args = (vec_params, mixed_grad, w_qkv, parts, 0, half, f32)
    tokens_grad, one_sums = row_grads(ones, tok, *row_args, edges=edges, after=[glob_part], share=(0, 2))
    joint.step(after=[one_sums])
    tokens_grad, two_sums = row_grads(ones, tok, *row_args, edges=edges, after=joint.parts, share=(1, 2), into=tokens_grad)
    tok_sums = one_sums + two_sums
    weight.step(after=[two_sums])
    glob_part = add_step(glob_part, glob_bits[-1], f32, after=weight.parts)
    while joint.stages:
        rest = joint.step(after=[glob_part])
    while weight.stages:
        shard_qkv = weight.step(after=[rest])
    decay = 1.0 - STEP ** (-0.8)
    units = w_up.shape[1]
    owner = lax.axis_index(("batch", "seq"))
    masters = []
    for matrix in (w_qkv, w_out, w_up, w_down):
        rows = matrix.shape[0] // lax.axis_size(("batch", "seq"))
        masters.append(lax.dynamic_slice_in_dim(matrix, owner * rows, rows, 0))
    stats, grad_out, grad_up, grad_down, *rows_new = pack(
        shard_qkv, rest, (row_qkv, row_out, row_up, row_down), halo_sums + glob_sums + tok_sums, vec_two, bias_sum, decay
    )
    every = batch_bits + seq_bits
    for bits in [every[n : n + 2] for n in range(0, len(every), 2)]:
        terms = [stats] + [flipped(stats, bits, n) for n in range(1, 1 << len(bits))]
        while len(terms) > 1:
            terms = [a + b for a, b in zip(terms[::2], terms[1::2])]
        stats = terms[0]
    new_qkv, new_out, new_up, new_down, col_qkv_new, col_out_new, col_up_new, col_down_new, *vectors = update(
        stats, shard_qkv, rest, rows_new[4:], masters, (col_qkv, col_out, col_up, col_down), vec_params, vec_state, hidden_bias, bias_state,
        decay, (w_qkv.shape[0], w_out.shape[0], w_up.shape[0], w_down.shape[0]),
    )
    return (
        out_tok[None],
        out_glob[None],
        tokens_grad[None],
        glob_part[None],
        shard_qkv,
        rows_new[0],
        col_qkv_new,
        new_qkv,
        grad_out,
        rows_new[1],
        col_out_new,
        new_out,
        grad_up,
        rows_new[2],
        col_up_new,
        new_up,
        grad_down,
        rows_new[3],
        col_down_new,
        new_down,
        *vectors,
    )


def solution(mesh):
    in_specs = (
        P("batch", "seq", None),
        P("batch", None, None),
        P(),
        P(),
        P(),
        P(),
        P(),
        P(),
        P(("batch", "seq")),
        P(),
        P(("batch", "seq")),
        P(),
        P(("batch", "seq")),
        P(),
        P(("batch", "seq")),
        P(),
        P(),
        P(),
        P("batch", None),
        P("batch", None),
        P("batch", "seq", None),
        P("batch", None, None),
    )
    out_specs = (
        P("batch", "seq", None),
        P("batch", None, None),
        P("batch", "seq", None),
        P("batch", None, None),
        P(("batch", "seq"), None),
        P(("batch", "seq")),
        P(),
        P(("batch", "seq"), None),
        P(("batch", "seq"), None),
        P(("batch", "seq")),
        P(),
        P(("batch", "seq"), None),
        P(("batch", "seq"), None),
        P(("batch", "seq")),
        P(),
        P(("batch", "seq"), None),
        P(("batch", "seq"), None),
        P(("batch", "seq")),
        P(),
        P(("batch", "seq"), None),
        P(),
        P(),
        P(),
        P(),
        P(),
        P(),
    )
    return jax.shard_map(body, mesh=mesh, in_specs=in_specs, out_specs=out_specs, check_vma=False)
```

```python
import functools

import jax
import jax.numpy as jnp
import numpy as np
from jax import lax
from jax.experimental import pallas as pl
from jax.experimental.pallas import tpu as pltpu
from jax.sharding import PartitionSpec as P

HEADS = 12
BLOCK = 512
STEP = 10

NEG_FILL = -8e9
NORM_EPS = 1e-06
TINY_SQUARE = 1e-30
RATE_MATRIX = 0.03
RATE_VECTOR = 0.2
LANES = 128
LOG2E = 1.4426950408889634

f32, bf16 = jnp.float32, jnp.bfloat16
NN = (((1,), (0,)), ((), ()))
NT = (((1,), (1,)), ((), ()))
TN = (((0,), (0,)), ((), ()))
SDS = jax.ShapeDtypeStruct


def bits_of(axis):
    size = lax.axis_size(axis)
    assert size & (size - 1) == 0
    return [(axis, 1 << k) for k in range(size.bit_length() - 1)]


def side_of(axis, bit):
    return (lax.axis_index(axis) // bit) % 2


def swapped(values, axis, bit):
    return lax.ppermute(values, axis, [(i, i ^ bit) for i in range(lax.axis_size(axis))])


def shifted(values, axis, distance):
    devices = range(lax.axis_size(axis))
    return lax.ppermute(values, axis, [(i, i + distance) for i in devices if i + distance in devices])


def summed(parts, bits):
    leaves, tree = jax.tree.flatten(parts)
    flat = jnp.concatenate([leaf.reshape(-1) for leaf in leaves])
    count = flat.shape[0]
    flat = jnp.pad(flat, (0, -count % 1024)).reshape(-1, LANES)
    for axis, bit in bits:
        flat = flat + swapped(flat, axis, bit)
    flat = flat.reshape(-1)
    out, place = [], 0
    for leaf in leaves:
        out.append(flat[place : place + leaf.size].reshape(leaf.shape))
        place += leaf.size
    return jax.tree.unflatten(tree, out)


def flipped(values, bits, flips):
    sizes = {axis: lax.axis_size(axis) for axis in ("batch", "seq")}
    change = {axis: sum(bit for n, (name, bit) in enumerate(bits) if name == axis and flips >> n & 1) for axis in sizes}
    route = [
        (b * sizes["seq"] + s, (b ^ change["batch"]) * sizes["seq"] + (s ^ change["seq"]))
        for b in range(sizes["batch"])
        for s in range(sizes["seq"])
    ]
    return lax.ppermute(values, ("batch", "seq"), route)


def mm(a, b, dims=NN):
    return lax.dot_general(a, b, dims, preferred_element_type=f32)


def limits(mib):
    return pltpu.CompilerParams(vmem_limit_bytes=mib * 2**20)


def cost(us):
    return pl.CostEstimate(flops=int(us * 1.15e9), bytes_accessed=1 << 20, transcendentals=0)


def whole(array):
    return pl.BlockSpec(array.shape, lambda *_: (0,) * array.ndim)


def following(kernel, inputs, after):
    return lambda *refs: kernel(*refs[:inputs], *refs[inputs + len(after) :])


def untouched(after):
    return [pl.BlockSpec(memory_space=pl.ANY)] * len(after)


def normalize(x):
    mean = jnp.mean(x, axis=1, keepdims=True)
    centred = x - mean
    rstd = lax.rsqrt(jnp.mean(centred * centred, axis=1, keepdims=True) + NORM_EPS)
    return centred * rstd, rstd


def norm_back(normalized, rstd, gain, grad):
    g = grad * gain
    inner = jnp.mean(g * normalized, axis=1, keepdims=True)
    return rstd * (g - jnp.mean(g, axis=1, keepdims=True) - normalized * inner)


def gelu_both(u):
    phi = 0.5 + 0.5 * lax.erf(u * 0.7071067811865476)
    density = jnp.exp2(u * u * (-0.5 * LOG2E)) * 0.3989422804014327
    return u * phi, phi + u * density


def head_part(values, head, size):
    lanes = lax.broadcasted_iota(jnp.int32, values.shape, 1)
    return jnp.where((lanes // size) == head, values, jnp.zeros_like(values))


def stage_kernel(side_ref, kept_ref, *refs, arrived, parts):
    for n in range(parts):
        at = side_ref[0] ^ n if parts > 1 else 0
        total = kept_ref[at].astype(f32)
        for ref in refs[:arrived]:
            total = total + ref[at].astype(f32)
        out = refs[arrived + n]
        out[...] = total.astype(out.dtype)


class Scatter:
    def __init__(self, sent, kept, stages):
        self.stages, self.parts, self.kept = list(stages), [sent], kept

    def step(self, after=(), us=2):
        bits = self.stages.pop(0)
        arrived = [flipped(part, bits[::-1], n + 1) for n, part in enumerate(self.parts)]
        bits = self.stages[0] if self.stages else []
        parts, columns = 1 << len(bits), self.kept.shape[-1]
        rows = self.kept.size // columns // parts
        block = columns if self.kept.size < 1 << 20 else columns // 3 if columns % 1152 == 0 or columns % 3840 == 0 else columns
        tall = 3 if columns == block and rows % 32 == 0 and self.kept.size > 1 << 19 else 1
        args = [a.reshape(parts, rows, columns) for a in [self.kept] + arrived]
        side = sum(side_of(*bit) << n for n, bit in enumerate(reversed(bits))) if bits else jnp.int32(0)
        spec = pl.BlockSpec((parts, rows // tall, block), lambda c, r: (0, r, c))
        out = pl.BlockSpec((rows // tall, block), lambda c, r: (r, c))
        after = list(after)
        self.kept, *self.parts = pl.pallas_call(
            following(functools.partial(stage_kernel, arrived=len(arrived), parts=parts), 1 + len(args), after),
            grid=(columns // block, tall),
            in_specs=[pl.BlockSpec(memory_space=pltpu.SMEM)] + [spec] * len(args) + untouched(after),
            out_specs=[out] * parts,
            out_shape=[SDS((rows, columns), bf16 if bits else f32)] + [SDS((rows, columns), bf16)] * (parts - 1),
            compiler_params=limits(24),
            cost_estimate=cost(us),
            name="sum_stage",
        )(side.reshape(1), *args, *after)
        return self.kept


def joint_kernel(side_ref, wk_ref, wa_ref, dk_ref, da_ref, sent_ref, kept_ref, total, *, chunk, starts):
    columns = wk_ref.shape[2]
    block = dk_ref.shape[2]
    for ref, flip in ((sent_ref, 1), (kept_ref, 0)):
        at = side_ref[0] ^ flip
        ref[:, :columns] = (wk_ref[at].astype(f32) + wa_ref[at].astype(f32)).astype(bf16)
        total[...] = dk_ref[at].astype(f32) + da_ref[at].astype(f32)
        for k, places in enumerate(starts):
            ref[:, columns + k * block : columns + (k + 1) * block] = gathered(total, places, chunk)


def joint_scatter(wide, down, stages, after=()):
    (bit,) = stages[0]
    args = []
    for scatter in (wide, down):
        bits = scatter.stages.pop(0)
        arrived = flipped(scatter.parts[0], bits, 1)
        args += [a.reshape(2, -1, a.shape[-1]) for a in (scatter.kept, arrived)]
    _, rows, columns = args[0].shape
    _, rows_down, block = args[2].shape
    owners = 1 << (len(stages) - 1)
    chunk = rows // owners
    groups = rows_down // rows
    starts = [[(n * groups + k) * chunk for n in range(owners)] for k in range(groups)]
    shape = SDS((rows, columns + groups * block), bf16)
    after = list(after)
    sent, kept = pl.pallas_call(
        following(functools.partial(joint_kernel, chunk=chunk, starts=starts), 5, after),
        in_specs=[pl.BlockSpec(memory_space=pltpu.SMEM)] + [whole(a) for a in args] + untouched(after),
        out_specs=[pl.BlockSpec(shape.shape, lambda: (0, 0))] * 2,
        out_shape=[shape, shape],
        scratch_shapes=[pltpu.VMEM((rows_down, block), f32)],
        compiler_params=limits(24),
        cost_estimate=cost(100),
        name="joint_stage",
    )(side_of(*bit).reshape(1), *args, *after)
    return Scatter(sent, kept, stages)


def row_places(width, stages):
    labels = bits_of("batch")[::-1] + bits_of("seq")[::-1]
    owners = np.arange(1 << len(labels)).reshape([2] * len(labels))
    owners = owners.transpose([labels.index(bit) for stage in stages for bit in stage]).reshape(2, -1)
    chunk = width // owners.size
    return tuple(int(owner) * chunk for owner in owners[0]), chunk, int(owners[1, 0] - owners[0, 0]) * chunk


def project_kernel(tok_ref, glob_ref, w_ref, vec_ref, qkv_ref, nt_ref, n_s):
    own = tok_ref.shape[0]

    @pl.when(pl.program_id(0) == 0)
    def _():
        for ref, rows in ((tok_ref, slice(0, own)), (glob_ref, slice(own, n_s.shape[0]))):
            n = normalize(ref[...].astype(f32))[0] * vec_ref[0:1, :] + vec_ref[1:2, :]
            n = n.astype(bf16)
            n_s[rows, :] = n
            nt_ref[:, rows] = n.T

    qkv_ref[...] = mm(n_s[...], w_ref[...]).astype(bf16)


def project(tok, glob, w, vec):
    width = tok.shape[1]
    rows = tok.shape[0] + glob.shape[0]
    return pl.pallas_call(
        project_kernel,
        grid=(w.shape[1] // width,),
        in_specs=[whole(tok), whole(glob), pl.BlockSpec((width, width), lambda c: (0, c)), whole(vec)],
        out_specs=[
            pl.BlockSpec((rows, width), lambda c: (0, c)),
            pl.BlockSpec((width, rows), lambda c: (0, 0)),
        ],
        out_shape=[SDS((rows, w.shape[1]), bf16), SDS((width, rows), bf16)],
        scratch_shapes=[pltpu.VMEM((rows, width), bf16)],
        compiler_params=limits(60),
        cost_estimate=cost(9),
        name="project",
    )(tok, glob, w, vec)


def halo_kernel(l_ref, r_ref, w_ref, vec_ref, lkv_ref, rkv_ref, nt_ref):
    half = l_ref.shape[0]
    for ref, out, at in ((l_ref, lkv_ref, 0), (r_ref, rkv_ref, half)):
        n = normalize(ref[...].astype(f32))[0] * vec_ref[0:1, :] + vec_ref[1:2, :]
        n = n.astype(bf16)
        nt_ref[:, at : at + half] = n.T
        out[...] = mm(n, w_ref[...]).astype(bf16)


def project_halos(left, right, w, vec):
    half, width = left.shape
    kv = pl.BlockSpec((half, width), lambda c: (0, c))
    return pl.pallas_call(
        halo_kernel,
        grid=(2,),
        in_specs=[whole(left), whole(right), pl.BlockSpec((width, width), lambda c: (0, c + 1)), whole(vec)],
        out_specs=[kv, kv, pl.BlockSpec((width, 2 * half), lambda c: (0, 0))],
        out_shape=[SDS((half, 2 * width), bf16)] * 2 + [SDS((width, 2 * half), bf16)],
        compiler_params=limits(60),
        cost_estimate=cost(3),
        name="project_halos",
    )(left, right, w, vec)


def attend_pairs(tiles, lse_rows, step, size, coef):
    scores = []
    for q, qx, keys, _ in tiles:
        for h in range(2):
            scores.append(mm(keys, jnp.concatenate([head_part(q, h, size), qx], axis=1), NT))
    tops = [jnp.max(s, axis=0, keepdims=True) * coef for s in scores]
    weights = [jnp.exp2(s * coef - top) for s, top in zip(scores, tops)]
    totals = [jnp.sum(p, axis=0, keepdims=True) for p in weights]
    outs = []
    for n, p in enumerate(weights):
        h = n % 2
        values_t = tiles[n // 2][3].T[h * size : (h + 1) * size]
        outs.append(mm(values_t, p.astype(bf16)) * (1.0 / totals[n]))
    results = []
    for n, lse in enumerate(lse_rows):
        row = lax.broadcasted_iota(jnp.int32, lse.shape, 0)
        for h in range(2):
            lse = jnp.where(row == 2 * step + h, tops[2 * n + h] + jnp.log2(totals[2 * n + h]), lse)
        results.append((jnp.concatenate(outs[2 * n : 2 * n + 2], axis=0).T.astype(bf16), lse))
    return results


def mask_piece(kx_ref, name, low, rows, own, half):
    if name == "l":
        start = low
    elif name == "r":
        start = half + own + low
    else:
        start = half + low if low < own else 2 * half + low
    return kx_ref[start : start + rows, :]


def fill_inner(src, dst, own, half):
    for b in range(dst.shape[0]):
        low = half + b * 2 * half
        dst[b, : 2 * half, :LANES] = src[low : low + 2 * half]
        dst[b, 2 * half :, :LANES] = src[own:]


def fill_inner_masks(kx_ref, dst, own, half, glob):
    for b in range(dst.shape[0]):
        dst[b, : 2 * half, LANES:] = mask_piece(kx_ref, "o", half + b * 2 * half, 2 * half, own, half)
        dst[b, 2 * half :, LANES:] = mask_piece(kx_ref, "o", own, glob, own, half)


def fill_edges(src, l_ref, r_ref, dst, own, half):
    dst[0, :half, :LANES] = l_ref[...]
    dst[0, half : 2 * half, :LANES] = src[:half]
    dst[1, :half, :LANES] = src[own - half : own]
    dst[1, half : 2 * half, :LANES] = r_ref[...]
    for b in range(2):
        dst[b, 2 * half :, :LANES] = src[own:]


def fill_edge_masks(kx_ref, dst, own, half, glob):
    for at, name, low in ((0, "l", 0), (1, "o", 0), (2, "o", own - half), (3, "r", 0)):
        dst[at // 2, at % 2 * half : (at % 2 + 1) * half, LANES:] = mask_piece(kx_ref, name, low, half, own, half)
    for b in range(2):
        dst[b, 2 * half :, LANES:] = mask_piece(kx_ref, "o", own, glob, own, half)


def local_inner_kernel(q_ref, k_ref, v_ref, qx_ref, kx_ref, o_ref, lse_ref, ks, vs, *, size, coef, own, half):
    step = pl.program_id(0)
    glob = k_ref.shape[0] - own

    @pl.when(step == 0)
    def _():
        fill_inner_masks(kx_ref, ks, own, half, glob)
        lse_ref[...] = jnp.zeros_like(lse_ref)

    fill_inner(k_ref, ks, own, half)
    fill_inner(v_ref, vs, own, half)
    places = [slice(j * half, (j + 1) * half) for j in range(own // half - 2)]
    tiles = []
    for j, there in enumerate(places):
        rows = slice(there.start + half, there.stop + half)
        tiles.append((q_ref[rows, :], qx_ref[rows, :], ks[j // 2], vs[j // 2]))
    for there, (o, lse) in zip(places, attend_pairs(tiles, [lse_ref[:, there] for there in places], step, size, coef)):
        o_ref[there, :], lse_ref[:, there] = o, lse


def local_edge_kernel(q_ref, k_ref, v_ref, lk_ref, lv_ref, rk_ref, rv_ref, qx_ref, kx_ref, io_ref, ilse_ref, o_ref, lse_ref, ks, vs, *, size, coef):
    step = pl.program_id(0)
    own, half = q_ref.shape[0], lk_ref.shape[0]
    glob = k_ref.shape[0] - own

    @pl.when(step == 0)
    def _():
        fill_edge_masks(kx_ref, ks, own, half, glob)
        lse_ref[...] = jnp.zeros_like(lse_ref)
        lse_ref[:, half : own - half] = ilse_ref[...]

    fill_edges(k_ref, lk_ref, rk_ref, ks, own, half)
    fill_edges(v_ref, lv_ref, rv_ref, vs, own, half)
    o_ref[half : own - half, :] = io_ref[...]
    places = [slice(0, half), slice(own - half, own)]
    tiles = [(q_ref[rows, :], qx_ref[rows, :], ks[b], vs[b]) for b, rows in enumerate(places)]
    for rows, (o, lse) in zip(places, attend_pairs(tiles, [lse_ref[:, rows] for rows in places], step, size, coef)):
        o_ref[rows, :], lse_ref[:, rows] = o, lse


def local_inner(qkv, qx, kx, own, half, size, coef, after=()):
    rows, width = qkv.shape[0], qkv.shape[1] // 3
    pairs, inner = width // LANES, own - 2 * half
    blocks, span = own // (2 * half) - 1, 2 * half + rows - own

    def cols(n, off=0):
        return pl.BlockSpec((n, LANES), lambda p: (0, p + off))

    def fixed(n):
        return pl.BlockSpec((n, LANES), lambda p: (0, 0))

    return pl.pallas_call(
        following(functools.partial(local_inner_kernel, size=size, coef=coef, own=own, half=half), 5, after),
        grid=(pairs,),
        in_specs=[cols(own), cols(rows, pairs), cols(rows, 2 * pairs), fixed(own), whole(kx)] + untouched(after),
        out_specs=[cols(inner), pl.BlockSpec((16, inner), lambda p: (0, 0))],
        out_shape=[SDS((inner, width), bf16), SDS((16, inner), f32)],
        scratch_shapes=[pltpu.VMEM((blocks, span, 2 * LANES), bf16), pltpu.VMEM((blocks, span, LANES), bf16)],
        compiler_params=limits(60),
        cost_estimate=cost(12),
        name="local_inner",
    )(qkv, qkv, qkv, qx, kx, *after)


def local_edge(qkv, left, right, qx, kx, io, ilse, own, half, size, coef, after=()):
    rows, width = qkv.shape[0], qkv.shape[1] // 3
    pairs, inner, span = width // LANES, own - 2 * half, 2 * half + rows - own

    def cols(n, off=0):
        return pl.BlockSpec((n, LANES), lambda p: (0, p + off))

    def fixed(n):
        return pl.BlockSpec((n, LANES), lambda p: (0, 0))

    return pl.pallas_call(
        following(functools.partial(local_edge_kernel, size=size, coef=coef), 11, after),
        grid=(pairs,),
        in_specs=[cols(own), cols(rows, pairs), cols(rows, 2 * pairs), cols(half), cols(half, pairs), cols(half), cols(half, pairs), fixed(own), whole(kx), cols(inner), whole(ilse)] + untouched(after),
        out_specs=[cols(own), pl.BlockSpec((16, own), lambda p: (0, 0))],
        out_shape=[SDS((own, width), bf16), SDS((16, own), f32)],
        scratch_shapes=[pltpu.VMEM((2, span, 2 * LANES), bf16), pltpu.VMEM((2, span, LANES), bf16)],
        compiler_params=limits(60),
        cost_estimate=cost(12),
        name="local_edge",
    )(qkv, qkv, qkv, left, left, right, right, qx, kx, io, ilse, *after)


def to_thirds(lse):
    high = lse.astype(bf16).astype(f32)
    middle = (lse - high).astype(bf16).astype(f32)
    low = lse - high - middle
    lane = lax.broadcasted_iota(jnp.int32, lse.shape, 1)
    packed = jnp.where(lane < 16, high, jnp.where(lane < 32, pltpu.roll(middle, 16, 1), pltpu.roll(low, 32, 1)))
    return jnp.where(lane < 48, packed, 0.0).astype(bf16)


def from_thirds(packed):
    packed = packed.astype(f32)
    lane = lax.broadcasted_iota(jnp.int32, packed.shape, 1)
    total = packed + (pltpu.roll(packed, LANES - 16, 1) + pltpu.roll(packed, LANES - 32, 1))
    return jnp.where(lane < 16, total, 0.0)


def glob_kernel(q_ref, k_ref, v_ref, qx_ref, kx_ref, out_ref, ks, lse_ref, *, size, coef, half):
    step = pl.program_id(0)
    glob = q_ref.shape[0]
    own = k_ref.shape[0] - glob

    @pl.when(step == 0)
    def _():
        ks[:own, LANES:] = kx_ref[half : half + own, :]
        ks[own:, LANES:] = kx_ref[2 * half + own :, :]
        lse_ref[...] = jnp.zeros_like(lse_ref)

    ks[:, :LANES] = k_ref[...]
    ((o, lse),) = attend_pairs([(q_ref[...], qx_ref[...], ks[...], v_ref[...])], [lse_ref[...]], step, size, coef)
    lse_ref[...] = lse
    out_ref[:, pl.ds(pl.multiple_of(step * LANES, LANES), LANES)] = o

    @pl.when(step == pl.num_programs(0) - 1)
    def _():
        out_ref[:, out_ref.shape[1] - LANES :] = to_thirds(lse.T)


def glob_attention(qkv, qx, kx, own, half, size, coef):
    rows, width = qkv.shape[0], qkv.shape[1] // 3
    pairs, glob = width // LANES, rows - own
    at = own // glob

    def cols(off):
        return pl.BlockSpec((rows, LANES), lambda p: (0, p + off))

    return pl.pallas_call(
        functools.partial(glob_kernel, size=size, coef=coef, half=half),
        grid=(pairs,),
        in_specs=[pl.BlockSpec((glob, LANES), lambda p: (at, p)), cols(pairs), cols(2 * pairs), pl.BlockSpec((glob, LANES), lambda p: (at, 0)), whole(kx)],
        out_specs=pl.BlockSpec((glob, width + LANES), lambda p: (0, 0)),
        out_shape=SDS((glob, width + LANES), bf16),
        scratch_shapes=[pltpu.VMEM((rows, 2 * LANES), bf16), pltpu.VMEM((LANES, glob), f32)],
        compiler_params=limits(60),
        cost_estimate=cost(8),
        name="glob_attention",
    )(qkv, qkv, qkv, qx, kx)


def merge_kernel(upper_ref, own_ref, other_ref, out_ref, lse_ref, *, size):
    upper = upper_ref[0] == 1
    width = own_ref.shape[1] - LANES
    own_l, other_l = from_thirds(own_ref[:, width:]), from_thirds(other_ref[:, width:])
    first, second = jnp.where(upper, other_l, own_l), jnp.where(upper, own_l, other_l)
    top = jnp.maximum(first, second)
    wa, wb = jnp.exp2(first - top), jnp.exp2(second - top)
    total = wa + wb
    lse = top + jnp.log2(total)
    lane = lax.broadcasted_iota(jnp.int32, lse.shape, 1)
    lse = jnp.where(lane < 16, lse, 0.0)
    lse_ref[...] = lse
    out_ref[:, width:] = to_thirds(lse)
    wa, wb = wa / total, wb / total
    for p in range(width // LANES):
        at = slice(p * LANES, (p + 1) * LANES)
        own_o, other_o = own_ref[:, at].astype(f32), other_ref[:, at].astype(f32)
        a, b = jnp.where(upper, other_o, own_o), jnp.where(upper, own_o, other_o)
        ka = jnp.where(lane < size, wa[:, 2 * p : 2 * p + 1], wa[:, 2 * p + 1 : 2 * p + 2])
        kb = jnp.where(lane < size, wb[:, 2 * p : 2 * p + 1], wb[:, 2 * p + 1 : 2 * p + 2])
        out_ref[:, at] = (a * ka + b * kb).astype(bf16)


def merge_step(part, axis, bit, size, after=()):
    other = swapped(part, axis, bit)
    return pl.pallas_call(
        following(functools.partial(merge_kernel, size=size), 3, after),
        in_specs=[pl.BlockSpec(memory_space=pltpu.SMEM), whole(part), whole(part)] + untouched(after),
        out_specs=[whole(part), pl.BlockSpec((part.shape[0], LANES), lambda: (0, 0))],
        out_shape=[SDS(part.shape, bf16), SDS((part.shape[0], LANES), f32)],
        compiler_params=limits(8),
        cost_estimate=cost(2),
        name="merge",
    )(side_of(axis, bit).reshape(1), part, other, *after)


def gathered(total, starts, chunk, shift=0):
    if chunk % 8 == 0:
        rows = [total[pl.ds(pl.multiple_of(start + shift, 8), chunk), :] for start in starts]
        return jnp.concatenate(rows, axis=0).astype(bf16)
    shape = (len(starts) * chunk, total.shape[0])
    place, row = lax.broadcasted_iota(jnp.int32, shape, 0), lax.broadcasted_iota(jnp.int32, shape, 1)
    wanted = place % chunk + shift
    for n, start in enumerate(starts):
        wanted = wanted + jnp.where(place // chunk == n, start, 0)
    return mm((wanted == row).astype(f32).astype(bf16), total[...].astype(bf16)).astype(bf16)


def split_rows(total, side, sent_ref, kept_ref, places):
    starts, chunk, apart = places
    sent_ref[...] = gathered(total, starts, chunk, (1 - side) * apart)
    kept_ref[...] = gathered(total, starts, chunk, side * apart)


def ffn_kernel(side_ref, flag_ref, att_ref, gatt_ref, tok_ref, glob_ref, wo_ref, up_ref, down_ref, vec_ref, bias_ref, br_tok_ref, br_glob_ref,
               out_tok_ref, out_glob_ref, mg_ref, hd_ref, wsent_ref, wkept_ref, dsent_ref, dkept_ref, vsum_ref, bsum_ref,
               att_s, n2s, n2t, br, act_s, hg_s, mixed_s, res_s, dn_s, sums_s, total, *, places, tall_places, pieces):
    step, last = pl.program_id(0), pl.num_programs(0) - 1
    own, width = tok_ref.shape
    rows = br.shape[0]
    flag = flag_ref[0]
    side = side_ref[0]
    size, steps = rows // pieces, act_s.shape[0]

    def at(n):
        return pl.ds(pl.multiple_of(n * size, size), size)

    def counted(x):
        return (x.astype(f32) * flag).astype(bf16)

    @pl.when(step == 0)
    def _():
        br[:own] = br_tok_ref[...]
        br[own:] = br_glob_ref[...]
        att_s[:own] = att_ref[...]
        att_s[own:] = gatt_ref[:, :width]
        mixed_s[:own] = tok_ref[...].astype(f32)
        mixed_s[own:] = glob_ref[...].astype(f32)

        def block(n, _):
            here = at(n)
            mixed = mixed_s[here, :] + mm(att_s[here, :], wo_ref[...])
            mixed_s[here, :] = mixed
            n2 = (normalize(mixed)[0] * vec_ref[2:3, :] + vec_ref[3:4, :]).astype(bf16)
            n2s[here, :] = n2
            res_s[here, :] = mixed + vec_ref[4:5, :]
            return 0

        lax.fori_loop(0, pieces, block, 0)
        n2t[:, :own] = n2s[:own, :].T
        n2t[:, own:] = counted(n2s[own:, :]).T
        dn_s[...] = jnp.zeros_like(dn_s)

    @pl.when((step >= steps) & (step < last))
    def _():
        slot = step - steps
        count = out_tok_ref.shape[0]
        out_tok_ref[...] = res_s[pl.ds(pl.multiple_of(slot * count, 16), count), :].astype(bf16)
        count = hd_ref.shape[0]
        here = pl.ds(pl.multiple_of(slot * count, 16), count)
        normalized, rstd = normalize(mixed_s[here, :])
        dn = dn_s[here, :]
        bf = br[here, :].astype(f32)
        ag = (bf + norm_back(normalized, rstd, vec_ref[2:3, :], dn)).astype(bf16)
        mg_ref[...] = ag
        hd_ref[...] = mm(ag, wo_ref[...], NT).astype(bf16)
        row = lax.broadcasted_iota(jnp.int32, (count, 1), 0) + slot * count
        keep = jnp.where(row < own, 1.0, flag)
        n2s[here, :] = (ag.astype(f32) * keep).astype(bf16)
        dn = dn * keep
        terms = [jnp.sum(term, axis=0, keepdims=True) for term in (dn * normalized, dn, bf * keep)]
        terms = jnp.concatenate(terms + [jnp.zeros((5, width), f32)], axis=0)
        sums_s[...] = terms + jnp.where(slot == 0, 0.0, sums_s[...])
        total[...] = mm(n2t[...], hg_s[slot])
        split_rows(total, side, wsent_ref, wkept_ref, places)
        hg = hg_s[slot].astype(f32)
        bsum_ref[...] = jnp.sum(hg[:own], axis=0, keepdims=True) + flag * jnp.sum(hg[own:], axis=0, keepdims=True)
        act_s[slot, own:, :] = counted(act_s[slot, own:, :])
        total[...] = mm(act_s[slot], br[...], TN)
        starts, rows_each = tall_places
        grad = gathered(total, starts, rows_each)
        part_rows = dsent_ref.shape[2]
        mine = slot % 2 == side
        for ref, wanted in ((dkept_ref, mine), (dsent_ref, jnp.logical_not(mine))):

            @pl.when(wanted)
            def _():
                for n in range(ref.shape[0]):
                    ref[n, 0] = grad[n * part_rows : (n + 1) * part_rows]

    @pl.when(step < steps)
    def _():
        slot = step

        def block(n, _):
            here = at(n)
            hidden = mm(n2s[here, :], up_ref[...]) + bias_ref[...]
            d_active = mm(br[here, :], down_ref[...], NT)
            active, slope = gelu_both(hidden)
            active = active.astype(bf16)
            hg = (d_active * slope).astype(bf16)
            act_s[slot, here, :] = active
            hg_s[slot, here, :] = hg
            res_s[here, :] += mm(active, down_ref[...])
            dn_s[here, :] += mm(hg, up_ref[...], NT)
            return 0

        lax.fori_loop(0, pieces, block, 0)

    @pl.when(step == last)
    def _():
        total[...] = mm(att_s[...], n2s[...], TN)
        split_rows(total, side, wsent_ref, wkept_ref, places)
        vsum_ref[...] = sums_s[...]
        out_glob_ref[...] = res_s[own:, :].astype(bf16)


def feed_forward(side, flag, att, gatt, tok, glob, wo, up, down, vec, bias, br_tok, br_glob, places, tall_places):
    own, width = tok.shape
    glob_rows = glob.shape[0]
    rows, units, chunk = own + glob_rows, up.shape[1], width
    steps = units // chunk
    pairs = lax.axis_size("batch") // 2
    assert steps == 2 * pairs

    def fixed(n):
        return pl.BlockSpec((n, width), lambda c: (0, 0))

    def once(array):
        return pl.BlockSpec(array.shape, lambda c: (0,) * array.ndim, pipeline_mode=pl.Buffered(1))

    def now(c):
        return jnp.minimum(c, steps - 1)

    def before(c):
        return jnp.clip(c - steps, 0, steps - 1)

    def by_part(n):
        assert n % (16 * steps) == 0
        return pl.BlockSpec((n // steps, width), lambda c: (before(c), 0))

    wide = pl.BlockSpec((width // 2, chunk), lambda c: (0, jnp.maximum(c - steps, 0)))
    parts = 2
    tall = pl.BlockSpec((parts, 1, chunk // parts, width), lambda c: (0, before(c) // 2, 0, 0))
    wide_shape = SDS((width // 2, units + width), bf16)
    tall_shape = SDS((parts, pairs, chunk // parts, width), bf16)
    smem = pl.BlockSpec(memory_space=pltpu.SMEM)
    low, full = pltpu.VMEM((rows, width), bf16), pltpu.VMEM((rows, width), f32)
    both = pltpu.VMEM((steps, rows, chunk), bf16)
    return pl.pallas_call(
        functools.partial(ffn_kernel, places=places, tall_places=tall_places, pieces=3),
        grid=(2 * steps + 1,),
        in_specs=[
            smem, smem, once(att), once(gatt), once(tok), once(glob), once(wo),
            pl.BlockSpec((width, chunk), lambda c: (0, now(c))), pl.BlockSpec((chunk, width), lambda c: (now(c), 0)), whole(vec),
            pl.BlockSpec((1, chunk), lambda c: (0, now(c))), once(br_tok), once(br_glob),
        ],
        out_specs=[
            by_part(own), fixed(glob_rows), by_part(rows), by_part(rows), wide, wide, tall, tall, fixed(8), pl.BlockSpec((1, chunk), lambda c: (0, before(c))),
        ],
        out_shape=[
            SDS((own, width), bf16), SDS((glob_rows, width), bf16), SDS((rows, width), bf16), SDS((rows, width), bf16),
            wide_shape, wide_shape, tall_shape, tall_shape, SDS((8, width), f32), SDS((1, units), f32),
        ],
        scratch_shapes=[low, low, pltpu.VMEM((width, rows), bf16), low, both, both, full, full, full, pltpu.VMEM((8, width), f32), pltpu.VMEM((width, width), f32)],
        compiler_params=limits(63),
        cost_estimate=cost(55),
        name="feed_forward",
    )(side, flag, att, gatt, tok, glob, wo, up, down, vec, bias, br_tok, br_glob)


def norm_rows(x_ref, gain, dn):
    normalized, rstd = normalize(x_ref[...].astype(f32))
    sums = [jnp.sum(dn * normalized, axis=0, keepdims=True), jnp.sum(dn, axis=0, keepdims=True)]
    return norm_back(normalized, rstd, gain, dn), jnp.concatenate(sums + [jnp.zeros((6, dn.shape[1]), f32)], axis=0)


def pair_backward(blocks, lse_rows, delta_rows, size, coef, scale):
    units = []
    for keys, values, tiles in blocks:
        for q, qx, do, at in tiles:
            for h in range(2):
                units.append((keys, values, head_part(q, h, size), qx, head_part(do, h, size), lse_rows[h][:, at], delta_rows[h][:, at]))
    scores = [mm(keys, jnp.concatenate([q, qx], axis=1), NT) for keys, _, q, qx, _, _, _ in units]
    dps = [mm(values, do, NT) for _, values, _, _, do, _, _ in units]
    weights = [jnp.exp2(s * coef - unit[5]) for s, unit in zip(scores, units)]
    dss = [(p * (dp - unit[6])).astype(bf16) for p, dp, unit in zip(weights, dps, units)]
    weights = [p.astype(bf16) for p in weights]
    results, first = [], 0
    for keys, _, tiles in blocks:
        here = range(first, first + 2 * len(tiles))
        first += 2 * len(tiles)
        keys_t = keys[:, :LANES].T
        dqs = []
        for n in here[::2]:
            parts = [mm(keys_t[h * size : (h + 1) * size], dss[n + h]) for h in range(2)]
            dqs.append((jnp.concatenate(parts, axis=0).T * scale).astype(bf16))
        dk = mm(jnp.concatenate([dss[n] for n in here], axis=1), jnp.concatenate([units[n][2] for n in here], axis=0)) * scale
        dv = mm(jnp.concatenate([weights[n] for n in here], axis=1), jnp.concatenate([units[n][4] for n in here], axis=0))
        results.append((dqs, dk, dv))
    return results


def inner_rows(o, do, size):
    prod = (o.astype(f32) * do.astype(f32)).T
    return [jnp.sum(prod[h * size : (h + 1) * size], axis=0, keepdims=True) for h in range(2)]


def edge_kernel(q_ref, k_ref, v_ref, lk_ref, lv_ref, rk_ref, rv_ref, qx_ref, kx_ref, o_ref, do_ref, lse_ref,
                dq_ref, dkv_ref, dg_ref, dl_ref, dr_ref, ks, vs, lses, *, size, coef, scale, own):
    step = pl.program_id(0)
    half = lk_ref.shape[0]
    glob = k_ref.shape[0] - own
    low = own - half

    @pl.when(step == 0)
    def _():
        fill_edge_masks(kx_ref, ks, own, half, glob)
        lses[:, :half] = lse_ref[:, :half]
        lses[:, half:] = lse_ref[:, low:]

    fill_edges(k_ref, lk_ref, rk_ref, ks, own, half)
    fill_edges(v_ref, lv_ref, rv_ref, vs, own, half)
    do = jnp.concatenate([do_ref[:half], do_ref[low:own]], axis=0)
    o = jnp.concatenate([o_ref[:half], o_ref[low:own]], axis=0)
    lse_rows = [lses[pl.ds(2 * step + h, 1), :] for h in range(2)]
    blocks = []
    for b, rows in enumerate((slice(0, half), slice(low, own))):
        there = slice(b * half, (b + 1) * half)
        blocks.append((ks[b], vs[b], [(q_ref[rows, :], qx_ref[rows, :], do[there], there)]))
    tails = []
    for b, (dqs, dk, dv) in enumerate(pair_backward(blocks, lse_rows, inner_rows(o, do, size), size, coef, scale)):
        there = slice(b * half, (b + 1) * half)
        dq_ref[there, :] = dqs[0]
        inside, outside = (slice(half, 2 * half), slice(0, half)) if b == 0 else (slice(0, half), slice(half, 2 * half))
        for n, part in enumerate((dk, dv)):
            dkv_ref[n, there, :] = part[inside]
            (dl_ref, dr_ref)[b][n] = part[outside].astype(bf16)
        tails.append((dk[2 * half :], dv[2 * half :]))
    for n in range(2):
        dg_ref[n] = tails[0][n] + tails[1][n]


def edge_backward(qkv, left, right, qx, kx, o, do, lse, own, size, coef, scale, after=()):
    rows, width = qkv.shape[0], qkv.shape[1] // 3
    pairs, half, glob = width // LANES, left.shape[0], rows - own

    def cols(n, off):
        return pl.BlockSpec((n, LANES), lambda p: (0, p + off))

    def both(n):
        return pl.BlockSpec((2, n, LANES), lambda p: (0, 0, p))

    fixed = pl.BlockSpec((own, LANES), lambda p: (0, 0))
    return pl.pallas_call(
        following(functools.partial(edge_kernel, size=size, coef=coef, scale=scale, own=own), 12, after),
        grid=(pairs,),
        in_specs=[
            cols(own, 0), cols(rows, pairs), cols(rows, 2 * pairs), cols(half, 0), cols(half, pairs), cols(half, 0), cols(half, pairs),
            fixed, whole(kx), cols(own, 0), cols(own, 0), whole(lse),
        ] + untouched(after),
        out_specs=[cols(2 * half, 0), both(2 * half), both(glob), both(half), both(half)],
        out_shape=[SDS((2 * half, width), bf16), SDS((2, 2 * half, width), f32), SDS((2, glob, width), f32)] + [SDS((2, half, width), bf16)] * 2,
        scratch_shapes=[
            pltpu.VMEM((2, 2 * half + glob, 2 * LANES), bf16), pltpu.VMEM((2, 2 * half + glob, LANES), bf16), pltpu.VMEM((16, 2 * half), f32),
        ],
        compiler_params=limits(60),
        cost_estimate=cost(17),
        name="edge_backward",
    )(qkv, qkv, qkv, left, left, right, right, qx, kx, o, do, lse, *after)


def inner_kernel(q_ref, k_ref, v_ref, qx_ref, kx_ref, o_ref, go_ref, do_ref, lse_ref, glse_ref, edq_ref, edkv_ref, edg_ref,
                 flag_ref, x_ref, vec_ref, mg_ref, wq_ref, wk_ref, wv_ref, dq_ref, dkv_ref, out_ref, sums_ref, ks, vs, lses, acc, dn_s, *, size, coef, scale, own, half):
    step = pl.program_id(0)
    rows = k_ref.shape[0]
    glob = rows - own
    blocks = ks.shape[0]

    @pl.when(step == 0)
    def _():
        fill_inner_masks(kx_ref, ks, own, half, glob)
        lses[:, :own] = lse_ref[...]
        lses[:, own:] = glse_ref[...].T[:16]

    fill_inner(k_ref, ks, own, half)
    fill_inner(v_ref, vs, own, half)
    o = jnp.concatenate([o_ref[...], go_ref[...]], axis=0)
    lse_rows = [lses[pl.ds(2 * step + h, 1), :] for h in range(2)]
    deltas = inner_rows(o, do_ref[...], size)
    kx_own = jnp.concatenate([kx_ref[half : half + own, :], kx_ref[2 * half + own :, :]], axis=0)

    def tile(at):
        return q_ref[at, :], qx_ref[at, :], do_ref[at, :], at

    every = [(jnp.concatenate([k_ref[...], kx_own], axis=1), v_ref[...], [tile(slice(own, rows))])]
    for b in range(blocks):
        low = half + b * 2 * half
        every.append((ks[b], vs[b], [tile(slice(low + j * half, low + (j + 1) * half)) for j in range(2)]))
    for b, (dqs, dk, dv) in enumerate(pair_backward(every, lse_rows, deltas, size, coef, scale)):
        for dq, (_, _, _, at) in zip(dqs, every[b][2]):
            dq_ref[at, :] = dq
        low = half + (b - 1) * 2 * half
        for n, part in enumerate((dk, dv)):
            if b == 0:
                acc[n] = part
            else:
                acc[n, low : low + 2 * half, :] += part[: 2 * half]
                acc[n, own:, :] += part[2 * half :]
    dq_ref[:half, :] = edq_ref[:half]
    dq_ref[own - half : own, :] = edq_ref[half:]
    for n in range(2):
        acc[n, :half, :] += edkv_ref[n, :half]
        acc[n, own - half : own, :] += edkv_ref[n, half:]
        acc[n, own:, :] += edg_ref[n]
    dkv_ref[...] = acc[...].astype(bf16)
    to_rows = mm(dq_ref[own:, :], wq_ref[...], NT) + mm(acc[0, own:, :].astype(bf16), wk_ref[...], NT) + mm(acc[1, own:, :].astype(bf16), wv_ref[...], NT)
    dn_s[...] = to_rows + jnp.where(step == 0, 0.0, dn_s[...])

    @pl.when(step == pl.num_programs(0) - 1)
    def _():
        back, sums = norm_rows(x_ref, vec_ref[0:1, :], dn_s[...])
        out_ref[...] = (mg_ref[...].astype(f32) * flag_ref[0] + back).astype(bf16)
        sums_ref[...] = sums


def inner_backward(qkv, qx, kx, o, go, do, lse, glse, edq, edkv, edg, flag, x, vec, mg, w, own, half, size, coef, scale, after=()):
    rows, width = qkv.shape[0], qkv.shape[1] // 3
    pairs, glob = width // LANES, rows - own
    blocks = own // (2 * half) - 1

    def cols(n, off=0):
        return pl.BlockSpec((n, LANES), lambda p: (0, p + off))

    def both(n):
        return pl.BlockSpec((2, n, LANES), lambda p: (0, 0, p))

    return pl.pallas_call(
        following(functools.partial(inner_kernel, size=size, coef=coef, scale=scale, own=own, half=half), 20, after),
        grid=(pairs,),
        in_specs=[
            cols(rows), cols(rows, pairs), cols(rows, 2 * pairs), whole(qx), whole(kx), cols(own), cols(glob), cols(rows), whole(lse), whole(glse),
            cols(2 * half), both(2 * half), both(glob), pl.BlockSpec(memory_space=pltpu.SMEM), whole(x), whole(vec),
            pl.BlockSpec((glob, width), lambda p: (own // glob, 0)), cols(width), cols(width, pairs), cols(width, 2 * pairs),
        ] + untouched(after),
        out_specs=[pl.BlockSpec((rows, LANES), lambda p: (0, p)), pl.BlockSpec((2, rows, LANES), lambda p: (0, 0, p)), whole(x), pl.BlockSpec((8, width), lambda p: (0, 0))],
        out_shape=[SDS((rows, width), bf16), SDS((2, rows, width), bf16), SDS(x.shape, bf16), SDS((8, width), f32)],
        scratch_shapes=[
            pltpu.VMEM((blocks, 2 * half + glob, 2 * LANES), bf16), pltpu.VMEM((blocks, 2 * half + glob, LANES), bf16),
            pltpu.VMEM((16, rows), f32), pltpu.VMEM((2, rows, LANES), f32), pltpu.VMEM((glob, width), f32),
        ],
        compiler_params=limits(60),
        cost_estimate=cost(13),
        name="inner_backward",
    )(qkv, qkv, qkv, qx, kx, o, go, do, lse, glse, edq, edkv, edg, flag, x, vec, mg, w, w, w, *after)


def weight_kernel(side_ref, nt_ref, ht_ref, dq_ref, dkv_ref, l_ref, r_ref, sent_ref, kept_ref, total, *, places):
    step = pl.program_id(0)

    @pl.when(step == 0)
    def _():
        total[...] = mm(nt_ref[...], dq_ref[...])

    @pl.when(step > 0)
    def _():
        total[...] = mm(nt_ref[...], dkv_ref[0]) + mm(ht_ref[...], jnp.concatenate([l_ref[0], r_ref[0]], axis=0))

    split_rows(total, side_ref[0], sent_ref, kept_ref, places)


def qkv_weight_grad(group, side, nt, ht, dq, dkv, dl, dr, places, after=()):
    width, rows = nt.shape
    cols, half = dq.shape[1], dl.shape[1]
    out = pl.BlockSpec((width // 2, cols), lambda c: (0, c))
    shape = SDS((width // 2, 3 * cols), bf16)
    halo = pl.BlockSpec((1, half, cols), lambda c: (jnp.maximum(c - 1, 0), 0, group))
    return pl.pallas_call(
        following(functools.partial(weight_kernel, places=places), 7, after),
        grid=(3,),
        in_specs=[
            pl.BlockSpec(memory_space=pltpu.SMEM), whole(nt), whole(ht), whole(dq),
            pl.BlockSpec((1, rows, cols), lambda c: (jnp.maximum(c - 1, 0), 0, 0)), halo, halo,
        ] + untouched(after),
        out_specs=[out, out],
        out_shape=[shape, shape],
        scratch_shapes=[pltpu.VMEM((width, cols), f32)],
        compiler_params=limits(60),
        cost_estimate=cost(0.1),
        name="qkv_weight_grad",
    )(side, nt, ht, dq, dkv, dl, dr, *after)


def halo_rows_kernel(lt_ref, rt_ref, vec_ref, w_ref, l_ref, r_ref, lout_ref, rout_ref, sums_ref):
    width = lt_ref.shape[1]
    sums = 0.0
    for x_ref, d_ref, out_ref in ((lt_ref, l_ref, lout_ref), (rt_ref, r_ref, rout_ref)):
        dn = mm(d_ref[0], w_ref[:, width : 2 * width], NT) + mm(d_ref[1], w_ref[:, 2 * width :], NT)
        back, part = norm_rows(x_ref, vec_ref[0:1, :], dn)
        out_ref[...] = back.astype(bf16)
        sums = sums + part
    sums_ref[...] = sums


def halo_rows(left, right, vec, w, dl, dr, after=()):
    args = (left, right, vec, w, dl, dr)
    half, width = left.shape
    return pl.pallas_call(
        following(halo_rows_kernel, len(args), after),
        in_specs=[whole(a) for a in args] + untouched(after),
        out_specs=[whole(left), whole(right), pl.BlockSpec((8, width), lambda: (0, 0))],
        out_shape=[SDS(left.shape, bf16), SDS(right.shape, bf16), SDS((8, width), f32)],
        compiler_params=limits(60),
        cost_estimate=cost(4),
        name="halo_rows",
    )(*args, *after)


def rows_kernel(flag_ref, x_ref, vec_ref, mg_ref, w_ref, *refs, groups, first, last):
    step = pl.program_id(0)
    assert groups == 1
    out_ref, sums_ref = refs[-2:]
    dq_ref, dkv_ref = refs[:2]
    dn = mm(jnp.concatenate([dq_ref[...], dkv_ref[0], dkv_ref[1]], axis=1), w_ref[...], NT)
    back, sums = norm_rows(x_ref, vec_ref[0:1, :], dn)
    out = mg_ref[...].astype(f32) * flag_ref[0] + back
    out_ref[...] = out.astype(out_ref.dtype)

    @pl.when(step == 0)
    def _():
        sums_ref[...] = sums

    @pl.when(step > 0)
    def _():
        sums_ref[...] += sums

    for ref, place in zip(refs[2:-2], (first, last)):
        if place is not None:

            @pl.when(step == place)
            def _():
                out_ref[...] = out + ref[...].astype(f32)


def row_grads(flag, x, vec, mg, w, parts, start, block, dtype, edges=(), after=(), share=(0, 1), into=None):
    count, width = x.shape
    groups = len(parts)
    cols = width // groups
    steps = count // block // share[1]
    ahead = share[0] * steps
    base = start // block + ahead
    after = ([] if into is None else [into]) + list(after)
    specs, args = [], []
    for dq, dkv in parts:
        specs += [pl.BlockSpec((block, cols), lambda r: (base + r, 0)), pl.BlockSpec((2, block, cols), lambda r: (0, base + r, 0))]
        args += [dq, dkv]
    here = pl.BlockSpec((block, width), lambda r: (ahead + r, 0))
    args = [flag, x, vec, mg, w] + args + list(edges)
    return pl.pallas_call(
        following(functools.partial(rows_kernel, groups=groups, first=0 if share[0] == 0 else None, last=steps - 1 if share[0] == share[1] - 1 else None), len(args), after),
        grid=(steps,),
        input_output_aliases={} if into is None else {len(args): 0},
        in_specs=[pl.BlockSpec(memory_space=pltpu.SMEM), here, whole(vec), pl.BlockSpec((block, width), lambda r: (base + r, 0)), whole(w)] + specs + [whole(e) for e in edges] + untouched(after),
        out_specs=[here, pl.BlockSpec((8, width), lambda r: (0, 0))],
        out_shape=[SDS(x.shape, dtype), SDS((8, width), f32)],
        compiler_params=limits(60),
        cost_estimate=cost(10 if edges else 0.1),
        name="row_grads",
    )(*args, *after)


def add_kernel(own_ref, other_ref, out_ref):
    out_ref[...] = (own_ref[...].astype(f32) + other_ref[...].astype(f32)).astype(out_ref.dtype)


def add_step(part, bit, dtype, after=()):
    return pl.pallas_call(
        following(add_kernel, 2, after),
        in_specs=[whole(part), whole(part)] + untouched(after),
        out_specs=whole(part),
        out_shape=SDS(part.shape, dtype),
        cost_estimate=cost(1),
        compiler_params=limits(8),
        name="add_step",
    )(part, swapped(part, *bit), *after)


def as_column(row):
    n = row.shape[1]
    eye = lax.broadcasted_iota(jnp.int32, (n, n), 0) == lax.broadcasted_iota(jnp.int32, (n, n), 1)
    return jnp.sum(jnp.where(eye, row, 0.0), axis=1, keepdims=True)


def split_shards(qkv_ref, rest_ref, units, width):
    groups = (rest_ref.shape[1] - units - width) // width
    starts = [units + width * (k + 1) for k in range(groups)]
    return qkv_ref[...], rest_ref[:, units : units + width], rest_ref[:, :units], [rest_ref[:, at : at + width] for at in starts]


def pack_kernel(qkv_ref, rest_ref, rq_ref, ro_ref, ru_ref, rd_ref, vone_ref, vtwo_ref, bias_ref,
                stats_ref, gout_ref, gup_ref, gdown_ref, nq_ref, no_ref, nu_ref, nd_ref, cq_ref, co_ref, cu_ref, cd_ref, *, decay):
    units, width = bias_ref.shape[1], vone_ref.shape[1]
    g_qkv, g_out, g_up, g_down = split_shards(qkv_ref, rest_ref, units, width)
    rows = g_qkv.shape[0]
    gout_ref[...], gup_ref[...] = g_out, g_up
    at, totals = 0, []
    for g, old_ref, new_ref, col_ref in ((g_qkv, rq_ref, nq_ref, cq_ref), (g_out, ro_ref, no_ref, co_ref), (g_up, ru_ref, nu_ref, cu_ref), (g_down, rd_ref, nd_ref, cd_ref)):
        groups = g if isinstance(g, list) else [g]
        columns, total, means = 0.0, 0.0, []
        for k, part in enumerate(groups):
            square = part * part + TINY_SQUARE
            columns = columns + jnp.sum(square, axis=0, keepdims=True)
            means.append(jnp.mean(square, axis=1, keepdims=True))
            if len(groups) > 1:
                gdown_ref[k * rows : (k + 1) * rows, :] = part
        mean = means[0] if len(means) == 1 else jnp.concatenate(means, axis=0)
        new = decay * as_column(old_ref[...].reshape(1, -1)) + (1.0 - decay) * mean
        col_ref[...] = new
        new_ref[...] = jnp.sum(jnp.where(lax.broadcasted_iota(jnp.int32, (new.shape[0],) * 2, 0) == lax.broadcasted_iota(jnp.int32, (new.shape[0],) * 2, 1), new, 0.0), axis=0)
        totals.append(jnp.sum(new, axis=0, keepdims=True))
        stats_ref[:, at : at + columns.shape[1]] = columns
        at += columns.shape[1]
    for ref, count in ((vone_ref, 2), (vtwo_ref, 3)):
        for n in range(count):
            stats_ref[:, at : at + width] = ref[n : n + 1, :]
            at += width
    stats_ref[:, at : at + units] = bias_ref[...]
    at += units
    lane = lax.broadcasted_iota(jnp.int32, (1, LANES), 1)
    last = jnp.zeros((1, LANES), f32)
    for n, total in enumerate(totals):
        last = jnp.where(lane == n, total, last)
    stats_ref[:, at : at + LANES] = last


def pack(qkv, rest, row_olds, vec_one, vec_two, bias, decay):
    units, width, rows = bias.shape[1], vec_one.shape[1], qkv.shape[0]
    tall = rest.shape[1] // width - units // width - 1
    count = qkv.shape[1] + width + units + width + 5 * width + units + LANES
    shapes = [(1, count), (rows, width), (rows, units), (tall * rows, width)]
    shapes += [old.shape for old in row_olds] + [(old.shape[0], 1) for old in row_olds]
    args = (qkv, rest, *row_olds, vec_one, vec_two, bias)
    return pl.pallas_call(
        functools.partial(pack_kernel, decay=decay),
        out_shape=[SDS(shape, f32) for shape in shapes],
        compiler_params=limits(24),
        cost_estimate=cost(3),
        name="pack",
    )(*args)


def update_kernel(stats_ref, qkv_ref, rest_ref, rq_ref, ro_ref, ru_ref, rd_ref, mq_ref, mo_ref, mu_ref, md_ref, oq_ref, oo_ref, ou_ref, od_ref,
                  vec_ref, vstate_ref, bias_ref, bstate_ref,
                  nq_ref, no_ref, nu_ref, nd_ref, cq_ref, co_ref, cu_ref, cd_ref, vg_ref, vs_ref, vn_ref, bg_ref, bs_ref, bn_ref, *, decay, full_rows):
    width, units = vec_ref.shape[1], bias_ref.shape[0]
    shards = split_shards(qkv_ref, rest_ref, units, width)
    rows = qkv_ref.shape[0]
    stats = stats_ref[...]
    totals = stats[:, stats.shape[1] - LANES :]
    at = 0
    sets = zip(shards, (rq_ref, ro_ref, ru_ref, rd_ref), (mq_ref, mo_ref, mu_ref, md_ref), (oq_ref, oo_ref, ou_ref, od_ref), (nq_ref, no_ref, nu_ref, nd_ref), (cq_ref, co_ref, cu_ref, cd_ref), full_rows)
    for n, (shard, row_ref, master_ref, old_ref, new_ref, col_ref, count) in enumerate(sets):
        columns = old_ref.shape[0]
        col = decay * old_ref[...].reshape(1, columns) + (1.0 - decay) * (stats[:, at : at + columns] / count)
        at += columns
        col_ref[...] = col[0]
        row_mean = totals[:, n : n + 1] / count
        parts = shard if isinstance(shard, list) else [shard]
        master = master_ref[...].astype(f32)
        for k, part in enumerate(parts):
            here = slice(k * rows, (k + 1) * rows)
            estimate = row_ref[here, :] * col / row_mean
            new_ref[here, :] = master[here] - RATE_MATRIX * part * lax.rsqrt(estimate)
    grad = jnp.concatenate([stats[:, at + n * width : at + (n + 1) * width] for n in range(5)], axis=0)
    at += 5 * width
    vg_ref[...] = grad
    state = decay * vstate_ref[...] + (1.0 - decay) * (grad * grad + TINY_SQUARE)
    vs_ref[...] = state
    vn_ref[...] = vec_ref[...] - RATE_VECTOR * grad * lax.rsqrt(state)
    grad = stats[:, at : at + units]
    bg_ref[...] = grad[0]
    state = decay * bstate_ref[...].reshape(1, units) + (1.0 - decay) * (grad * grad + TINY_SQUARE)
    bs_ref[...] = state[0]
    bn_ref[...] = (bias_ref[...].reshape(1, units) - RATE_VECTOR * grad * lax.rsqrt(state))[0]


def update(stats, qkv, rest, row_columns, masters, col_olds, vec, vec_state, bias, bias_state, decay, full_rows):
    args = (stats, qkv, rest, *row_columns, *masters, *col_olds, vec, vec_state, bias, bias_state)
    shapes = [m.shape for m in masters] + [c.shape for c in col_olds] + [vec.shape] * 3 + [bias.shape] * 3
    return pl.pallas_call(
        functools.partial(update_kernel, decay=decay, full_rows=full_rows),
        out_shape=[SDS(shape, f32) for shape in shapes],
        compiler_params=limits(24),
        cost_estimate=cost(3),
        name="update",
    )(*args)


def mask_kernel(info_ref, seg_ref, ok_ref, qx_ref, kx_ref, *, half, glob):
    lead, total = half // LANES, seg_ref.shape[1] // LANES
    own = qx_ref.shape[0] - glob
    lane = lax.broadcasted_iota(jnp.int32, (LANES, LANES), 1).astype(f32)
    for n in range(own // LANES + 2 * lead):
        block = info_ref[0] - lead + n
        at = pl.ds(pl.multiple_of(jnp.clip(block, 0, total - 1) * LANES, LANES), LANES)
        code = (seg_ref[:, at] + jnp.where(ok_ref[:, at] > 0, 8, 0)).astype(f32)
        code = jnp.broadcast_to(code, (LANES, LANES)).T
        valid = (code >= 8.0) & (block >= 0) & (block < total)
        document = jnp.where(code >= 8.0, code - 8.0, code) == lane
        seen = ((document | (lane == 4.0)) & valid) | (lane > 4.0)
        kx_ref[n * LANES : (n + 1) * LANES, :] = jnp.where(seen, 0.0, NEG_FILL).astype(bf16)
        if lead <= n < lead + own // LANES:
            qx_ref[(n - lead) * LANES : (n - lead + 1) * LANES, :] = jnp.where(document, 1.0, 0.0).astype(bf16)
    lane = lax.broadcasted_iota(jnp.int32, (glob, LANES), 1)
    kx_ref[own + 2 * half :, :] = jnp.where((lane == 4) & (info_ref[1] == 0), NEG_FILL, 0.0).astype(bf16)
    qx_ref[own:, :] = jnp.where(lane == 4, 1.0, 0.0).astype(bf16)


def mask_lanes(segments, valid, start, own, half, glob, first):
    info = jnp.stack([start // LANES, first.astype(jnp.int32)])
    return pl.pallas_call(
        functools.partial(mask_kernel, half=half, glob=glob),
        in_specs=[pl.BlockSpec(memory_space=pltpu.SMEM), whole(segments), whole(valid)],
        out_specs=[pl.BlockSpec((own + glob, LANES), lambda: (0, 0)), pl.BlockSpec((own + 2 * half + glob, LANES), lambda: (0, 0))],
        out_shape=[SDS((own + glob, LANES), bf16), SDS((own + 2 * half + glob, LANES), bf16)],
        compiler_params=limits(60),
        cost_estimate=cost(2),
        name="mask_lanes",
    )(info, segments, valid)


def body(
    tokens,
    glob_tokens,
    w_qkv,
    w_out,
    w_up,
    w_down,
    vec_params,
    hidden_bias,
    row_qkv,
    col_qkv,
    row_out,
    col_out,
    row_up,
    col_up,
    row_down,
    col_down,
    vec_state,
    bias_state,
    segments,
    valid_mask,
    out_cotangent,
    glob_cotangent,
):
    width = w_out.shape[0]
    size = width // HEADS
    assert 2 * size == LANES
    scale = size ** (-0.5)
    coef = scale * LOG2E
    half = BLOCK // 2
    tok, glob = tokens[0], glob_tokens[0]
    own, globs = tok.shape[0], glob.shape[0]
    seq_index = lax.axis_index("seq")
    first = seq_index == 0
    flag = first.astype(f32).reshape(1)
    bias_row = hidden_bias[None, :]
    batch_bits, seq_bits = bits_of("batch"), bits_of("seq")

    low, high = [batch_bits[:1]], [[bit] for bit in batch_bits[1:]]
    far = [seq_bits[1:][n : n + 2] for n in range(0, len(seq_bits) - 1, 2)]
    wide_stages = low + high + [seq_bits[:1]]
    tall_stages = low + [seq_bits[:1]] + high
    joint_stages = [[bit] for bit in seq_bits[1:]]
    pair_stages = low + [batch_bits[1:] + seq_bits[:1]] + far
    places = row_places(width, pair_stages)
    sequence = np.arange(1 << len(seq_bits)).reshape([2] * len(seq_bits)).transpose(
        [seq_bits[::-1].index(bit) for bit in seq_bits]
    ).reshape(-1)
    tall_chunk = w_down.shape[0] // lax.axis_size("batch") // sequence.size
    tall_places = tuple(int(n) * tall_chunk for n in sequence), tall_chunk
    halo_left, halo_right = shifted(tok[own - half :], "seq", 1), shifted(tok[:half], "seq", -1)
    qx, kx = mask_lanes(segments, valid_mask, seq_index * own, own, half, globs, first)
    qkv, normed_t = project(tok, glob, w_qkv, vec_params)
    part = glob_attention(qkv, qx, kx, own, half, size, coef)
    left, right, halo_t = project_halos(halo_left, halo_right, w_qkv, vec_params)
    part, glob_lse = merge_step(part, *seq_bits[0], size, after=[left])
    inner_att, inner_lse = local_inner(qkv, qx, kx, own, half, size, coef, after=[part])
    for bit in seq_bits[1:-1]:
        part, glob_lse = merge_step(part, *bit, size, after=[inner_lse])
    att, lse = local_edge(qkv, left, right, qx, kx, inner_att, inner_lse, own, half, size, coef, after=[part])
    part, glob_lse = merge_step(part, *seq_bits[-1], size, after=[lse])
    side = side_of(*batch_bits[0]).reshape(1)
    out_tok, out_glob, mixed_grad, heads_grad, *matrices, vec_two, bias_sum = feed_forward(
        side, flag, att, part, tok, glob, w_out, w_up, w_down, vec_params, bias_row, out_cotangent[0], glob_cotangent[0], places, tall_places
    )
    wide, down = Scatter(*matrices[:2], wide_stages), Scatter(*matrices[2:], tall_stages)
    edge = edge_backward(qkv, left, right, qx, kx, att, heads_grad, lse, own, size, coef, scale, after=wide.parts + down.parts)
    grad_left, grad_right = edge[3:]
    down.step(after=edge[:1])
    wide.step(after=down.parts)
    to_left, to_right, halo_sums = halo_rows(halo_left, halo_right, vec_params, w_qkv, grad_left, grad_right, after=wide.parts)
    edges = (shifted(to_right, "seq", 1), shifted(to_left, "seq", -1))
    dq, dkv, glob_part, glob_sums = inner_backward(
        qkv, qx, kx, att, part, heads_grad, lse, glob_lse, *edge[:3], flag, glob, vec_params, mixed_grad, w_qkv, own, half, size, coef, scale,
        after=[to_left, to_right],
    )
    parts = [(dq, dkv)]
    down.step(after=[parts[0][0]], us=0.01)
    wide.step(after=[*down.parts, *edges], us=0.01)
    weight = Scatter(*qkv_weight_grad(0, side, normed_t, halo_t, dq, dkv, grad_left, grad_right, places, after=wide.parts), pair_stages)
    glob_bits = seq_bits[1:] + seq_bits[:1]
    glob_part = add_step(glob_part, glob_bits[0], bf16, after=weight.parts)
    joint = joint_scatter(wide, down, joint_stages, after=[glob_part])
    weight.step(after=joint.parts)
    for bit in glob_bits[1:-1]:
        glob_part = add_step(glob_part, bit, bf16, after=weight.parts)
    ones = jnp.ones((1,), f32)
    row_args = (vec_params, mixed_grad, w_qkv, parts, 0, half, f32)
    tokens_grad, one_sums = row_grads(ones, tok, *row_args, edges=edges, after=[glob_part], share=(0, 2))
    joint.step(after=[one_sums])
    tokens_grad, two_sums = row_grads(ones, tok, *row_args, edges=edges, after=joint.parts, share=(1, 2), into=tokens_grad)
    tok_sums = one_sums + two_sums
    weight.step(after=[two_sums])
    glob_part = add_step(glob_part, glob_bits[-1], f32, after=weight.parts)
    while joint.stages:
        rest = joint.step(after=[glob_part])
    while weight.stages:
        shard_qkv = weight.step(after=[rest])
    decay = 1.0 - STEP ** (-0.8)
    units = w_up.shape[1]
    owner = lax.axis_index(("batch", "seq"))
    masters = []
    for matrix in (w_qkv, w_out, w_up, w_down):
        rows = matrix.shape[0] // lax.axis_size(("batch", "seq"))
        masters.append(lax.dynamic_slice_in_dim(matrix, owner * rows, rows, 0))
    stats, grad_out, grad_up, grad_down, *rows_new = pack(
        shard_qkv, rest, (row_qkv, row_out, row_up, row_down), halo_sums + glob_sums + tok_sums, vec_two, bias_sum, decay
    )
    every = batch_bits + seq_bits
    for bits in [every[n : n + 2] for n in range(0, len(every), 2)]:
        terms = [stats] + [flipped(stats, bits, n) for n in range(1, 1 << len(bits))]
        while len(terms) > 1:
            terms = [a + b for a, b in zip(terms[::2], terms[1::2])]
        stats = terms[0]
    new_qkv, new_out, new_up, new_down, col_qkv_new, col_out_new, col_up_new, col_down_new, *vectors = update(
        stats, shard_qkv, rest, rows_new[4:], masters, (col_qkv, col_out, col_up, col_down), vec_params, vec_state, hidden_bias, bias_state,
        decay, (w_qkv.shape[0], w_out.shape[0], w_up.shape[0], w_down.shape[0]),
    )
    return (
        out_tok[None],
        out_glob[None],
        tokens_grad[None],
        glob_part[None],
        shard_qkv,
        rows_new[0],
        col_qkv_new,
        new_qkv,
        grad_out,
        rows_new[1],
        col_out_new,
        new_out,
        grad_up,
        rows_new[2],
        col_up_new,
        new_up,
        grad_down,
        rows_new[3],
        col_down_new,
        new_down,
        *vectors,
    )


def solution(mesh):
    in_specs = (
        P("batch", "seq", None),
        P("batch", None, None),
        P(),
        P(),
        P(),
        P(),
        P(),
        P(),
        P(("batch", "seq")),
        P(),
        P(("batch", "seq")),
        P(),
        P(("batch", "seq")),
        P(),
        P(("batch", "seq")),
        P(),
        P(),
        P(),
        P("batch", None),
        P("batch", None),
        P("batch", "seq", None),
        P("batch", None, None),
    )
    out_specs = (
        P("batch", "seq", None),
        P("batch", None, None),
        P("batch", "seq", None),
        P("batch", None, None),
        P(("batch", "seq"), None),
        P(("batch", "seq")),
        P(),
        P(("batch", "seq"), None),
        P(("batch", "seq"), None),
        P(("batch", "seq")),
        P(),
        P(("batch", "seq"), None),
        P(("batch", "seq"), None),
        P(("batch", "seq")),
        P(),
        P(("batch", "seq"), None),
        P(("batch", "seq"), None),
        P(("batch", "seq")),
        P(),
        P(("batch", "seq"), None),
        P(),
        P(),
        P(),
        P(),
        P(),
        P(),
    )
    return jax.shard_map(body, mesh=mesh, in_specs=in_specs, out_specs=out_specs, check_vma=False)
```

```python
import functools

import jax
import jax.numpy as jnp
import numpy as np
from jax import lax
from jax.experimental import pallas as pl
from jax.experimental.pallas import tpu as pltpu
from jax.sharding import PartitionSpec as P

HEADS = 12
BLOCK = 512
STEP = 10

NEG_FILL = -8e9
NORM_EPS = 1e-06
TINY_SQUARE = 1e-30
RATE_MATRIX = 0.03
RATE_VECTOR = 0.2
LANES = 128
LOG2E = 1.4426950408889634

f32, bf16 = jnp.float32, jnp.bfloat16
NN = (((1,), (0,)), ((), ()))
NT = (((1,), (1,)), ((), ()))
TN = (((0,), (0,)), ((), ()))
SDS = jax.ShapeDtypeStruct


def bits_of(axis):
    size = lax.axis_size(axis)
    assert size & (size - 1) == 0
    return [(axis, 1 << k) for k in range(size.bit_length() - 1)]


def side_of(axis, bit):
    return (lax.axis_index(axis) // bit) % 2


def swapped(values, axis, bit):
    return lax.ppermute(values, axis, [(i, i ^ bit) for i in range(lax.axis_size(axis))])


def shifted(values, axis, distance):
    devices = range(lax.axis_size(axis))
    return lax.ppermute(values, axis, [(i, i + distance) for i in devices if i + distance in devices])


def summed(parts, bits):
    leaves, tree = jax.tree.flatten(parts)
    flat = jnp.concatenate([leaf.reshape(-1) for leaf in leaves])
    count = flat.shape[0]
    flat = jnp.pad(flat, (0, -count % 1024)).reshape(-1, LANES)
    for axis, bit in bits:
        flat = flat + swapped(flat, axis, bit)
    flat = flat.reshape(-1)
    out, place = [], 0
    for leaf in leaves:
        out.append(flat[place : place + leaf.size].reshape(leaf.shape))
        place += leaf.size
    return jax.tree.unflatten(tree, out)


def flipped(values, bits, flips):
    sizes = {axis: lax.axis_size(axis) for axis in ("batch", "seq")}
    change = {axis: sum(bit for n, (name, bit) in enumerate(bits) if name == axis and flips >> n & 1) for axis in sizes}
    route = [
        (b * sizes["seq"] + s, (b ^ change["batch"]) * sizes["seq"] + (s ^ change["seq"]))
        for b in range(sizes["batch"])
        for s in range(sizes["seq"])
    ]
    return lax.ppermute(values, ("batch", "seq"), route)


def mm(a, b, dims=NN):
    return lax.dot_general(a, b, dims, preferred_element_type=f32)


def limits(mib):
    return pltpu.CompilerParams(vmem_limit_bytes=mib * 2**20)


def cost(us):
    return pl.CostEstimate(flops=int(us * 1.15e9), bytes_accessed=1 << 20, transcendentals=0)


def whole(array):
    return pl.BlockSpec(array.shape, lambda *_: (0,) * array.ndim)


def following(kernel, inputs, after):
    return lambda *refs: kernel(*refs[:inputs], *refs[inputs + len(after) :])


def untouched(after):
    return [pl.BlockSpec(memory_space=pl.ANY)] * len(after)


def normalize(x):
    mean = jnp.mean(x, axis=1, keepdims=True)
    centred = x - mean
    rstd = lax.rsqrt(jnp.mean(centred * centred, axis=1, keepdims=True) + NORM_EPS)
    return centred * rstd, rstd


def norm_back(normalized, rstd, gain, grad):
    g = grad * gain
    inner = jnp.mean(g * normalized, axis=1, keepdims=True)
    return rstd * (g - jnp.mean(g, axis=1, keepdims=True) - normalized * inner)


def gelu_both(u):
    phi = 0.5 + 0.5 * lax.erf(u * 0.7071067811865476)
    density = jnp.exp2(u * u * (-0.5 * LOG2E)) * 0.3989422804014327
    return u * phi, phi + u * density


def head_part(values, head, size):
    lanes = lax.broadcasted_iota(jnp.int32, values.shape, 1)
    return jnp.where((lanes // size) == head, values, jnp.zeros_like(values))


def stage_kernel(side_ref, kept_ref, *refs, arrived, parts):
    for n in range(parts):
        at = side_ref[0] ^ n if parts > 1 else 0
        total = kept_ref[at].astype(f32)
        for ref in refs[:arrived]:
            total = total + ref[at].astype(f32)
        out = refs[arrived + n]
        out[...] = total.astype(out.dtype)


class Scatter:
    def __init__(self, sent, kept, stages):
        self.stages, self.parts, self.kept = list(stages), [sent], kept

    def step(self, after=(), us=2):
        bits = self.stages.pop(0)
        arrived = [flipped(part, bits[::-1], n + 1) for n, part in enumerate(self.parts)]
        bits = self.stages[0] if self.stages else []
        parts, columns = 1 << len(bits), self.kept.shape[-1]
        rows = self.kept.size // columns // parts
        block = columns if self.kept.size < 1 << 20 else columns // 3 if columns % 1152 == 0 or columns % 3840 == 0 else columns
        tall = 3 if columns == block and rows % 32 == 0 and self.kept.size > 1 << 19 else 1
        args = [a.reshape(parts, rows, columns) for a in [self.kept] + arrived]
        side = sum(side_of(*bit) << n for n, bit in enumerate(reversed(bits))) if bits else jnp.int32(0)
        spec = pl.BlockSpec((parts, rows // tall, block), lambda c, r: (0, r, c))
        out = pl.BlockSpec((rows // tall, block), lambda c, r: (r, c))
        after = list(after)
        self.kept, *self.parts = pl.pallas_call(
            following(functools.partial(stage_kernel, arrived=len(arrived), parts=parts), 1 + len(args), after),
            grid=(columns // block, tall),
            in_specs=[pl.BlockSpec(memory_space=pltpu.SMEM)] + [spec] * len(args) + untouched(after),
            out_specs=[out] * parts,
            out_shape=[SDS((rows, columns), bf16 if bits else f32)] + [SDS((rows, columns), bf16)] * (parts - 1),
            compiler_params=limits(24),
            cost_estimate=cost(us),
            name="sum_stage",
        )(side.reshape(1), *args, *after)
        return self.kept


def joint_kernel(side_ref, wk_ref, wa_ref, dk_ref, da_ref, sent_ref, kept_ref, total, *, chunk, starts):
    columns = wk_ref.shape[2]
    block = dk_ref.shape[2]
    for ref, flip in ((sent_ref, 1), (kept_ref, 0)):
        at = side_ref[0] ^ flip
        ref[:, :columns] = (wk_ref[at].astype(f32) + wa_ref[at].astype(f32)).astype(bf16)
        total[...] = dk_ref[at].astype(f32) + da_ref[at].astype(f32)
        for k, places in enumerate(starts):
            ref[:, columns + k * block : columns + (k + 1) * block] = gathered(total, places, chunk)


def joint_scatter(wide, down, stages, after=()):
    (bit,) = stages[0]
    args = []
    for scatter in (wide, down):
        bits = scatter.stages.pop(0)
        arrived = flipped(scatter.parts[0], bits, 1)
        args += [a.reshape(2, -1, a.shape[-1]) for a in (scatter.kept, arrived)]
    _, rows, columns = args[0].shape
    _, rows_down, block = args[2].shape
    owners = 1 << (len(stages) - 1)
    chunk = rows // owners
    groups = rows_down // rows
    starts = [[(n * groups + k) * chunk for n in range(owners)] for k in range(groups)]
    shape = SDS((rows, columns + groups * block), bf16)
    after = list(after)
    sent, kept = pl.pallas_call(
        following(functools.partial(joint_kernel, chunk=chunk, starts=starts), 5, after),
        in_specs=[pl.BlockSpec(memory_space=pltpu.SMEM)] + [whole(a) for a in args] + untouched(after),
        out_specs=[pl.BlockSpec(shape.shape, lambda: (0, 0))] * 2,
        out_shape=[shape, shape],
        scratch_shapes=[pltpu.VMEM((rows_down, block), f32)],
        compiler_params=limits(24),
        cost_estimate=cost(100),
        name="joint_stage",
    )(side_of(*bit).reshape(1), *args, *after)
    return Scatter(sent, kept, stages)


def row_places(width, stages):
    labels = bits_of("batch")[::-1] + bits_of("seq")[::-1]
    owners = np.arange(1 << len(labels)).reshape([2] * len(labels))
    owners = owners.transpose([labels.index(bit) for stage in stages for bit in stage]).reshape(2, -1)
    chunk = width // owners.size
    return tuple(int(owner) * chunk for owner in owners[0]), chunk, int(owners[1, 0] - owners[0, 0]) * chunk


def project_kernel(tok_ref, glob_ref, w_ref, vec_ref, qkv_ref, nt_ref, n_s):
    own = tok_ref.shape[0]

    @pl.when(pl.program_id(0) == 0)
    def _():
        for ref, rows in ((tok_ref, slice(0, own)), (glob_ref, slice(own, n_s.shape[0]))):
            n = normalize(ref[...].astype(f32))[0] * vec_ref[0:1, :] + vec_ref[1:2, :]
            n = n.astype(bf16)
            n_s[rows, :] = n
            nt_ref[:, rows] = n.T

    qkv_ref[...] = mm(n_s[...], w_ref[...]).astype(bf16)


def project(tok, glob, w, vec):
    width = tok.shape[1]
    rows = tok.shape[0] + glob.shape[0]
    return pl.pallas_call(
        project_kernel,
        grid=(w.shape[1] // width,),
        in_specs=[whole(tok), whole(glob), pl.BlockSpec((width, width), lambda c: (0, c)), whole(vec)],
        out_specs=[
            pl.BlockSpec((rows, width), lambda c: (0, c)),
            pl.BlockSpec((width, rows), lambda c: (0, 0)),
        ],
        out_shape=[SDS((rows, w.shape[1]), bf16), SDS((width, rows), bf16)],
        scratch_shapes=[pltpu.VMEM((rows, width), bf16)],
        compiler_params=limits(32),
        cost_estimate=cost(9),
        name="project",
    )(tok, glob, w, vec)


def halo_kernel(l_ref, r_ref, w_ref, vec_ref, lkv_ref, rkv_ref, nt_ref):
    half = l_ref.shape[0]
    for ref, out, at in ((l_ref, lkv_ref, 0), (r_ref, rkv_ref, half)):
        n = normalize(ref[...].astype(f32))[0] * vec_ref[0:1, :] + vec_ref[1:2, :]
        n = n.astype(bf16)
        nt_ref[:, at : at + half] = n.T
        out[...] = mm(n, w_ref[...]).astype(bf16)


def project_halos(left, right, w, vec):
    half, width = left.shape
    kv = pl.BlockSpec((half, width), lambda c: (0, c))
    return pl.pallas_call(
        halo_kernel,
        grid=(2,),
        in_specs=[whole(left), whole(right), pl.BlockSpec((width, width), lambda c: (0, c + 1)), whole(vec)],
        out_specs=[kv, kv, pl.BlockSpec((width, 2 * half), lambda c: (0, 0))],
        out_shape=[SDS((half, 2 * width), bf16)] * 2 + [SDS((width, 2 * half), bf16)],
        compiler_params=limits(60),
        cost_estimate=cost(3),
        name="project_halos",
    )(left, right, w, vec)


def attend_pairs(tiles, lse_rows, step, size, coef):
    scores = []
    for q, qx, keys, _ in tiles:
        for h in range(2):
            scores.append(mm(keys, jnp.concatenate([head_part(q, h, size), qx], axis=1), NT))
    tops = [jnp.max(s, axis=0, keepdims=True) * coef for s in scores]
    weights = [jnp.exp2(s * coef - top) for s, top in zip(scores, tops)]
    totals = [jnp.sum(p, axis=0, keepdims=True) for p in weights]
    outs = []
    for n, p in enumerate(weights):
        h = n % 2
        values_t = tiles[n // 2][3].T[h * size : (h + 1) * size]
        outs.append(mm(values_t, p.astype(bf16)) * (1.0 / totals[n]))
    results = []
    for n, lse in enumerate(lse_rows):
        row = lax.broadcasted_iota(jnp.int32, lse.shape, 0)
        for h in range(2):
            lse = jnp.where(row == 2 * step + h, tops[2 * n + h] + jnp.log2(totals[2 * n + h]), lse)
        results.append((jnp.concatenate(outs[2 * n : 2 * n + 2], axis=0).T.astype(bf16), lse))
    return results


def mask_piece(kx_ref, name, low, rows, own, half):
    if name == "l":
        start = low
    elif name == "r":
        start = half + own + low
    else:
        start = half + low if low < own else 2 * half + low
    return kx_ref[start : start + rows, :]


def fill_inner(src, dst, own, half):
    for b in range(dst.shape[0]):
        low = half + b * 2 * half
        dst[b, : 2 * half, :LANES] = src[low : low + 2 * half]
        dst[b, 2 * half :, :LANES] = src[own:]


def fill_inner_masks(kx_ref, dst, own, half, glob):
    for b in range(dst.shape[0]):
        dst[b, : 2 * half, LANES:] = mask_piece(kx_ref, "o", half + b * 2 * half, 2 * half, own, half)
        dst[b, 2 * half :, LANES:] = mask_piece(kx_ref, "o", own, glob, own, half)


def fill_edges(src, l_ref, r_ref, dst, own, half):
    dst[0, :half, :LANES] = l_ref[...]
    dst[0, half : 2 * half, :LANES] = src[:half]
    dst[1, :half, :LANES] = src[own - half : own]
    dst[1, half : 2 * half, :LANES] = r_ref[...]
    for b in range(2):
        dst[b, 2 * half :, :LANES] = src[own:]


def fill_edge_masks(kx_ref, dst, own, half, glob):
    for at, name, low in ((0, "l", 0), (1, "o", 0), (2, "o", own - half), (3, "r", 0)):
        dst[at // 2, at % 2 * half : (at % 2 + 1) * half, LANES:] = mask_piece(kx_ref, name, low, half, own, half)
    for b in range(2):
        dst[b, 2 * half :, LANES:] = mask_piece(kx_ref, "o", own, glob, own, half)


def local_inner_kernel(q_ref, k_ref, v_ref, qx_ref, kx_ref, o_ref, lse_ref, ks, vs, *, size, coef, own, half):
    step = pl.program_id(0)
    glob = k_ref.shape[0] - own

    @pl.when(step == 0)
    def _():
        fill_inner_masks(kx_ref, ks, own, half, glob)
        lse_ref[...] = jnp.zeros_like(lse_ref)

    fill_inner(k_ref, ks, own, half)
    fill_inner(v_ref, vs, own, half)
    places = [slice(j * half, (j + 1) * half) for j in range(own // half - 2)]
    tiles = []
    for j, there in enumerate(places):
        rows = slice(there.start + half, there.stop + half)
        tiles.append((q_ref[rows, :], qx_ref[rows, :], ks[j // 2], vs[j // 2]))
    for there, (o, lse) in zip(places, attend_pairs(tiles, [lse_ref[:, there] for there in places], step, size, coef)):
        o_ref[there, :], lse_ref[:, there] = o, lse


def local_edge_kernel(q_ref, k_ref, v_ref, lk_ref, lv_ref, rk_ref, rv_ref, qx_ref, kx_ref, io_ref, ilse_ref, o_ref, lse_ref, ks, vs, *, size, coef):
    step = pl.program_id(0)
    own, half = q_ref.shape[0], lk_ref.shape[0]
    glob = k_ref.shape[0] - own

    @pl.when(step == 0)
    def _():
        fill_edge_masks(kx_ref, ks, own, half, glob)
        lse_ref[...] = jnp.zeros_like(lse_ref)
        lse_ref[:, half : own - half] = ilse_ref[...]

    fill_edges(k_ref, lk_ref, rk_ref, ks, own, half)
    fill_edges(v_ref, lv_ref, rv_ref, vs, own, half)
    o_ref[half : own - half, :] = io_ref[...]
    places = [slice(0, half), slice(own - half, own)]
    tiles = [(q_ref[rows, :], qx_ref[rows, :], ks[b], vs[b]) for b, rows in enumerate(places)]
    for rows, (o, lse) in zip(places, attend_pairs(tiles, [lse_ref[:, rows] for rows in places], step, size, coef)):
        o_ref[rows, :], lse_ref[:, rows] = o, lse


def local_inner(qkv, qx, kx, own, half, size, coef, after=()):
    rows, width = qkv.shape[0], qkv.shape[1] // 3
    pairs, inner = width // LANES, own - 2 * half
    blocks, span = own // (2 * half) - 1, 2 * half + rows - own

    def cols(n, off=0):
        return pl.BlockSpec((n, LANES), lambda p: (0, p + off))

    def fixed(n):
        return pl.BlockSpec((n, LANES), lambda p: (0, 0))

    return pl.pallas_call(
        following(functools.partial(local_inner_kernel, size=size, coef=coef, own=own, half=half), 5, after),
        grid=(pairs,),
        in_specs=[cols(own), cols(rows, pairs), cols(rows, 2 * pairs), fixed(own), whole(kx)] + untouched(after),
        out_specs=[cols(inner), pl.BlockSpec((16, inner), lambda p: (0, 0))],
        out_shape=[SDS((inner, width), bf16), SDS((16, inner), f32)],
        scratch_shapes=[pltpu.VMEM((blocks, span, 2 * LANES), bf16), pltpu.VMEM((blocks, span, LANES), bf16)],
        compiler_params=limits(32),
        cost_estimate=cost(12),
        name="local_inner",
    )(qkv, qkv, qkv, qx, kx, *after)


def local_edge(qkv, left, right, qx, kx, io, ilse, own, half, size, coef, after=()):
    rows, width = qkv.shape[0], qkv.shape[1] // 3
    pairs, inner, span = width // LANES, own - 2 * half, 2 * half + rows - own

    def cols(n, off=0):
        return pl.BlockSpec((n, LANES), lambda p: (0, p + off))

    def fixed(n):
        return pl.BlockSpec((n, LANES), lambda p: (0, 0))

    return pl.pallas_call(
        following(functools.partial(local_edge_kernel, size=size, coef=coef), 11, after),
        grid=(pairs,),
        in_specs=[cols(own), cols(rows, pairs), cols(rows, 2 * pairs), cols(half), cols(half, pairs), cols(half), cols(half, pairs), fixed(own), whole(kx), cols(inner), whole(ilse)] + untouched(after),
        out_specs=[cols(own), pl.BlockSpec((16, own), lambda p: (0, 0))],
        out_shape=[SDS((own, width), bf16), SDS((16, own), f32)],
        scratch_shapes=[pltpu.VMEM((2, span, 2 * LANES), bf16), pltpu.VMEM((2, span, LANES), bf16)],
        compiler_params=limits(32),
        cost_estimate=cost(12),
        name="local_edge",
    )(qkv, qkv, qkv, left, left, right, right, qx, kx, io, ilse, *after)


def to_thirds(lse):
    high = lse.astype(bf16).astype(f32)
    middle = (lse - high).astype(bf16).astype(f32)
    low = lse - high - middle
    lane = lax.broadcasted_iota(jnp.int32, lse.shape, 1)
    packed = jnp.where(lane < 16, high, jnp.where(lane < 32, pltpu.roll(middle, 16, 1), pltpu.roll(low, 32, 1)))
    return jnp.where(lane < 48, packed, 0.0).astype(bf16)


def from_thirds(packed):
    packed = packed.astype(f32)
    lane = lax.broadcasted_iota(jnp.int32, packed.shape, 1)
    total = packed + (pltpu.roll(packed, LANES - 16, 1) + pltpu.roll(packed, LANES - 32, 1))
    return jnp.where(lane < 16, total, 0.0)


def glob_kernel(q_ref, k_ref, v_ref, qx_ref, kx_ref, out_ref, ks, lse_ref, *, size, coef, half):
    step = pl.program_id(0)
    glob = q_ref.shape[0]
    own = k_ref.shape[0] - glob

    @pl.when(step == 0)
    def _():
        ks[:own, LANES:] = kx_ref[half : half + own, :]
        ks[own:, LANES:] = kx_ref[2 * half + own :, :]
        lse_ref[...] = jnp.zeros_like(lse_ref)

    ks[:, :LANES] = k_ref[...]
    ((o, lse),) = attend_pairs([(q_ref[...], qx_ref[...], ks[...], v_ref[...])], [lse_ref[...]], step, size, coef)
    lse_ref[...] = lse
    out_ref[:, pl.ds(pl.multiple_of(step * LANES, LANES), LANES)] = o

    @pl.when(step == pl.num_programs(0) - 1)
    def _():
        out_ref[:, out_ref.shape[1] - LANES :] = to_thirds(lse.T)


def glob_attention(qkv, qx, kx, own, half, size, coef):
    rows, width = qkv.shape[0], qkv.shape[1] // 3
    pairs, glob = width // LANES, rows - own
    at = own // glob

    def cols(off):
        return pl.BlockSpec((rows, LANES), lambda p: (0, p + off))

    return pl.pallas_call(
        functools.partial(glob_kernel, size=size, coef=coef, half=half),
        grid=(pairs,),
        in_specs=[pl.BlockSpec((glob, LANES), lambda p: (at, p)), cols(pairs), cols(2 * pairs), pl.BlockSpec((glob, LANES), lambda p: (at, 0)), whole(kx)],
        out_specs=pl.BlockSpec((glob, width + LANES), lambda p: (0, 0)),
        out_shape=SDS((glob, width + LANES), bf16),
        scratch_shapes=[pltpu.VMEM((rows, 2 * LANES), bf16), pltpu.VMEM((LANES, glob), f32)],
        compiler_params=limits(32),
        cost_estimate=cost(8),
        name="glob_attention",
    )(qkv, qkv, qkv, qx, kx)


def merge_kernel(upper_ref, own_ref, other_ref, out_ref, lse_ref, *, size):
    upper = upper_ref[0] == 1
    width = own_ref.shape[1] - LANES
    own_l, other_l = from_thirds(own_ref[:, width:]), from_thirds(other_ref[:, width:])
    first, second = jnp.where(upper, other_l, own_l), jnp.where(upper, own_l, other_l)
    top = jnp.maximum(first, second)
    wa, wb = jnp.exp2(first - top), jnp.exp2(second - top)
    total = wa + wb
    lse = top + jnp.log2(total)
    lane = lax.broadcasted_iota(jnp.int32, lse.shape, 1)
    lse = jnp.where(lane < 16, lse, 0.0)
    lse_ref[...] = lse
    out_ref[:, width:] = to_thirds(lse)
    wa, wb = wa / total, wb / total
    for p in range(width // LANES):
        at = slice(p * LANES, (p + 1) * LANES)
        own_o, other_o = own_ref[:, at].astype(f32), other_ref[:, at].astype(f32)
        a, b = jnp.where(upper, other_o, own_o), jnp.where(upper, own_o, other_o)
        ka = jnp.where(lane < size, wa[:, 2 * p : 2 * p + 1], wa[:, 2 * p + 1 : 2 * p + 2])
        kb = jnp.where(lane < size, wb[:, 2 * p : 2 * p + 1], wb[:, 2 * p + 1 : 2 * p + 2])
        out_ref[:, at] = (a * ka + b * kb).astype(bf16)


def merge_step(part, axis, bit, size, after=()):
    other = swapped(part, axis, bit)
    return pl.pallas_call(
        following(functools.partial(merge_kernel, size=size), 3, after),
        in_specs=[pl.BlockSpec(memory_space=pltpu.SMEM), whole(part), whole(part)] + untouched(after),
        out_specs=[whole(part), pl.BlockSpec((part.shape[0], LANES), lambda: (0, 0))],
        out_shape=[SDS(part.shape, bf16), SDS((part.shape[0], LANES), f32)],
        compiler_params=limits(8),
        cost_estimate=cost(2),
        name="merge",
    )(side_of(axis, bit).reshape(1), part, other, *after)


def gathered(total, starts, chunk, shift=0):
    if chunk % 8 == 0:
        rows = [total[pl.ds(pl.multiple_of(start + shift, 8), chunk), :] for start in starts]
        return jnp.concatenate(rows, axis=0).astype(bf16)
    shape = (len(starts) * chunk, total.shape[0])
    place, row = lax.broadcasted_iota(jnp.int32, shape, 0), lax.broadcasted_iota(jnp.int32, shape, 1)
    wanted = place % chunk + shift
    for n, start in enumerate(starts):
        wanted = wanted + jnp.where(place // chunk == n, start, 0)
    return mm((wanted == row).astype(f32).astype(bf16), total[...].astype(bf16)).astype(bf16)


def split_rows(total, side, sent_ref, kept_ref, places):
    starts, chunk, apart = places
    sent_ref[...] = gathered(total, starts, chunk, (1 - side) * apart)
    kept_ref[...] = gathered(total, starts, chunk, side * apart)


def ffn_kernel(side_ref, flag_ref, att_ref, gatt_ref, tok_ref, glob_ref, wo_ref, up_ref, down_ref, vec_ref, bias_ref, br_tok_ref, br_glob_ref,
               out_tok_ref, out_glob_ref, mg_ref, hd_ref, wsent_ref, wkept_ref, dsent_ref, dkept_ref, vsum_ref, bsum_ref,
               att_s, n2s, n2t, br, act_s, hg_s, mixed_s, res_s, dn_s, sums_s, total, *, places, tall_places, pieces):
    step, last = pl.program_id(0), pl.num_programs(0) - 1
    own, width = tok_ref.shape
    rows = br.shape[0]
    flag = flag_ref[0]
    side = side_ref[0]
    size, steps = rows // pieces, act_s.shape[0]

    def at(n):
        return pl.ds(pl.multiple_of(n * size, size), size)

    def counted(x):
        return (x.astype(f32) * flag).astype(bf16)

    @pl.when(step == 0)
    def _():
        br[:own] = br_tok_ref[...]
        br[own:] = br_glob_ref[...]
        att_s[:own] = att_ref[...]
        att_s[own:] = gatt_ref[:, :width]
        mixed_s[:own] = tok_ref[...].astype(f32)
        mixed_s[own:] = glob_ref[...].astype(f32)

        def block(n, _):
            here = at(n)
            mixed = mixed_s[here, :] + mm(att_s[here, :], wo_ref[...])
            mixed_s[here, :] = mixed
            n2 = (normalize(mixed)[0] * vec_ref[2:3, :] + vec_ref[3:4, :]).astype(bf16)
            n2s[here, :] = n2
            res_s[here, :] = mixed + vec_ref[4:5, :]
            return 0

        lax.fori_loop(0, pieces, block, 0)
        n2t[:, :own] = n2s[:own, :].T
        n2t[:, own:] = counted(n2s[own:, :]).T
        dn_s[...] = jnp.zeros_like(dn_s)

    @pl.when((step >= steps) & (step < last))
    def _():
        slot = step - steps
        count = out_tok_ref.shape[0]
        out_tok_ref[...] = res_s[pl.ds(pl.multiple_of(slot * count, 16), count), :].astype(bf16)
        count = hd_ref.shape[0]
        here = pl.ds(pl.multiple_of(slot * count, 16), count)
        normalized, rstd = normalize(mixed_s[here, :])
        dn = dn_s[here, :]
        bf = br[here, :].astype(f32)
        ag = (bf + norm_back(normalized, rstd, vec_ref[2:3, :], dn)).astype(bf16)
        mg_ref[...] = ag
        hd_ref[...] = mm(ag, wo_ref[...], NT).astype(bf16)
        row = lax.broadcasted_iota(jnp.int32, (count, 1), 0) + slot * count
        keep = jnp.where(row < own, 1.0, flag)
        n2s[here, :] = (ag.astype(f32) * keep).astype(bf16)
        dn = dn * keep
        terms = [jnp.sum(term, axis=0, keepdims=True) for term in (dn * normalized, dn, bf * keep)]
        terms = jnp.concatenate(terms + [jnp.zeros((5, width), f32)], axis=0)
        sums_s[...] = terms + jnp.where(slot == 0, 0.0, sums_s[...])
        total[...] = mm(n2t[...], hg_s[slot])
        split_rows(total, side, wsent_ref, wkept_ref, places)
        hg = hg_s[slot].astype(f32)
        bsum_ref[...] = jnp.sum(hg[:own], axis=0, keepdims=True) + flag * jnp.sum(hg[own:], axis=0, keepdims=True)
        act_s[slot, own:, :] = counted(act_s[slot, own:, :])
        total[...] = mm(act_s[slot], br[...], TN)
        starts, rows_each = tall_places
        grad = gathered(total, starts, rows_each)
        part_rows = dsent_ref.shape[2]
        mine = slot % 2 == side
        for ref, wanted in ((dkept_ref, mine), (dsent_ref, jnp.logical_not(mine))):

            @pl.when(wanted)
            def _():
                for n in range(ref.shape[0]):
                    ref[n, 0] = grad[n * part_rows : (n + 1) * part_rows]

    @pl.when(step < steps)
    def _():
        slot = step

        def block(n, _):
            here = at(n)
            hidden = mm(n2s[here, :], up_ref[...]) + bias_ref[...]
            d_active = mm(br[here, :], down_ref[...], NT)
            active, slope = gelu_both(hidden)
            active = active.astype(bf16)
            hg = (d_active * slope).astype(bf16)
            act_s[slot, here, :] = active
            hg_s[slot, here, :] = hg
            res_s[here, :] += mm(active, down_ref[...])
            dn_s[here, :] += mm(hg, up_ref[...], NT)
            return 0

        lax.fori_loop(0, pieces, block, 0)

    @pl.when(step == last)
    def _():
        total[...] = mm(att_s[...], n2s[...], TN)
        split_rows(total, side, wsent_ref, wkept_ref, places)
        vsum_ref[...] = sums_s[...]
        out_glob_ref[...] = res_s[own:, :].astype(bf16)


def feed_forward(side, flag, att, gatt, tok, glob, wo, up, down, vec, bias, br_tok, br_glob, places, tall_places):
    own, width = tok.shape
    glob_rows = glob.shape[0]
    rows, units, chunk = own + glob_rows, up.shape[1], width
    steps = units // chunk
    pairs = lax.axis_size("batch") // 2
    assert steps == 2 * pairs

    def fixed(n):
        return pl.BlockSpec((n, width), lambda c: (0, 0))

    def once(array):
        return pl.BlockSpec(array.shape, lambda c: (0,) * array.ndim, pipeline_mode=pl.Buffered(1))

    def now(c):
        return jnp.minimum(c, steps - 1)

    def before(c):
        return jnp.clip(c - steps, 0, steps - 1)

    def by_part(n):
        assert n % (16 * steps) == 0
        return pl.BlockSpec((n // steps, width), lambda c: (before(c), 0))

    wide = pl.BlockSpec((width // 2, chunk), lambda c: (0, jnp.maximum(c - steps, 0)))
    parts = 2
    tall = pl.BlockSpec((parts, 1, chunk // parts, width), lambda c: (0, before(c) // 2, 0, 0))
    wide_shape = SDS((width // 2, units + width), bf16)
    tall_shape = SDS((parts, pairs, chunk // parts, width), bf16)
    smem = pl.BlockSpec(memory_space=pltpu.SMEM)
    low, full = pltpu.VMEM((rows, width), bf16), pltpu.VMEM((rows, width), f32)
    both = pltpu.VMEM((steps, rows, chunk), bf16)
    return pl.pallas_call(
        functools.partial(ffn_kernel, places=places, tall_places=tall_places, pieces=3),
        grid=(2 * steps + 1,),
        in_specs=[
            smem, smem, once(att), once(gatt), once(tok), once(glob), once(wo),
            pl.BlockSpec((width, chunk), lambda c: (0, now(c))), pl.BlockSpec((chunk, width), lambda c: (now(c), 0)), whole(vec),
            pl.BlockSpec((1, chunk), lambda c: (0, now(c))), once(br_tok), once(br_glob),
        ],
        out_specs=[
            by_part(own), fixed(glob_rows), by_part(rows), by_part(rows), wide, wide, tall, tall, fixed(8), pl.BlockSpec((1, chunk), lambda c: (0, before(c))),
        ],
        out_shape=[
            SDS((own, width), bf16), SDS((glob_rows, width), bf16), SDS((rows, width), bf16), SDS((rows, width), bf16),
            wide_shape, wide_shape, tall_shape, tall_shape, SDS((8, width), f32), SDS((1, units), f32),
        ],
        scratch_shapes=[low, low, pltpu.VMEM((width, rows), bf16), low, both, both, full, full, full, pltpu.VMEM((8, width), f32), pltpu.VMEM((width, width), f32)],
        compiler_params=limits(63),
        cost_estimate=cost(55),
        name="feed_forward",
    )(side, flag, att, gatt, tok, glob, wo, up, down, vec, bias, br_tok, br_glob)


def norm_rows(x_ref, gain, dn):
    normalized, rstd = normalize(x_ref[...].astype(f32))
    sums = [jnp.sum(dn * normalized, axis=0, keepdims=True), jnp.sum(dn, axis=0, keepdims=True)]
    return norm_back(normalized, rstd, gain, dn), jnp.concatenate(sums + [jnp.zeros((6, dn.shape[1]), f32)], axis=0)


def pair_backward(blocks, lse_rows, delta_rows, size, coef, scale):
    units = []
    for keys, values, tiles in blocks:
        for q, qx, do, at in tiles:
            for h in range(2):
                units.append((keys, values, head_part(q, h, size), qx, head_part(do, h, size), lse_rows[h][:, at], delta_rows[h][:, at]))
    scores = [mm(keys, jnp.concatenate([q, qx], axis=1), NT) for keys, _, q, qx, _, _, _ in units]
    dps = [mm(values, do, NT) for _, values, _, _, do, _, _ in units]
    weights = [jnp.exp2(s * coef - unit[5]) for s, unit in zip(scores, units)]
    dss = [(p * (dp - unit[6])).astype(bf16) for p, dp, unit in zip(weights, dps, units)]
    weights = [p.astype(bf16) for p in weights]
    results, first = [], 0
    for keys, _, tiles in blocks:
        here = range(first, first + 2 * len(tiles))
        first += 2 * len(tiles)
        keys_t = keys[:, :LANES].T
        dqs = []
        for n in here[::2]:
            parts = [mm(keys_t[h * size : (h + 1) * size], dss[n + h]) for h in range(2)]
            dqs.append((jnp.concatenate(parts, axis=0).T * scale).astype(bf16))
        dk = mm(jnp.concatenate([dss[n] for n in here], axis=1), jnp.concatenate([units[n][2] for n in here], axis=0)) * scale
        dv = mm(jnp.concatenate([weights[n] for n in here], axis=1), jnp.concatenate([units[n][4] for n in here], axis=0))
        results.append((dqs, dk, dv))
    return results


def inner_rows(o, do, size):
    prod = (o.astype(f32) * do.astype(f32)).T
    return [jnp.sum(prod[h * size : (h + 1) * size], axis=0, keepdims=True) for h in range(2)]


def edge_kernel(q_ref, k_ref, v_ref, lk_ref, lv_ref, rk_ref, rv_ref, qx_ref, kx_ref, o_ref, do_ref, lse_ref,
                dq_ref, dkv_ref, dg_ref, dl_ref, dr_ref, ks, vs, lses, *, size, coef, scale, own):
    step = pl.program_id(0)
    half = lk_ref.shape[0]
    glob = k_ref.shape[0] - own
    low = own - half

    @pl.when(step == 0)
    def _():
        fill_edge_masks(kx_ref, ks, own, half, glob)
        lses[:, :half] = lse_ref[:, :half]
        lses[:, half:] = lse_ref[:, low:]

    fill_edges(k_ref, lk_ref, rk_ref, ks, own, half)
    fill_edges(v_ref, lv_ref, rv_ref, vs, own, half)
    do = jnp.concatenate([do_ref[:half], do_ref[low:own]], axis=0)
    o = jnp.concatenate([o_ref[:half], o_ref[low:own]], axis=0)
    lse_rows = [lses[pl.ds(2 * step + h, 1), :] for h in range(2)]
    blocks = []
    for b, rows in enumerate((slice(0, half), slice(low, own))):
        there = slice(b * half, (b + 1) * half)
        blocks.append((ks[b], vs[b], [(q_ref[rows, :], qx_ref[rows, :], do[there], there)]))
    tails = []
    for b, (dqs, dk, dv) in enumerate(pair_backward(blocks, lse_rows, inner_rows(o, do, size), size, coef, scale)):
        there = slice(b * half, (b + 1) * half)
        dq_ref[there, :] = dqs[0]
        inside, outside = (slice(half, 2 * half), slice(0, half)) if b == 0 else (slice(0, half), slice(half, 2 * half))
        for n, part in enumerate((dk, dv)):
            dkv_ref[n, there, :] = part[inside]
            (dl_ref, dr_ref)[b][n] = part[outside].astype(bf16)
        tails.append((dk[2 * half :], dv[2 * half :]))
    for n in range(2):
        dg_ref[n] = tails[0][n] + tails[1][n]


def edge_backward(qkv, left, right, qx, kx, o, do, lse, own, size, coef, scale, after=()):
    rows, width = qkv.shape[0], qkv.shape[1] // 3
    pairs, half, glob = width // LANES, left.shape[0], rows - own

    def cols(n, off):
        return pl.BlockSpec((n, LANES), lambda p: (0, p + off))

    def both(n):
        return pl.BlockSpec((2, n, LANES), lambda p: (0, 0, p))

    fixed = pl.BlockSpec((own, LANES), lambda p: (0, 0))
    return pl.pallas_call(
        following(functools.partial(edge_kernel, size=size, coef=coef, scale=scale, own=own), 12, after),
        grid=(pairs,),
        in_specs=[
            cols(own, 0), cols(rows, pairs), cols(rows, 2 * pairs), cols(half, 0), cols(half, pairs), cols(half, 0), cols(half, pairs),
            fixed, whole(kx), cols(own, 0), cols(own, 0), whole(lse),
        ] + untouched(after),
        out_specs=[cols(2 * half, 0), both(2 * half), both(glob), both(half), both(half)],
        out_shape=[SDS((2 * half, width), bf16), SDS((2, 2 * half, width), f32), SDS((2, glob, width), f32)] + [SDS((2, half, width), bf16)] * 2,
        scratch_shapes=[
            pltpu.VMEM((2, 2 * half + glob, 2 * LANES), bf16), pltpu.VMEM((2, 2 * half + glob, LANES), bf16), pltpu.VMEM((16, 2 * half), f32),
        ],
        compiler_params=limits(60),
        cost_estimate=cost(17),
        name="edge_backward",
    )(qkv, qkv, qkv, left, left, right, right, qx, kx, o, do, lse, *after)


def inner_kernel(q_ref, k_ref, v_ref, qx_ref, kx_ref, o_ref, go_ref, do_ref, lse_ref, glse_ref, edq_ref, edkv_ref, edg_ref,
                 flag_ref, x_ref, vec_ref, mg_ref, wq_ref, wk_ref, wv_ref, dq_ref, dkv_ref, out_ref, sums_ref, ks, vs, lses, acc, dn_s, *, size, coef, scale, own, half):
    step = pl.program_id(0)
    rows = k_ref.shape[0]
    glob = rows - own
    blocks = ks.shape[0]

    @pl.when(step == 0)
    def _():
        fill_inner_masks(kx_ref, ks, own, half, glob)
        lses[:, :own] = lse_ref[...]
        lses[:, own:] = glse_ref[...].T[:16]

    fill_inner(k_ref, ks, own, half)
    fill_inner(v_ref, vs, own, half)
    o = jnp.concatenate([o_ref[...], go_ref[...]], axis=0)
    lse_rows = [lses[pl.ds(2 * step + h, 1), :] for h in range(2)]
    deltas = inner_rows(o, do_ref[...], size)
    kx_own = jnp.concatenate([kx_ref[half : half + own, :], kx_ref[2 * half + own :, :]], axis=0)

    def tile(at):
        return q_ref[at, :], qx_ref[at, :], do_ref[at, :], at

    every = [(jnp.concatenate([k_ref[...], kx_own], axis=1), v_ref[...], [tile(slice(own, rows))])]
    for b in range(blocks):
        low = half + b * 2 * half
        every.append((ks[b], vs[b], [tile(slice(low + j * half, low + (j + 1) * half)) for j in range(2)]))
    for b, (dqs, dk, dv) in enumerate(pair_backward(every, lse_rows, deltas, size, coef, scale)):
        for dq, (_, _, _, at) in zip(dqs, every[b][2]):
            dq_ref[at, :] = dq
        low = half + (b - 1) * 2 * half
        for n, part in enumerate((dk, dv)):
            if b == 0:
                acc[n] = part
            else:
                acc[n, low : low + 2 * half, :] += part[: 2 * half]
                acc[n, own:, :] += part[2 * half :]
    dq_ref[:half, :] = edq_ref[:half]
    dq_ref[own - half : own, :] = edq_ref[half:]
    for n in range(2):
        acc[n, :half, :] += edkv_ref[n, :half]
        acc[n, own - half : own, :] += edkv_ref[n, half:]
        acc[n, own:, :] += edg_ref[n]
    dkv_ref[...] = acc[...].astype(bf16)
    to_rows = mm(dq_ref[own:, :], wq_ref[...], NT) + mm(acc[0, own:, :].astype(bf16), wk_ref[...], NT) + mm(acc[1, own:, :].astype(bf16), wv_ref[...], NT)
    dn_s[...] = to_rows + jnp.where(step == 0, 0.0, dn_s[...])

    @pl.when(step == pl.num_programs(0) - 1)
    def _():
        back, sums = norm_rows(x_ref, vec_ref[0:1, :], dn_s[...])
        out_ref[...] = (mg_ref[...].astype(f32) * flag_ref[0] + back).astype(bf16)
        sums_ref[...] = sums


def inner_backward(qkv, qx, kx, o, go, do, lse, glse, edq, edkv, edg, flag, x, vec, mg, w, own, half, size, coef, scale, after=()):
    rows, width = qkv.shape[0], qkv.shape[1] // 3
    pairs, glob = width // LANES, rows - own
    blocks = own // (2 * half) - 1

    def cols(n, off=0):
        return pl.BlockSpec((n, LANES), lambda p: (0, p + off))

    def both(n):
        return pl.BlockSpec((2, n, LANES), lambda p: (0, 0, p))

    return pl.pallas_call(
        following(functools.partial(inner_kernel, size=size, coef=coef, scale=scale, own=own, half=half), 20, after),
        grid=(pairs,),
        in_specs=[
            cols(rows), cols(rows, pairs), cols(rows, 2 * pairs), whole(qx), whole(kx), cols(own), cols(glob), cols(rows), whole(lse), whole(glse),
            cols(2 * half), both(2 * half), both(glob), pl.BlockSpec(memory_space=pltpu.SMEM), whole(x), whole(vec),
            pl.BlockSpec((glob, width), lambda p: (own // glob, 0)), cols(width), cols(width, pairs), cols(width, 2 * pairs),
        ] + untouched(after),
        out_specs=[pl.BlockSpec((rows, LANES), lambda p: (0, p)), pl.BlockSpec((2, rows, LANES), lambda p: (0, 0, p)), whole(x), pl.BlockSpec((8, width), lambda p: (0, 0))],
        out_shape=[SDS((rows, width), bf16), SDS((2, rows, width), bf16), SDS(x.shape, bf16), SDS((8, width), f32)],
        scratch_shapes=[
            pltpu.VMEM((blocks, 2 * half + glob, 2 * LANES), bf16), pltpu.VMEM((blocks, 2 * half + glob, LANES), bf16),
            pltpu.VMEM((16, rows), f32), pltpu.VMEM((2, rows, LANES), f32), pltpu.VMEM((glob, width), f32),
        ],
        compiler_params=limits(60),
        cost_estimate=cost(13),
        name="inner_backward",
    )(qkv, qkv, qkv, qx, kx, o, go, do, lse, glse, edq, edkv, edg, flag, x, vec, mg, w, w, w, *after)


def weight_kernel(side_ref, nt_ref, ht_ref, dq_ref, dkv_ref, l_ref, r_ref, sent_ref, kept_ref, total, *, places):
    step = pl.program_id(0)

    @pl.when(step == 0)
    def _():
        total[...] = mm(nt_ref[...], dq_ref[...])

    @pl.when(step > 0)
    def _():
        total[...] = mm(nt_ref[...], dkv_ref[0]) + mm(ht_ref[...], jnp.concatenate([l_ref[0], r_ref[0]], axis=0))

    split_rows(total, side_ref[0], sent_ref, kept_ref, places)


def qkv_weight_grad(group, side, nt, ht, dq, dkv, dl, dr, places, after=()):
    width, rows = nt.shape
    cols, half = dq.shape[1], dl.shape[1]
    out = pl.BlockSpec((width // 2, cols), lambda c: (0, c))
    shape = SDS((width // 2, 3 * cols), bf16)
    halo = pl.BlockSpec((1, half, cols), lambda c: (jnp.maximum(c - 1, 0), 0, group))
    return pl.pallas_call(
        following(functools.partial(weight_kernel, places=places), 7, after),
        grid=(3,),
        in_specs=[
            pl.BlockSpec(memory_space=pltpu.SMEM), whole(nt), whole(ht), whole(dq),
            pl.BlockSpec((1, rows, cols), lambda c: (jnp.maximum(c - 1, 0), 0, 0)), halo, halo,
        ] + untouched(after),
        out_specs=[out, out],
        out_shape=[shape, shape],
        scratch_shapes=[pltpu.VMEM((width, cols), f32)],
        compiler_params=limits(60),
        cost_estimate=cost(0.1),
        name="qkv_weight_grad",
    )(side, nt, ht, dq, dkv, dl, dr, *after)


def halo_rows_kernel(lt_ref, rt_ref, vec_ref, w_ref, l_ref, r_ref, lout_ref, rout_ref, sums_ref):
    width = lt_ref.shape[1]
    sums = 0.0
    for x_ref, d_ref, out_ref in ((lt_ref, l_ref, lout_ref), (rt_ref, r_ref, rout_ref)):
        dn = mm(d_ref[0], w_ref[:, width : 2 * width], NT) + mm(d_ref[1], w_ref[:, 2 * width :], NT)
        back, part = norm_rows(x_ref, vec_ref[0:1, :], dn)
        out_ref[...] = back.astype(bf16)
        sums = sums + part
    sums_ref[...] = sums


def halo_rows(left, right, vec, w, dl, dr, after=()):
    args = (left, right, vec, w, dl, dr)
    half, width = left.shape
    return pl.pallas_call(
        following(halo_rows_kernel, len(args), after),
        in_specs=[whole(a) for a in args] + untouched(after),
        out_specs=[whole(left), whole(right), pl.BlockSpec((8, width), lambda: (0, 0))],
        out_shape=[SDS(left.shape, bf16), SDS(right.shape, bf16), SDS((8, width), f32)],
        compiler_params=limits(24),
        cost_estimate=cost(4),
        name="halo_rows",
    )(*args, *after)


def rows_kernel(flag_ref, x_ref, vec_ref, mg_ref, w_ref, *refs, groups, first, last):
    step = pl.program_id(0)
    assert groups == 1
    out_ref, sums_ref = refs[-2:]
    dq_ref, dkv_ref = refs[:2]
    dn = mm(jnp.concatenate([dq_ref[...], dkv_ref[0], dkv_ref[1]], axis=1), w_ref[...], NT)
    back, sums = norm_rows(x_ref, vec_ref[0:1, :], dn)
    out = mg_ref[...].astype(f32) * flag_ref[0] + back
    out_ref[...] = out.astype(out_ref.dtype)

    @pl.when(step == 0)
    def _():
        sums_ref[...] = sums

    @pl.when(step > 0)
    def _():
        sums_ref[...] += sums

    for ref, place in zip(refs[2:-2], (first, last)):
        if place is not None:

            @pl.when(step == place)
            def _():
                out_ref[...] = out + ref[...].astype(f32)


def row_grads(flag, x, vec, mg, w, parts, start, block, dtype, edges=(), after=(), share=(0, 1), into=None):
    count, width = x.shape
    groups = len(parts)
    cols = width // groups
    steps = count // block // share[1]
    ahead = share[0] * steps
    base = start // block + ahead
    after = ([] if into is None else [into]) + list(after)
    specs, args = [], []
    for dq, dkv in parts:
        specs += [pl.BlockSpec((block, cols), lambda r: (base + r, 0)), pl.BlockSpec((2, block, cols), lambda r: (0, base + r, 0))]
        args += [dq, dkv]
    here = pl.BlockSpec((block, width), lambda r: (ahead + r, 0))
    args = [flag, x, vec, mg, w] + args + list(edges)
    return pl.pallas_call(
        following(functools.partial(rows_kernel, groups=groups, first=0 if share[0] == 0 else None, last=steps - 1 if share[0] == share[1] - 1 else None), len(args), after),
        grid=(steps,),
        input_output_aliases={} if into is None else {len(args): 0},
        in_specs=[pl.BlockSpec(memory_space=pltpu.SMEM), here, whole(vec), pl.BlockSpec((block, width), lambda r: (base + r, 0)), whole(w)] + specs + [whole(e) for e in edges] + untouched(after),
        out_specs=[here, pl.BlockSpec((8, width), lambda r: (0, 0))],
        out_shape=[SDS(x.shape, dtype), SDS((8, width), f32)],
        compiler_params=limits(24),
        cost_estimate=cost(10 if edges else 0.1),
        name="row_grads",
    )(*args, *after)


def add_kernel(own_ref, other_ref, out_ref):
    out_ref[...] = (own_ref[...].astype(f32) + other_ref[...].astype(f32)).astype(out_ref.dtype)


def add_step(part, bit, dtype, after=()):
    return pl.pallas_call(
        following(add_kernel, 2, after),
        in_specs=[whole(part), whole(part)] + untouched(after),
        out_specs=whole(part),
        out_shape=SDS(part.shape, dtype),
        cost_estimate=cost(1),
        compiler_params=limits(8),
        name="add_step",
    )(part, swapped(part, *bit), *after)


def as_column(row):
    n = row.shape[1]
    eye = lax.broadcasted_iota(jnp.int32, (n, n), 0) == lax.broadcasted_iota(jnp.int32, (n, n), 1)
    return jnp.sum(jnp.where(eye, row, 0.0), axis=1, keepdims=True)


def split_shards(qkv_ref, rest_ref, units, width):
    groups = (rest_ref.shape[1] - units - width) // width
    starts = [units + width * (k + 1) for k in range(groups)]
    return qkv_ref[...], rest_ref[:, units : units + width], rest_ref[:, :units], [rest_ref[:, at : at + width] for at in starts]


def pack_kernel(qkv_ref, rest_ref, rq_ref, ro_ref, ru_ref, rd_ref, vone_ref, vtwo_ref, bias_ref,
                stats_ref, gout_ref, gup_ref, gdown_ref, nq_ref, no_ref, nu_ref, nd_ref, cq_ref, co_ref, cu_ref, cd_ref, *, decay):
    units, width = bias_ref.shape[1], vone_ref.shape[1]
    g_qkv, g_out, g_up, g_down = split_shards(qkv_ref, rest_ref, units, width)
    rows = g_qkv.shape[0]
    gout_ref[...], gup_ref[...] = g_out, g_up
    at, totals = 0, []
    for g, old_ref, new_ref, col_ref in ((g_qkv, rq_ref, nq_ref, cq_ref), (g_out, ro_ref, no_ref, co_ref), (g_up, ru_ref, nu_ref, cu_ref), (g_down, rd_ref, nd_ref, cd_ref)):
        groups = g if isinstance(g, list) else [g]
        columns, total, means = 0.0, 0.0, []
        for k, part in enumerate(groups):
            square = part * part + TINY_SQUARE
            columns = columns + jnp.sum(square, axis=0, keepdims=True)
            means.append(jnp.mean(square, axis=1, keepdims=True))
            if len(groups) > 1:
                gdown_ref[k * rows : (k + 1) * rows, :] = part
        mean = means[0] if len(means) == 1 else jnp.concatenate(means, axis=0)
        new = decay * as_column(old_ref[...].reshape(1, -1)) + (1.0 - decay) * mean
        col_ref[...] = new
        new_ref[...] = jnp.sum(jnp.where(lax.broadcasted_iota(jnp.int32, (new.shape[0],) * 2, 0) == lax.broadcasted_iota(jnp.int32, (new.shape[0],) * 2, 1), new, 0.0), axis=0)
        totals.append(jnp.sum(new, axis=0, keepdims=True))
        stats_ref[:, at : at + columns.shape[1]] = columns
        at += columns.shape[1]
    for ref, count in ((vone_ref, 2), (vtwo_ref, 3)):
        for n in range(count):
            stats_ref[:, at : at + width] = ref[n : n + 1, :]
            at += width
    stats_ref[:, at : at + units] = bias_ref[...]
    at += units
    lane = lax.broadcasted_iota(jnp.int32, (1, LANES), 1)
    last = jnp.zeros((1, LANES), f32)
    for n, total in enumerate(totals):
        last = jnp.where(lane == n, total, last)
    stats_ref[:, at : at + LANES] = last


def pack(qkv, rest, row_olds, vec_one, vec_two, bias, decay):
    units, width, rows = bias.shape[1], vec_one.shape[1], qkv.shape[0]
    tall = rest.shape[1] // width - units // width - 1
    count = qkv.shape[1] + width + units + width + 5 * width + units + LANES
    shapes = [(1, count), (rows, width), (rows, units), (tall * rows, width)]
    shapes += [old.shape for old in row_olds] + [(old.shape[0], 1) for old in row_olds]
    args = (qkv, rest, *row_olds, vec_one, vec_two, bias)
    return pl.pallas_call(
        functools.partial(pack_kernel, decay=decay),
        out_shape=[SDS(shape, f32) for shape in shapes],
        compiler_params=limits(24),
        cost_estimate=cost(3),
        name="pack",
    )(*args)


def update_kernel(stats_ref, qkv_ref, rest_ref, rq_ref, ro_ref, ru_ref, rd_ref, mq_ref, mo_ref, mu_ref, md_ref, oq_ref, oo_ref, ou_ref, od_ref,
                  vec_ref, vstate_ref, bias_ref, bstate_ref,
                  nq_ref, no_ref, nu_ref, nd_ref, cq_ref, co_ref, cu_ref, cd_ref, vg_ref, vs_ref, vn_ref, bg_ref, bs_ref, bn_ref, *, decay, full_rows):
    width, units = vec_ref.shape[1], bias_ref.shape[0]
    shards = split_shards(qkv_ref, rest_ref, units, width)
    rows = qkv_ref.shape[0]
    stats = stats_ref[...]
    totals = stats[:, stats.shape[1] - LANES :]
    at = 0
    sets = zip(shards, (rq_ref, ro_ref, ru_ref, rd_ref), (mq_ref, mo_ref, mu_ref, md_ref), (oq_ref, oo_ref, ou_ref, od_ref), (nq_ref, no_ref, nu_ref, nd_ref), (cq_ref, co_ref, cu_ref, cd_ref), full_rows)
    for n, (shard, row_ref, master_ref, old_ref, new_ref, col_ref, count) in enumerate(sets):
        columns = old_ref.shape[0]
        col = decay * old_ref[...].reshape(1, columns) + (1.0 - decay) * (stats[:, at : at + columns] / count)
        at += columns
        col_ref[...] = col[0]
        row_mean = totals[:, n : n + 1] / count
        parts = shard if isinstance(shard, list) else [shard]
        master = master_ref[...].astype(f32)
        for k, part in enumerate(parts):
            here = slice(k * rows, (k + 1) * rows)
            estimate = row_ref[here, :] * col / row_mean
            new_ref[here, :] = master[here] - RATE_MATRIX * part * lax.rsqrt(estimate)
    grad = jnp.concatenate([stats[:, at + n * width : at + (n + 1) * width] for n in range(5)], axis=0)
    at += 5 * width
    vg_ref[...] = grad
    state = decay * vstate_ref[...] + (1.0 - decay) * (grad * grad + TINY_SQUARE)
    vs_ref[...] = state
    vn_ref[...] = vec_ref[...] - RATE_VECTOR * grad * lax.rsqrt(state)
    grad = stats[:, at : at + units]
    bg_ref[...] = grad[0]
    state = decay * bstate_ref[...].reshape(1, units) + (1.0 - decay) * (grad * grad + TINY_SQUARE)
    bs_ref[...] = state[0]
    bn_ref[...] = (bias_ref[...].reshape(1, units) - RATE_VECTOR * grad * lax.rsqrt(state))[0]


def update(stats, qkv, rest, row_columns, masters, col_olds, vec, vec_state, bias, bias_state, decay, full_rows):
    args = (stats, qkv, rest, *row_columns, *masters, *col_olds, vec, vec_state, bias, bias_state)
    shapes = [m.shape for m in masters] + [c.shape for c in col_olds] + [vec.shape] * 3 + [bias.shape] * 3
    return pl.pallas_call(
        functools.partial(update_kernel, decay=decay, full_rows=full_rows),
        out_shape=[SDS(shape, f32) for shape in shapes],
        compiler_params=limits(24),
        cost_estimate=cost(3),
        name="update",
    )(*args)


def mask_kernel(info_ref, seg_ref, ok_ref, qx_ref, kx_ref, *, half, glob):
    lead, total = half // LANES, seg_ref.shape[1] // LANES
    own = qx_ref.shape[0] - glob
    lane = lax.broadcasted_iota(jnp.int32, (LANES, LANES), 1).astype(f32)
    for n in range(own // LANES + 2 * lead):
        block = info_ref[0] - lead + n
        at = pl.ds(pl.multiple_of(jnp.clip(block, 0, total - 1) * LANES, LANES), LANES)
        code = (seg_ref[:, at] + jnp.where(ok_ref[:, at] > 0, 8, 0)).astype(f32)
        code = jnp.broadcast_to(code, (LANES, LANES)).T
        valid = (code >= 8.0) & (block >= 0) & (block < total)
        document = jnp.where(code >= 8.0, code - 8.0, code) == lane
        seen = ((document | (lane == 4.0)) & valid) | (lane > 4.0)
        kx_ref[n * LANES : (n + 1) * LANES, :] = jnp.where(seen, 0.0, NEG_FILL).astype(bf16)
        if lead <= n < lead + own // LANES:
            qx_ref[(n - lead) * LANES : (n - lead + 1) * LANES, :] = jnp.where(document, 1.0, 0.0).astype(bf16)
    lane = lax.broadcasted_iota(jnp.int32, (glob, LANES), 1)
    kx_ref[own + 2 * half :, :] = jnp.where((lane == 4) & (info_ref[1] == 0), NEG_FILL, 0.0).astype(bf16)
    qx_ref[own:, :] = jnp.where(lane == 4, 1.0, 0.0).astype(bf16)


def mask_lanes(segments, valid, start, own, half, glob, first):
    info = jnp.stack([start // LANES, first.astype(jnp.int32)])
    return pl.pallas_call(
        functools.partial(mask_kernel, half=half, glob=glob),
        in_specs=[pl.BlockSpec(memory_space=pltpu.SMEM), whole(segments), whole(valid)],
        out_specs=[pl.BlockSpec((own + glob, LANES), lambda: (0, 0)), pl.BlockSpec((own + 2 * half + glob, LANES), lambda: (0, 0))],
        out_shape=[SDS((own + glob, LANES), bf16), SDS((own + 2 * half + glob, LANES), bf16)],
        compiler_params=limits(60),
        cost_estimate=cost(2),
        name="mask_lanes",
    )(info, segments, valid)


def body(
    tokens,
    glob_tokens,
    w_qkv,
    w_out,
    w_up,
    w_down,
    vec_params,
    hidden_bias,
    row_qkv,
    col_qkv,
    row_out,
    col_out,
    row_up,
    col_up,
    row_down,
    col_down,
    vec_state,
    bias_state,
    segments,
    valid_mask,
    out_cotangent,
    glob_cotangent,
):
    width = w_out.shape[0]
    size = width // HEADS
    assert 2 * size == LANES
    scale = size ** (-0.5)
    coef = scale * LOG2E
    half = BLOCK // 2
    tok, glob = tokens[0], glob_tokens[0]
    own, globs = tok.shape[0], glob.shape[0]
    seq_index = lax.axis_index("seq")
    first = seq_index == 0
    flag = first.astype(f32).reshape(1)
    bias_row = hidden_bias[None, :]
    batch_bits, seq_bits = bits_of("batch"), bits_of("seq")

    low, high = [batch_bits[:1]], [[bit] for bit in batch_bits[1:]]
    far = [seq_bits[1:][n : n + 2] for n in range(0, len(seq_bits) - 1, 2)]
    wide_stages = low + high + [seq_bits[:1]]
    tall_stages = low + [seq_bits[:1]] + high
    joint_stages = [[bit] for bit in seq_bits[1:]]
    pair_stages = low + [batch_bits[1:] + seq_bits[:1]] + far
    places = row_places(width, pair_stages)
    sequence = np.arange(1 << len(seq_bits)).reshape([2] * len(seq_bits)).transpose(
        [seq_bits[::-1].index(bit) for bit in seq_bits]
    ).reshape(-1)
    tall_chunk = w_down.shape[0] // lax.axis_size("batch") // sequence.size
    tall_places = tuple(int(n) * tall_chunk for n in sequence), tall_chunk
    halo_left, halo_right = shifted(tok[own - half :], "seq", 1), shifted(tok[:half], "seq", -1)
    qx, kx = mask_lanes(segments, valid_mask, seq_index * own, own, half, globs, first)
    qkv, normed_t = project(tok, glob, w_qkv, vec_params)
    part = glob_attention(qkv, qx, kx, own, half, size, coef)
    left, right, halo_t = project_halos(halo_left, halo_right, w_qkv, vec_params)
    part, glob_lse = merge_step(part, *seq_bits[0], size, after=[left])
    inner_att, inner_lse = local_inner(qkv, qx, kx, own, half, size, coef, after=[part])
    for bit in seq_bits[1:-1]:
        part, glob_lse = merge_step(part, *bit, size, after=[inner_lse])
    att, lse = local_edge(qkv, left, right, qx, kx, inner_att, inner_lse, own, half, size, coef, after=[part])
    part, glob_lse = merge_step(part, *seq_bits[-1], size, after=[lse])
    side = side_of(*batch_bits[0]).reshape(1)
    out_tok, out_glob, mixed_grad, heads_grad, *matrices, vec_two, bias_sum = feed_forward(
        side, flag, att, part, tok, glob, w_out, w_up, w_down, vec_params, bias_row, out_cotangent[0], glob_cotangent[0], places, tall_places
    )
    wide, down = Scatter(*matrices[:2], wide_stages), Scatter(*matrices[2:], tall_stages)
    edge = edge_backward(qkv, left, right, qx, kx, att, heads_grad, lse, own, size, coef, scale, after=wide.parts + down.parts)
    grad_left, grad_right = edge[3:]
    down.step(after=edge[:1])
    wide.step(after=down.parts)
    to_left, to_right, halo_sums = halo_rows(halo_left, halo_right, vec_params, w_qkv, grad_left, grad_right, after=wide.parts)
    edges = (shifted(to_right, "seq", 1), shifted(to_left, "seq", -1))
    dq, dkv, glob_part, glob_sums = inner_backward(
        qkv, qx, kx, att, part, heads_grad, lse, glob_lse, *edge[:3], flag, glob, vec_params, mixed_grad, w_qkv, own, half, size, coef, scale,
        after=[to_left, to_right],
    )
    parts = [(dq, dkv)]
    down.step(after=[parts[0][0]], us=0.01)
    wide.step(after=[*down.parts, *edges], us=0.01)
    weight = Scatter(*qkv_weight_grad(0, side, normed_t, halo_t, dq, dkv, grad_left, grad_right, places, after=wide.parts), pair_stages)
    glob_bits = seq_bits[1:] + seq_bits[:1]
    glob_part = add_step(glob_part, glob_bits[0], bf16, after=weight.parts)
    joint = joint_scatter(wide, down, joint_stages, after=[glob_part])
    weight.step(after=joint.parts)
    for bit in glob_bits[1:-1]:
        glob_part = add_step(glob_part, bit, bf16, after=weight.parts)
    ones = jnp.ones((1,), f32)
    row_args = (vec_params, mixed_grad, w_qkv, parts, 0, half, f32)
    tokens_grad, one_sums = row_grads(ones, tok, *row_args, edges=edges, after=[glob_part], share=(0, 2))
    joint.step(after=[one_sums])
    tokens_grad, two_sums = row_grads(ones, tok, *row_args, edges=edges, after=joint.parts, share=(1, 2), into=tokens_grad)
    tok_sums = one_sums + two_sums
    weight.step(after=[two_sums])
    glob_part = add_step(glob_part, glob_bits[-1], f32, after=weight.parts)
    while joint.stages:
        rest = joint.step(after=[glob_part])
    while weight.stages:
        shard_qkv = weight.step(after=[rest])
    decay = 1.0 - STEP ** (-0.8)
    units = w_up.shape[1]
    owner = lax.axis_index(("batch", "seq"))
    masters = []
    for matrix in (w_qkv, w_out, w_up, w_down):
        rows = matrix.shape[0] // lax.axis_size(("batch", "seq"))
        masters.append(lax.dynamic_slice_in_dim(matrix, owner * rows, rows, 0))
    stats, grad_out, grad_up, grad_down, *rows_new = pack(
        shard_qkv, rest, (row_qkv, row_out, row_up, row_down), halo_sums + glob_sums + tok_sums, vec_two, bias_sum, decay
    )
    every = batch_bits + seq_bits
    for bits in [every[n : n + 2] for n in range(0, len(every), 2)]:
        terms = [stats] + [flipped(stats, bits, n) for n in range(1, 1 << len(bits))]
        while len(terms) > 1:
            terms = [a + b for a, b in zip(terms[::2], terms[1::2])]
        stats = terms[0]
    new_qkv, new_out, new_up, new_down, col_qkv_new, col_out_new, col_up_new, col_down_new, *vectors = update(
        stats, shard_qkv, rest, rows_new[4:], masters, (col_qkv, col_out, col_up, col_down), vec_params, vec_state, hidden_bias, bias_state,
        decay, (w_qkv.shape[0], w_out.shape[0], w_up.shape[0], w_down.shape[0]),
    )
    return (
        out_tok[None],
        out_glob[None],
        tokens_grad[None],
        glob_part[None],
        shard_qkv,
        rows_new[0],
        col_qkv_new,
        new_qkv,
        grad_out,
        rows_new[1],
        col_out_new,
        new_out,
        grad_up,
        rows_new[2],
        col_up_new,
        new_up,
        grad_down,
        rows_new[3],
        col_down_new,
        new_down,
        *vectors,
    )


def solution(mesh):
    in_specs = (
        P("batch", "seq", None),
        P("batch", None, None),
        P(),
        P(),
        P(),
        P(),
        P(),
        P(),
        P(("batch", "seq")),
        P(),
        P(("batch", "seq")),
        P(),
        P(("batch", "seq")),
        P(),
        P(("batch", "seq")),
        P(),
        P(),
        P(),
        P("batch", None),
        P("batch", None),
        P("batch", "seq", None),
        P("batch", None, None),
    )
    out_specs = (
        P("batch", "seq", None),
        P("batch", None, None),
        P("batch", "seq", None),
        P("batch", None, None),
        P(("batch", "seq"), None),
        P(("batch", "seq")),
        P(),
        P(("batch", "seq"), None),
        P(("batch", "seq"), None),
        P(("batch", "seq")),
        P(),
        P(("batch", "seq"), None),
        P(("batch", "seq"), None),
        P(("batch", "seq")),
        P(),
        P(("batch", "seq"), None),
        P(("batch", "seq"), None),
        P(("batch", "seq")),
        P(),
        P(("batch", "seq"), None),
        P(),
        P(),
        P(),
        P(),
        P(),
        P(),
    )
    return jax.shard_map(body, mesh=mesh, in_specs=in_specs, out_specs=out_specs, check_vma=False)
```
